32 devices in a mesh: row: 8 (over z, x), ch: 4 (over y, core).
Axes of the slice: x: 2, y: 2, z: 4, core: 2. Of those that a mesh axis runs over, the one named last changes fastest.
Arguments:
- feats: bfloat16 [2048, 9216], P('ch', 'row'), may hold values from -6 to 6
- lowlevel: bfloat16 [256, 147456], P('ch', 'row'), may hold values from -6 to 6
- heights: int32 [6], replicated, may hold values from 1 to 64, 288 in all
- widths: int32 [6], replicated, may hold values from 8 to 32, as said below
- w_one: bfloat16 [256, 2048], P('ch'), may hold values from -0.125 to 0.125
- w_atrous: bfloat16 [3, 256, 9, 2048], P(None, 'ch'), may hold values from -0.046875 to 0.046875
- w_pool: bfloat16 [256, 2048], P('ch'), may hold values from -0.125 to 0.125
- w_proj: bfloat16 [256, 1280], P('ch'), may hold values from -0.15625 to 0.15625
- w_low: bfloat16 [48, 256], P(None, 'ch'), may hold values from -0.375 to 0.375
- w_dec1: bfloat16 [256, 9, 304], P('ch'), may hold values from -0.109375 to 0.109375
- w_dec2: bfloat16 [256, 9, 256], P('ch'), may hold values from -0.125 to 0.125
- w_cls: bfloat16 [21, 256], replicated, may hold values from -0.375 to 0.375
- b_cls: bfloat16 [21], replicated, may hold values from -3 to 3
- mid_gain: bfloat16 [6, 256], P(None, 'ch'), may hold values from 0.099609375 to 1.8984375
- mid_shift: bfloat16 [6, 256], P(None, 'ch'), may hold values from -3 to 3
- low_gain: bfloat16 [48], P('ch'), may hold values from 0.099609375 to 1.8984375
- low_shift: bfloat16 [48], P('ch'), may hold values from -3 to 3
- dec_gain: bfloat16 [2, 256], P(None, 'ch'), may hold values from 0.099609375 to 1.8984375
- dec_shift: bfloat16 [2, 256], P(None, 'ch'), may hold values from -3 to 3
- cotangent: bfloat16 [21, 147456], P(None, ('row', 'ch')), may hold values from -6 to 6
Outputs:
- logits: float32 [21, 147456], P(None, ('row', 'ch'))
- g_feats: float32 [2048, 9216], P('ch', 'row')
- g_lowlevel: float32 [256, 147456], P('ch', 'row')
- g_w_one: float32 [256, 2048], P('ch')
- g_w_atrous: float32 [3, 256, 9, 2048], P(None, 'ch')
- g_w_pool: float32 [256, 2048], P('ch')
- g_w_proj: float32 [256, 1280], P('ch')
- g_w_low: float32 [48, 256], P(None, 'ch')
- g_w_dec1: float32 [256, 9, 304], P('ch')
- g_w_dec2: float32 [256, 9, 256], P('ch')
- g_w_cls: float32 [21, 256], replicated
- g_b_cls: float32 [21], replicated
- g_mid_gain: float32 [6, 256], P(None, 'ch')
- g_mid_shift: float32 [6, 256], P(None, 'ch')
- g_low_gain: float32 [48], P('ch')
- g_low_shift: float32 [48], P('ch')
- g_dec_gain: float32 [2, 256], P(None, 'ch')
- g_dec_shift: float32 [2, 256], P(None, 'ch')
The draws below stay inside these ranges and needn't reach their ends.
Inputs may be any that keep to these rules, and one draw needn't show every extreme that they name: The heights sum to 288. `widths`: one image is 32 columns wide and one 32 // 4.
All inputs are finite; a program needn't handle non-finite values.
Results may differ from the reference program's by a relative error of at most 0.03.
Values may be sent and summed in bfloat16 or wider, within the bound.
No kernel may reach another device: no remote copies, remote signals or barrier semaphores. Data moves between devices by JAX's collectives and lax.ppermute only.
A program may use at most 512 MiB of HBM per device.

```python
import math
from functools import partial
import jax
import jax.numpy as jnp
import numpy as np
from jax import lax

CIN = 2048
ASPP_C = 256
LOWC = 48
CL = 256
CLS = 21
HMOST = 64
WS = 32
HS = 288
NIMG = 6


def draw_widths(key, part):
    key = jax.random.fold_in(key, 17)
    first_key, second_key = jax.random.split(key)
    values = jax.random.randint(first_key, (NIMG,), WS // 4, WS + 1, dtype=jnp.int32)
    chosen = jax.random.randint(second_key, (), 0, NIMG, dtype=jnp.int32)
    positions = jnp.arange(NIMG, dtype=jnp.int32)
    values = jnp.where(positions == chosen, WS, values)
    return jnp.where(positions == (chosen + 1) % NIMG, WS // 4, values).astype(jnp.int32)


def shard_levels(key, shape, cuts, low, top_value):
    def one(dim, blocks):
        draws = jax.random.uniform(jax.random.fold_in(jax.random.fold_in(key, 6), dim), (blocks,), jnp.float32, low / len(cuts), top_value / len(cuts))
        return jnp.repeat(jnp.exp(draws), shape[dim] // blocks).reshape((-1,) + (1,) * (len(shape) - dim - 1))

    level = one(*cuts[0])
    for cut in cuts[1:]:
        level = level * one(*cut)
    return level


def split_up(amount, total, reach, skew):
    loads = [(1 << 20) // math.isqrt(standing ** skew) + 1 for standing in range(2, amount + 1)]
    spare, given = total - reach - (amount - 1), [1] * (amount - 1)
    while spare > 0:
        movable = [i for i in range(amount - 1) if given[i] < reach]
        mass, budget = sum([loads[i] for i in movable]), spare
        for i in movable:
            extra = min(reach - given[i], max(1, budget * loads[i] // mass), spare)
            given[i] = given[i] + extra
            spare = spare - extra
    return np.array([reach] + given)


def ragged_sizes(key, amount, total, most, slope):
    if amount == 2:
        one = jax.random.randint(key, (), max(1, total - most), min(most, total - 1) + 1)
        return jnp.stack([one, total - one])
    tallies = jnp.asarray(split_up(amount, total, most, slope), jnp.int32)
    pairs = (amount - 1) // 2
    giver, sink = tallies[1:1 + 2 * pairs:2], tallies[2:2 + 2 * pairs:2]
    room = jnp.minimum(giver - 1, most - sink)
    passed = jax.random.randint(jax.random.fold_in(key, 1), (pairs,), 0, 1 << 20) % (room + 1)
    tallies = tallies.at[1:1 + 2 * pairs:2].set(giver - passed).at[2:2 + 2 * pairs:2].set(sink + passed)
    return tallies[jax.random.permutation(jax.random.fold_in(key, 2), amount)]


def noise(key, shape, scale, bound, shards=(), kind=jnp.bfloat16):
    values = jax.random.normal(key, shape, jnp.float32) * scale
    if len(shards) > 0:
        values = shard_levels(key, shape, shards, -0.22, 0.18) * values
    return jnp.clip(values, min=-bound, max=bound).astype(kind)


def setup_inputs(seed: int = 0) -> dict:
    streams_of = jax.random.split(jax.random.key(seed), 21)
    return {
        "feats": noise(streams_of[0], (CIN, HS * WS), 1.0, 6.0, ((0, 4), (1, 8))),
        "lowlevel": noise(streams_of[1], (CL, 16 * HS * WS), 1.0, 6.0, ((0, 4), (1, 8))),
        "heights": ragged_sizes(streams_of[2], NIMG, HS, HMOST, 2).astype(jnp.int32),
        "widths": draw_widths(jax.random.fold_in(streams_of[20], 71), 0),
        "w_one": noise(streams_of[4], (ASPP_C, CIN), CIN ** -0.5, 0.125, ((0, 4),)),
        "w_atrous": noise(streams_of[5], (3, ASPP_C, 9, CIN), (9 * CIN) ** -0.5, 0.046875, ((1, 4),)),
        "w_pool": noise(streams_of[6], (ASPP_C, CIN), CIN ** -0.5, 0.125, ((0, 4),)),
        "w_proj": noise(streams_of[7], (ASPP_C, 5 * ASPP_C), (5 * ASPP_C) ** -0.5, 0.15625, ((0, 4),)),
        "w_low": noise(streams_of[8], (LOWC, CL), CL ** -0.5, 0.375, ((1, 4),)),
        "w_dec1": noise(streams_of[9], (ASPP_C, 9, LOWC + ASPP_C), (9 * (LOWC + ASPP_C)) ** -0.5, 0.109375, ((0, 4),)),
        "w_dec2": noise(streams_of[10], (ASPP_C, 9, ASPP_C), (9 * ASPP_C) ** -0.5, 0.125, ((0, 4),)),
        "w_cls": noise(streams_of[11], (CLS, ASPP_C), ASPP_C ** -0.5, 0.375),
        "b_cls": noise(streams_of[12], (CLS,), 0.5, 3.0),
        "mid_gain": jnp.clip(1.0 + 0.18 * jax.random.normal(streams_of[13], (6, ASPP_C), jnp.float32), 0.099609375, 1.8984375).astype(jnp.bfloat16),
        "mid_shift": noise(streams_of[14], (6, ASPP_C), 0.5, 3.0, ((1, 4),)),
        "low_gain": jnp.clip(1.0 + 0.18 * jax.random.normal(streams_of[15], (LOWC,), jnp.float32), 0.099609375, 1.8984375).astype(jnp.bfloat16),
        "low_shift": noise(streams_of[16], (LOWC,), 0.5, 3.0, ((0, 4),)),
        "dec_gain": jnp.clip(1.0 + 0.18 * jax.random.normal(streams_of[17], (2, ASPP_C), jnp.float32), 0.099609375, 1.8984375).astype(jnp.bfloat16),
        "dec_shift": noise(streams_of[18], (2, ASPP_C), 0.5, 3.0, ((1, 4),)),
        "cotangent": noise(streams_of[19], (CLS, 16 * HS * WS), 1.0, 6.0, ((1, 32),)),
    }


EPSILON = 1e-05
DILATIONS = (6, 12, 18)
HIGHEST = lax.Precision.HIGHEST

@jax.custom_vjp
def low(v):
    return lax.optimization_barrier(v.astype(jnp.bfloat16)).astype(jnp.float32)

@jax.custom_vjp
def low_back(v):
    return v

def low_keep(v):
    return (low(v), None)

def low_pass(kept, grad):
    return (grad,)

def back_keep(v):
    return (v, None)

def back_low(kept, grad):
    return (low(grad),)
low.defvjp(low_keep, low_pass)
low_back.defvjp(back_keep, back_low)

def segment_of(indices, image_ends):
    return lax.optimization_barrier(jnp.sum((indices[:, None] >= image_ends[None, :]).astype(jnp.int32), axis=1))

def same_rows(first_row, row_count, offset, image_ends, total_rows):
    indices = first_row + jnp.arange(row_count, dtype=jnp.int32)
    others = indices + offset
    inside = (others >= 0) & (others < total_rows)
    return (inside & (segment_of(indices, image_ends) == segment_of(others, image_ends))).astype(jnp.float32)

def geometry(heights, widths, factor, first_row, row_count, col_count):
    image_ends = (jnp.cumsum(heights) * factor).astype(jnp.int32)
    starts = (image_ends - heights * factor).astype(jnp.int32)
    indices = first_row + jnp.arange(row_count, dtype=jnp.int32)
    inside = (indices[:, None] >= starts[None, :]) & (indices[:, None] < image_ends[None, :])
    limit = lax.optimization_barrier(jnp.sum(jnp.where(inside, widths[None, :] * factor, 0), axis=1))
    valid_mask = (jnp.arange(col_count, dtype=jnp.int32)[None, :] < limit[:, None]).astype(jnp.float32)
    return (inside.astype(jnp.float32), valid_mask, image_ends)

def upsample(earlier, middle, later):
    stacked = jnp.stack([0.375 * earlier + 0.625 * middle, 0.125 * earlier + 0.875 * middle, 0.875 * middle + 0.125 * later, 0.625 * middle + 0.375 * later], axis=2)
    channels, height, _, width = stacked.shape
    tall = stacked.reshape(channels, 4 * height, width)
    leftward = jnp.pad(tall, ((0, 0), (0, 0), (1, 0)))[:, :, :-1]
    rightward = jnp.pad(tall, ((0, 0), (0, 0), (0, 1)))[:, :, 1:]
    spread = jnp.stack([0.375 * leftward + 0.625 * tall, 0.125 * leftward + 0.875 * tall, 0.875 * tall + 0.125 * rightward, 0.625 * tall + 0.375 * rightward], axis=3)
    return spread.reshape(channels, 4 * height, 4 * width)

def shift_rows(values, offset):
    extent = values.shape[1]
    margin = abs(offset)
    if margin == 0:
        return values
    padded = jnp.pad(values, ((0, 0), (margin, margin), (0, 0)))
    return padded[:, margin + offset:margin + offset + extent]

def shift_cols(values, offset):
    extent = values.shape[2]
    margin = abs(offset)
    if margin == 0:
        return values
    padded = jnp.pad(values, ((0, 0), (0, 0), (margin, margin)))
    return padded[:, :, margin + offset:margin + offset + extent]

def tap_row(values, weight, row_mask, dilation, row_tap):
    moved = shift_rows(values, (row_tap - 1) * dilation)
    result = jnp.zeros((weight.shape[0], values.shape[1], values.shape[2]), jnp.float32)
    for col_tap in range(3):
        result = result + jnp.einsum('oc,chw->ohw', weight[:, row_tap * 3 + col_tap], shift_cols(moved, (col_tap - 1) * dilation), precision=HIGHEST)
    return result * row_mask[None, :, None]

def dilated(values, weight, dilation, image_ends, total_rows):
    height = values.shape[1]
    result = jnp.zeros((weight.shape[0], height, values.shape[2]), jnp.float32)
    for row_tap in range(3):
        row_mask = same_rows(0, height, (row_tap - 1) * dilation, image_ends, total_rows)
        result = result + jax.checkpoint(partial(tap_row, dilation=dilation, row_tap=row_tap))(values, weight, row_mask)
    return result

def norm_act(pre_act, gain, shift, valid_mask, pixel_count):
    centre = lax.optimization_barrier(jnp.sum(pre_act * valid_mask, axis=(1, 2))) / pixel_count
    centered = pre_act - centre[:, None, None]
    spread = lax.optimization_barrier(jnp.sum(centered * centered * valid_mask, axis=(1, 2))) / pixel_count
    normed = centered * lax.rsqrt(spread + EPSILON)[:, None, None]
    return jax.nn.silu(gain[:, None, None] * normed + shift[:, None, None]) * valid_mask

def reference(feats, lowlevel, heights, widths, w_one, w_atrous, w_pool, w_proj, w_low, w_dec1, w_dec2, w_cls, b_cls, mid_gain, mid_shift, low_gain, low_shift, dec_gain, dec_shift, cotangent):
    member, valid_mask, image_ends = geometry(heights, widths, 1, 0, HS, WS)
    member_fine, valid_fine, ends_fine = geometry(heights, widths, 4, 0, 4 * HS, 4 * WS)
    image_area = (heights * widths).astype(jnp.float32)
    pixel_count = jnp.sum(image_area)
    fine_count = 16.0 * pixel_count
    above = same_rows(0, HS, -1, image_ends, HS)
    below = same_rows(0, HS, 1, image_ends, HS)

    def forward(feats, lowlevel, w_one, w_atrous, w_pool, w_proj, w_low, w_dec1, w_dec2, w_cls, b_cls, mid_gain, mid_shift, low_gain, low_shift, dec_gain, dec_shift):
        inputs = feats.reshape(CIN, HS, WS) * valid_mask[None]
        branches = [low_back(jnp.einsum('oc,chw->ohw', w_one, inputs, precision=HIGHEST))]
        for branch_index in range(3):
            branches.append(low_back(dilated(inputs, w_atrous[branch_index], DILATIONS[branch_index], image_ends, HS)))
        acts = [low(norm_act(branches[branch_index], mid_gain[branch_index], mid_shift[branch_index], valid_mask, pixel_count)) for branch_index in range(4)]
        pooled = low(jnp.dot(lax.optimization_barrier(jnp.sum(inputs, axis=2)), member, precision=HIGHEST) / image_area[None, :])
        pool_pre = low_back(jnp.dot(w_pool, pooled, precision=HIGHEST))
        pool_mean = lax.optimization_barrier(jnp.mean(pool_pre, axis=1))
        pool_var = lax.optimization_barrier(jnp.mean(pool_pre * pool_pre, axis=1)) - pool_mean * pool_mean
        pool_normed = (pool_pre - pool_mean[:, None]) * lax.rsqrt(pool_var + EPSILON)[:, None]
        pool_act = low(jax.nn.silu(mid_gain[4][:, None] * pool_normed + mid_shift[4][:, None]))
        broad = jnp.dot(pool_act, member.T, precision=HIGHEST)[:, :, None] * valid_mask[None]
        joined = jnp.concatenate(acts + [broad], axis=0)
        proj_pre = low_back(jnp.einsum('oc,chw->ohw', w_proj, joined, precision=HIGHEST))
        coarse = low(norm_act(proj_pre, mid_gain[5], mid_shift[5], valid_mask, pixel_count))
        earlier = shift_rows(coarse, -1) * above[None, :, None]
        later = shift_rows(coarse, 1) * below[None, :, None]
        upsampled = low(upsample(earlier, coarse, later) * valid_fine[None])
        low_in = lowlevel.reshape(CL, 4 * HS, 4 * WS) * valid_fine[None]
        low_pre = low_back(jnp.einsum('oc,chw->ohw', w_low, low_in, precision=HIGHEST))
        low_act = low(norm_act(low_pre, low_gain, low_shift, valid_fine, fine_count))
        decoder_in = jnp.concatenate([low_act, upsampled], axis=0)
        first_pre = low_back(dilated(decoder_in, w_dec1, 1, ends_fine, 4 * HS))
        first_act = low(norm_act(first_pre, dec_gain[0], dec_shift[0], valid_fine, fine_count))
        second_pre = low_back(dilated(first_act, w_dec2, 1, ends_fine, 4 * HS))
        second_act = low_back(low(norm_act(second_pre, dec_gain[1], dec_shift[1], valid_fine, fine_count)))
        scores = jnp.einsum('kc,chw->khw', w_cls, second_act, precision=HIGHEST) + b_cls[:, None, None]
        return scores.reshape(CLS, 16 * HS * WS)
    floats = [array.astype(jnp.float32) for array in (feats, lowlevel, w_one, w_atrous, w_pool, w_proj, w_low, w_dec1, w_dec2, w_cls, b_cls, mid_gain, mid_shift, low_gain, low_shift, dec_gain, dec_shift)]
    logits, pullback = jax.vjp(forward, *floats)
    grads = pullback(cotangent.astype(jnp.float32))
    return (logits, grads[0], grads[1], grads[2], grads[3], grads[4], grads[5], grads[6], grads[7], grads[8], grads[9], grads[10], grads[11], grads[12], grads[13], grads[14], grads[15], grads[16])
```

```python
import jax
import jax.numpy as jnp
from jax import lax
from jax.experimental import pallas as pl
from jax.experimental.pallas import tpu as pltpu
from jax.sharding import PartitionSpec as P

LOWC = 48
WS = 32
WF = 4 * WS
REACH = 18
PAD = 640
EPSILON = 1e-05
HIGHEST = lax.Precision.HIGHEST
BF = jnp.bfloat16
F32 = jnp.float32
BOTH = ("row", "ch")
VMEM_LIMIT = 56 * 1024 * 1024
CHUNKS = (((0, 1, 2), True),)


def params():
    return pltpu.CompilerParams(vmem_limit_bytes=VMEM_LIMIT)


def dot(a, b):
    return jnp.dot(a, b, preferred_element_type=F32)


def dot_nt(a, b):
    return lax.dot_general(a, b, (((1,), (1,)), ((), ())), preferred_element_type=F32)


def tiles(extent, size):
    return [(start, min(size, extent - start)) for start in range(0, extent, size)]


class Images:
    def __init__(self, heights_ref, widths_ref):
        self.ends, self.widths, total = [], [], 0
        for i in range(heights_ref.shape[0]):
            total = total + heights_ref[i]
            self.ends.append(total)
            self.widths.append(widths_ref[i])
        self.total = total

    def image(self, rows, factor=1):
        return sum((rows >= end * factor).astype(jnp.int32) for end in self.ends)

    def same(self, rows, offset, factor=1):
        others = rows + offset
        inside = (rows >= 0) & (rows < self.total * factor) & (others >= 0) & (others < self.total * factor)
        return jnp.where(inside & (self.image(rows, factor) == self.image(others, factor)), 1.0, 0.0)

    def limit(self, rows, factor=1):
        image = self.image(rows, factor)
        value = jnp.zeros(rows.shape, jnp.int32)
        for i, width in enumerate(self.widths):
            value = jnp.where(image == i, width * factor, value)
        return jnp.where(rows >= 0, value, 0)


def iota(shape, axis):
    return lax.broadcasted_iota(jnp.int32, shape, axis)


def split(index, size):
    return jnp.right_shift(index, size.bit_length() - 1), jnp.bitwise_and(index, size - 1)


def tap_rows(images, rows, col):
    masks = [images.same(rows, -a * rate) for rate in (6, 12, 18) for a in (-1, 1)]
    return masks + [jnp.where(col < images.limit(rows), 1.0, 0.0)]


def strip_geometry_kernel(heights, widths, places, rows_ref, member_ref, fine_ref):
    images = Images(heights, widths)
    pixels = rows_ref.shape[1]
    row, col = split(places[0] * pixels + iota((1, pixels), 1), WS)
    values = tap_rows(images, row, col)
    for i, value in enumerate(values):
        rows_ref[i : i + 1] = value
    rows_ref[7:8] = jnp.zeros((1, pixels), F32)
    image = images.image(row)
    number = iota(member_ref.shape, 0)
    member_ref[...] = (jnp.where(number == image, 1.0, 0.0) * values[6]).astype(BF)
    row, col = split(places[0] * 16 * pixels + iota(fine_ref.shape, 1), WF)
    fine_ref[...] = jnp.where(col < images.limit(row, 4), 1.0, 0.0).astype(BF)


def geometry_kernel(
    margin, heights, widths, places,
    canvas_ref, member_ref, strips_ref, shares_ref, fines_ref, mine_ref, window_ref, ext_ref, masks_ref, enlarge_ref,
):
    images = Images(heights, widths)
    groups, _, pixels = canvas_ref.shape
    everyone, share = shares_ref.shape[0], mine_ref.shape[1]
    place = places[1]
    shape = (groups, pixels)
    row, col = split(iota(shape, 0) * pixels + iota(shape, 1), WS)
    values = tap_rows(images, row, col)
    for i, value in enumerate(values):
        canvas_ref[:, i] = value
    canvas_ref[:, 7] = jnp.zeros(shape, F32)
    image = images.image(row)
    for i in range(member_ref.shape[1]):
        member_ref[:, i] = jnp.where(image == i, values[6], 0.0)
    strips_ref[...] = jnp.sum(values[6], axis=1, keepdims=True)

    def counted(pixels, cols, factor):
        row, col = split(iota((everyone, pixels), 0) * pixels + iota((everyone, pixels), 1), cols)
        return jnp.sum(jnp.where(col < images.limit(row, factor), 1.0, 0.0), axis=1, keepdims=True)

    shares_ref[...] = counted(share, WS, 1)
    rows = masks_ref.shape[1] // WF
    number = iota((everyone, rows), 0) * rows + iota((everyone, rows), 1)
    fines_ref[...] = jnp.sum(images.limit(number, 4).astype(F32), axis=1, keepdims=True)

    row, col = split(place * share + iota((1, share), 1), WS)
    valid = jnp.where(col < images.limit(row), 1.0, 0.0)
    image = images.image(row)
    last = mine_ref.shape[0] - 8
    mine_ref[:last] = jnp.where(iota((last, share), 0) == image, 1.0, 0.0) * valid
    mine_ref[last:] = jnp.broadcast_to(valid, (8, share))
    row, col = split(place * share - margin + iota(window_ref.shape, 1), WS)
    window_ref[...] = jnp.where(col < images.limit(row), 1.0, 0.0)

    first = place * rows
    row, col = split(iota((1, masks_ref.shape[1]), 1), WF)
    for i, offset in enumerate((-1, 1)):
        masks_ref[i : i + 1] = images.same(first + row, offset, 4)
    window, ext = enlarge_ref.shape
    at_row, at_col = split(place * share - margin + iota((window, 1), 0), WS)
    for start, size in tiles(ext, 512):
        row, col = split(start + iota((1, size), 1), WF)
        row = first - 1 + row
        valid = jnp.where(col < images.limit(row, 4), 1.0, 0.0)
        ext_ref[:, start : start + size] = valid

        def weights(phase):
            middle = jnp.where((phase == 0) | (phase == 3), 0.625, 0.875)
            before = jnp.where(phase == 0, 0.375, jnp.where(phase == 1, 0.125, 0.0))
            after = jnp.where(phase == 3, 0.375, jnp.where(phase == 2, 0.125, 0.0))
            return middle, before, after

        def part(there, here, middle, before, after):
            apart = there - here
            return jnp.where(apart == 0, middle, jnp.where(apart == -1, before, jnp.where(apart == 1, after, 0.0)))

        q, phase = split(row, 4)
        middle, before, after = weights(phase)
        by_row = part(at_row, q, middle * valid, before * images.same(q, -1) * valid, after * images.same(q, 1) * valid)
        q, phase = split(col, 4)
        enlarge_ref[:, start : start + size] = (by_row * part(at_col, q, *weights(phase))).astype(BF)


def geometry_call(kernel, heights, widths, places, outputs):
    smem = pl.BlockSpec(memory_space=pltpu.SMEM)
    return pl.pallas_call(
        kernel,
        in_specs=[smem] * 3,
        out_specs=[pl.BlockSpec(memory_space=pltpu.VMEM)] * len(outputs),
        out_shape=outputs,
        compiler_params=params(),
        cost_estimate=pl.CostEstimate(flops=20000000, bytes_accessed=6000000, transcendentals=0),
    )(heights, widths, places)


def gather_blocks(x):
    count, me = lax.axis_size("ch"), lax.axis_index("ch")
    if count == 4:
        cross = lambda v, m: lax.ppermute(v, "ch", [(i, i ^ m) for i in range(count)])
        far = cross(x, 2)
        near = cross(x, 1)
        return [x, near, far, cross(far, 1)], [me, me ^ 1, me ^ 2, me ^ 3]
    every = lax.all_gather(x, "ch", axis=0)
    return [every[i] for i in range(count)], [jnp.int32(i) for i in range(count)]


def swap_row(x):
    groups, strip = lax.axis_size("row"), lax.axis_index("row")
    number = jnp.arange(groups, dtype=jnp.int32)
    if groups != 8:
        return lax.all_to_all(x, "row", 0, 0), number
    pick = lambda i: lax.dynamic_index_in_dim(x, i, 0, False)
    blocks = [pick(strip)]
    for m in range(1, groups):
        blocks.append(lax.ppermute(pick(strip ^ m), "row", [(i, i ^ m) for i in range(groups)]))
    return jnp.stack(blocks), number ^ strip


def swap_ch(x):
    count, me = lax.axis_size("ch"), lax.axis_index("ch")
    if count != 4:
        return lax.all_to_all(x, "ch", 0, 0)
    pick = lambda i: lax.dynamic_index_in_dim(x, i, 0, False)
    blocks = [pick(me)]
    for m in (1, 2, 3):
        blocks.append(lax.ppermute(pick(me ^ m), "ch", [(i, i ^ m) for i in range(count)]))
    return jnp.stack(blocks)


def reduce_blocks(blocks):
    count = lax.axis_size("ch")
    if count == 4:
        cross = lambda v, m: lax.ppermute(v, "ch", [(i, i ^ m) for i in range(count)])
        arrived = cross(jnp.stack([blocks[3], blocks[1]]), 1).astype(F32)
        onward = (blocks[2].astype(F32) + arrived[0]).astype(BF)
        return blocks[0].astype(F32) + arrived[1] + cross(onward, 2).astype(F32)
    return lax.psum_scatter(jnp.stack(blocks), "ch", scatter_dimension=0).astype(F32)


def gather_all(top, low):
    groups, count = lax.axis_size("row"), lax.axis_size("ch")
    strip, me = lax.axis_index("row"), lax.axis_index("ch")
    whole = jnp.arange(groups * count, dtype=jnp.int32)
    if groups != 8 or count != 4:
        every = lax.all_gather(jnp.stack([top, low]), BOTH, axis=0)
        top, low = every[:, 0], every[:, 1]
        return (top, top), (low, low), whole, whole
    line = groups // 2

    def around(v, step):
        pairs = [(2 * i + e, 2 * ((i + step) % line) + e) for i in range(line) for e in range(2)]
        return lax.ppermute(v, "row", pairs)

    beside = lambda v: lax.ppermute(v, "row", [(i, i ^ 1) for i in range(groups)])
    across = lambda v: lax.ppermute(v, "ch", [(i, i ^ 2) for i in range(count)])
    core = lambda v: lax.ppermute(v, "ch", [(i, i ^ 1) for i in range(count)])
    top = jnp.stack([top, around(top, 1), around(top, 2), around(top, 3)])
    low = jnp.stack([low, around(low, 1), around(low, 2), around(low, 3)])
    top_beside, low_across = beside(top), across(low)
    top = jnp.concatenate([top, top_beside, across(top), across(top_beside)])
    low = jnp.concatenate([low, low_across, beside(low), beside(low_across)])
    other_strip, other_me = whole // count, whole % count
    z = jnp.mod(strip // 2 - other_strip // 2, line)
    e = (strip ^ other_strip) & 1
    y = ((me ^ other_me) >> 1) & 1
    c = (me ^ other_me) & 1
    return (top, core(top)), (low, core(low)), ((c * 2 + y) * 2 + e) * line + z, ((c * 2 + e) * 2 + y) * line + z


def gather_line(x, rider):
    def along(v, places, step):
        return lax.ppermute(v, "row", [(2 * i + e, 2 * (i + step) + e) for i in places for e in range(2)])

    def beside(v, places):
        return lax.ppermute(v, "row", [(2 * i + e, 2 * i + 1 - e) for i in places for e in range(2)])

    def together(*keys):
        for key, value in zip(keys, lax.optimization_barrier(tuple(got[key] for key in keys))):
            got[key] = value

    got = {(0, 0, 0): x}
    got[-1, 0, 0], got[1, 0, 0] = along(x, (0, 1, 2), 1), along(x, (1, 2, 3), -1)
    got[0, 1, 0] = beside(x, (0, 1, 2, 3))
    together((-1, 0, 0), (1, 0, 0), (0, 1, 0))
    got[-2, 0, 0], got[2, 0, 0] = along(got[-1, 0, 0], (1, 2), 1), along(got[1, 0, 0], (1, 2), -1)
    got[-1, 1, 0], got[1, 1, 0] = beside(got[-1, 0, 0], (1, 2, 3)), beside(got[1, 0, 0], (0,))
    together((-2, 0, 0), (2, 0, 0), (-1, 1, 0), (1, 1, 0), (1, 0, 0))
    got[-3, 0, 0], got[3, 0, 0] = along(got[-2, 0, 0], (2,), 1), along(got[2, 0, 0], (1,), -1)
    got[1, 1, 1] = beside(got[1, 0, 0], (1, 2))
    got[-2, 1, 0], got[2, 1, 0] = beside(got[-2, 0, 0], (3,)), beside(got[2, 0, 0], (0,))
    together((-3, 0, 0), (3, 0, 0), (1, 1, 1), (-2, 1, 0), (2, 1, 0), (-2, 0, 0), (2, 0, 0))
    got[-3, 0, 0], *rider = lax.optimization_barrier((got[-3, 0, 0], *rider))
    got[-2, 1, 1], got[2, 1, 1] = beside(got[-2, 0, 0], (2,)), beside(got[2, 0, 0], (1,))
    got[-3, 1, 0], got[3, 1, 0] = beside(got[-3, 0, 0], (3,)), beside(got[3, 0, 0], (0,))
    return got, rider


def line_part(place, steps, side):
    first = {(1, 1): (0,), (-2, 1): (3,), (2, 1): (0,)}.get((steps, side))
    return (steps, side, 0 if first is None or place in first else 1)


def swap_all(values):
    return lax.all_to_all(values, BOTH, 0, 0)


def tell_all(values):
    count = lax.axis_size("row") * lax.axis_size("ch")
    return swap_all(jnp.broadcast_to(values[None], (count,) + values.shape))


def tell_row(values):
    count = lax.axis_size("row")
    return lax.all_to_all(jnp.broadcast_to(values[None], (count,) + values.shape), "row", 0, 0)


def vector_tile(*vectors):
    rows = [jnp.pad(v, (0, 256 - v.shape[0])).reshape(2, 128) for v in vectors]
    return jnp.pad(jnp.concatenate(rows), ((0, 8 - 2 * len(rows)), (0, 0)))


def to_next(x):
    count = lax.axis_size("row") * lax.axis_size("ch")
    return lax.ppermute(x, BOTH, [(i, i + 1) for i in range(count - 1)])


def to_previous(x):
    count = lax.axis_size("row") * lax.axis_size("ch")
    return lax.ppermute(x, BOTH, [(i + 1, i) for i in range(count - 1)])


def local_moments(x, valid):
    count = jnp.sum(valid)
    mean = jnp.sum(x * valid[None], axis=1) / jnp.maximum(count, 1.0)
    centered = (x - mean[:, None]) * valid[None]
    return mean, jnp.sum(centered * centered, axis=1)


def merge_moments(means, spreads, counts, total):
    mean = jnp.sum(means * counts[:, None], axis=0) / total
    away = means - mean[None]
    var = (jnp.sum(spreads, axis=0) + jnp.sum(counts[:, None] * away * away, axis=0)) / total
    return mean, lax.rsqrt(var + EPSILON)


def silu_slope(y):
    gate = jax.nn.sigmoid(y)
    return gate * (1.0 + y * (1.0 - gate))


def rows_per_step(rows):
    for step in (6, 4, 3, 2):
        if rows % step == 0:
            return step
    return 1


def pack_vectors(out_ref, first, second, more=None):
    more = jnp.zeros((4, 128), F32) if more is None else more
    tile = jnp.concatenate([first[:, :128], first[:, 128:], second[:, :128], second[:, 128:], more], axis=0)
    out_ref[:, :8] = jnp.broadcast_to(tile[None], (out_ref.shape[0], 8, 128))


def as_rows(columns):
    channels = columns[0].shape[0]
    lane = lax.broadcasted_iota(jnp.int32, (channels, 128), 1)
    block = jnp.zeros((channels, 128), F32)
    for i, column in enumerate(columns):
        block = jnp.where(lane == i, column, block)
    turned = block.T
    if channels < 256:
        turned = jnp.concatenate([turned, jnp.zeros((128, 256 - channels), F32)], axis=1)
    return [turned[i : i + 1] for i in range(len(columns))]


def as_columns(rows, channels):
    block = jnp.concatenate(rows + [jnp.zeros((8 - len(rows), rows[0].shape[1]), F32)], axis=0)
    turned = block.T
    return [turned[:channels, i : i + 1] for i in range(len(rows))]


def told_vectors(told):
    return jnp.concatenate([told[:, 0], told[:, 1]], axis=1), jnp.concatenate([told[:, 2], told[:, 3]], axis=1)


def merged(told, counts, inverse):
    means, spreads = told_vectors(told)
    mean = jnp.sum(means * counts, axis=0, keepdims=True) * inverse
    away = means - mean
    var = jnp.sum(spreads + counts * (away * away), axis=0, keepdims=True) * inverse
    return mean, lax.rsqrt(var + EPSILON)


def norm_columns(told_ref, counts_ref, inverse, gain_rows, channels, first=0):
    mean, scale = merged(told_ref[:, first : first + 4], counts_ref[...], inverse)
    return as_columns([mean, scale, gain_rows[0:1], gain_rows[1:2]], channels)


def sums_columns(told_ref, channels):
    first, second = told_vectors(told_ref[...])
    return as_columns([jnp.sum(first, axis=0, keepdims=True), jnp.sum(second, axis=0, keepdims=True)], channels)


def normed_of(pre, cols):
    return (pre - cols[0]) * cols[1]


def activation(pre, cols, valid):
    y = cols[2] * normed_of(pre, cols) + cols[3]
    return (y * jax.nn.sigmoid(y) * valid).astype(BF)


def fold(x):
    total = x[:, :128]
    for at in range(128, x.shape[1], 128):
        total = total + x[:, at : at + 128]
    return total


def moments_step(v, valid, state_ref, first):
    @pl.when(first)
    def _():
        count = jnp.maximum(jnp.sum(valid), 1.0)
        state_ref[0] = jnp.broadcast_to(jnp.sum(v * valid, axis=1, keepdims=True) / count, state_ref.shape[1:])
        state_ref[1] = jnp.zeros(state_ref.shape[1:], F32)
        state_ref[2] = jnp.zeros(state_ref.shape[1:], F32)

    away = (v - state_ref[0, :, 0:1]) * valid
    state_ref[1] += fold(away)
    state_ref[2] += fold(away * away)


def moments_end(state_ref, count, out_ref):
    total = jnp.sum(state_ref[1], axis=1, keepdims=True)
    squares = jnp.sum(state_ref[2], axis=1, keepdims=True)
    mean = state_ref[0, :, 0:1] + total / count
    pack_vectors(out_ref, *as_rows([mean, squares - total * total / count]))


def sums_step(dy, normed, state_ref, first):
    @pl.when(first)
    def _():
        state_ref[...] = jnp.zeros_like(state_ref)

    state_ref[0] += fold(dy)
    state_ref[1] += fold(dy * normed)


def sums_end(state_ref, out_ref):
    pack_vectors(out_ref, *as_rows([jnp.sum(state_ref[i], axis=1, keepdims=True) for i in range(2)]))


def ext_parts(rows_ext, piece):
    own = rows_ext * WF - 2 * WF
    yield 0, slice(0, WF), slice(0, WF)
    for start, size in tiles(own, piece):
        yield 1, slice(start, start + size), slice(WF + start, WF + start + size)
    yield 2, slice(0, WF), slice(WF + own, 2 * WF + own)


def stacked(a_ref, start, lanes, mask_ref, flip, rows):
    first, last = (1, 0) if flip else (0, 1)
    before = a_ref[rows, pl.ds(start, lanes)]
    middle = a_ref[rows, pl.ds(start + WF, lanes)]
    after = a_ref[rows, pl.ds(start + 2 * WF, lanes)]
    before = before * mask_ref[0:1, pl.ds(start, lanes)].astype(BF)
    after = after * mask_ref[1:2, pl.ds(start, lanes)].astype(BF)
    return [after, middle, before] if flip else [before, middle, after]


def columns_joined(acc, outs, flip):
    lanes = acc.shape[1]
    col = lax.broadcasted_iota(jnp.int32, (1, lanes), 1) % WF
    left, right = (acc[2 * outs :], acc[:outs]) if flip else (acc[:outs], acc[2 * outs :])
    left = jnp.where(col > 0, pltpu.roll(left, 1, 1), 0.0)
    right = jnp.where(col < WF - 1, pltpu.roll(right, lanes - 1, 1), 0.0)
    return acc[outs : 2 * outs] + left + right


def forward_weights(w_ref, up, out_ref):
    devices, _, outs, cin = w_ref.shape
    wide, extra = devices * outs, cin - up
    for c in range(devices):
        for b in range(3):
            rows = slice(b * wide + c * outs, b * wide + (c + 1) * outs)
            for a in range(3):
                piece = w_ref[c, 3 * a + b]
                out_ref[rows, a * up : (a + 1) * up] = piece[:, :up]
                if extra:
                    at = 3 * up + a * extra
                    out_ref[rows, at : at + extra] = piece[:, up:]


def backward_weights(w_ref, up, out_ref):
    devices, _, outs, cin = w_ref.shape
    wide, extra = devices * outs, cin - up
    for a in range(3):
        for b in range(3):
            whole = jnp.concatenate([w_ref[c, 3 * a + b] for c in range(devices)], axis=0).astype(F32)
            columns = slice(a * wide, (a + 1) * wide)
            out_ref[b * up : (b + 1) * up, columns] = whole[:, :up].T.astype(BF)
            if extra:
                tail = jnp.concatenate([whole[:, up:], jnp.zeros((wide, 128 - extra), F32)], axis=1).T
                at = 3 * up + b * extra
                out_ref[at : at + extra, columns] = tail[:extra].astype(BF)


def first_kernel(
    lanes,
    proj_prev, proj_own, proj_next, told_proj, counts_c, proj_gain, window_valid,
    enlarge, low_prev, low_own, low_next, told_low, counts_f, low_gain, valid_ext, mask, w_all, scalars,
    a_ref, out_ref, top_ref, bottom_ref, stats_ref, coarse_ref, w_ref, state_ref,
):
    step, last = pl.program_id(0), pl.num_programs(0) - 1
    up = proj_own.shape[0]
    margin, share = proj_prev.shape[1], proj_own.shape[1]

    @pl.when(step == 0)
    def _():
        forward_weights(w_all, up, w_ref)
        cols = norm_columns(told_proj, counts_c, scalars[0], proj_gain, up)
        for ref, start in ((proj_prev, 0), (proj_own, margin), (proj_next, margin + share)):
            part = slice(start, start + ref.shape[1])
            coarse_ref[:, part] = activation(ref[...], cols, window_valid[:, part])
        ext = a_ref.shape[1]
        for start, size in tiles(ext, 512):
            a_ref[:up, start : start + size] = dot(coarse_ref[...], enlarge[:, start : start + size]).astype(BF)
        cols = norm_columns(told_low, counts_f, scalars[1], low_gain, LOWC, 4)
        for which, part, there in ext_parts(ext // WF, 1536):
            a_ref[up:, there] = activation((low_prev, low_own, low_next)[which][:, part], cols, valid_ext[:, there])

    start = pl.multiple_of(step * lanes, 128)
    taps = stacked(a_ref, start, lanes, mask, False, slice(0, up)) + stacked(a_ref, start, lanes, mask, False, slice(up, up + LOWC))
    acc = dot(w_ref[...], jnp.concatenate(taps, axis=0))
    conv_end(acc, False, step, last, start, lanes, valid_ext, out_ref, top_ref, bottom_ref, stats_ref, state_ref)


def conv_end(acc, flip, step, last, start, lanes, valid_ext, out_ref, top_ref, bottom_ref, stats_ref, state_ref):
    outs = out_ref.shape[0]
    v = columns_joined(acc, outs, flip)
    out_ref[...] = v
    moments_step(v, valid_ext[:, pl.ds(start + WF, lanes)], state_ref, step == 0)

    @pl.when(step == 0)
    def _():
        top_ref[...] = v[:, :WF]

    @pl.when(step == last)
    def _():
        bottom_ref[...] = v[:, lanes - WF :]
        count = jnp.maximum(jnp.sum(valid_ext[:, WF : valid_ext.shape[1] - WF]), 1.0)
        moments_end(state_ref, count, stats_ref)


def second_kernel(
    lanes, prev, own, after, told, counts, gain, valid_ext, mask, w_all, scalars,
    a_ref, out_ref, top_ref, bottom_ref, stats_ref, w_ref, state_ref,
):
    step, last = pl.program_id(0), pl.num_programs(0) - 1

    @pl.when(step == 0)
    def _():
        forward_weights(w_all, w_all.shape[3], w_ref)
        cols = norm_columns(told, counts, scalars[1], gain, a_ref.shape[0])
        for which, part, there in ext_parts(a_ref.shape[1] // WF, 768):
            a_ref[:, there] = activation((prev, own, after)[which][:, part], cols, valid_ext[:, there])

    start = pl.multiple_of(step * lanes, 128)
    taps = stacked(a_ref, start, lanes, mask, False, slice(None))
    acc = dot(w_ref[...], jnp.concatenate(taps, axis=0))
    conv_end(acc, False, step, last, start, lanes, valid_ext, out_ref, top_ref, bottom_ref, stats_ref, state_ref)


def class_kernel(
    pre, cotangent, valid, told, counts, gain, w_cls, w_turned, bias, scalars,
    logits_ref, weights_ref, bias_ref, sums_ref, state_ref, cols_ref,
):
    step, last = pl.program_id(0), pl.num_programs(0) - 1
    classes = logits_ref.shape[0]

    @pl.when(step == 0)
    def _():
        for i, col in enumerate(norm_columns(told, counts, scalars[1], gain, pre.shape[0])):
            cols_ref[:, i : i + 1] = col
        weights_ref[...] = jnp.zeros_like(weights_ref)
        bias_ref[...] = jnp.zeros_like(bias_ref)

    cols = [cols_ref[:, i : i + 1] for i in range(4)]
    normed = normed_of(pre[...], cols)
    y = cols[2] * normed + cols[3]
    gate = jax.nn.sigmoid(y)
    act = (y * gate * valid[...]).astype(BF)
    logits_ref[...] = (dot(w_cls[...], act) + bias[...])[:classes]
    weights_ref[...] += dot_nt(cotangent[...], act)
    bias_ref[...] += fold(cotangent[...].astype(F32))
    d = dot(w_turned[...], cotangent[...]).astype(BF).astype(F32)
    dy = d * (gate * (1.0 + y * (1.0 - gate)) * valid[...])
    sums_step(dy, normed, state_ref, step == 0)

    @pl.when(step == last)
    def _():
        sums_end(state_ref, sums_ref)


def back_dz(dy, normed, cols, sums, valid, inverse):
    return ((cols[1] * cols[2]) * (dy - (sums[0] + normed * sums[1]) * (valid * inverse))).astype(BF)


def second_back_kernel(
    lanes,
    prev, own, after, told, counts, gain, sums, cot_prev, cot_own, cot_after, w_turned, valid_ext, mask, w_all,
    first_pre, told_first, gain_first, riders, scalars,
    dz_ref, dy_ref, top_ref, bottom_ref, sums_ref, w_ref, state_ref, cols_ref,
):
    step, last = pl.program_id(0), pl.num_programs(0) - 1

    @pl.when(step == 0)
    def _():
        backward_weights(w_all, w_all.shape[3], w_ref)
        channels = dz_ref.shape[0]
        cols = norm_columns(told, counts, scalars[1], gain, channels)
        totals = sums_columns(sums, channels)
        for which, part, there in ext_parts(dz_ref.shape[1] // WF, 768):
            pre, cot = ((prev, cot_prev), (own, cot_own), (after, cot_after))[which]
            normed = normed_of(pre[:, part], cols)
            valid = valid_ext[:, there]
            d = dot(w_turned[...], cot[:, part]).astype(BF).astype(F32)
            dy = d * silu_slope(cols[2] * normed + cols[3]) * valid
            dz_ref[:, there] = back_dz(dy, normed, cols, totals, valid, scalars[1])
        for i, col in enumerate(norm_columns(told_first, counts, scalars[1], gain_first, channels)):
            cols_ref[:, i : i + 1] = col

    start = pl.multiple_of(step * lanes, 128)
    taps = stacked(dz_ref, start, lanes, mask, True, slice(None))
    acc = dot(w_ref[...], jnp.concatenate(taps, axis=0))
    grad = columns_joined(acc, dy_ref.shape[0], True)
    cols = [cols_ref[:, i : i + 1] for i in range(4)]
    normed = normed_of(first_pre[...], cols)
    dy = grad * silu_slope(cols[2] * normed + cols[3]) * valid_ext[:, pl.ds(start + WF, lanes)]
    dy_ref[...] = dy
    sums_step(dy, normed, state_ref, step == 0)

    @pl.when(step == 0)
    def _():
        top_ref[...] = dy[:, :WF]

    @pl.when(step == last)
    def _():
        bottom_ref[...] = dy[:, lanes - WF :]
        sums_end(state_ref, sums_ref)
        sums_ref[:, 8:] = riders[...]


def first_back_kernel(
    lanes,
    prev, own, after, dy_prev, dy_own, dy_after, told, counts, gain, sums, valid_ext, mask, w_all,
    enlarge, low_pre, told_low, low_gain, scalars,
    dz_ref, window_ref, low_ref, low_sums_ref, w_ref, state_ref, cols_ref,
):
    step, last = pl.program_id(0), pl.num_programs(0) - 1
    up = window_ref.shape[0]

    @pl.when(step == 0)
    def _():
        backward_weights(w_all, up, w_ref)
        channels = dz_ref.shape[0]
        cols = norm_columns(told, counts, scalars[1], gain, channels)
        totals = sums_columns(sums, channels)
        for which, part, there in ext_parts(dz_ref.shape[1] // WF, 768):
            pre, dy = ((prev, dy_prev), (own, dy_own), (after, dy_after))[which]
            normed = normed_of(pre[:, part], cols)
            dz_ref[:, there] = back_dz(dy[:, part], normed, cols, totals, valid_ext[:, there], scalars[1])
        for i, col in enumerate(norm_columns(told_low, counts, scalars[1], low_gain, LOWC, 4)):
            cols_ref[:, i : i + 1] = col
        window_ref[...] = jnp.zeros_like(window_ref)

    start = pl.multiple_of(step * lanes, 128)
    taps = stacked(dz_ref, start, lanes, mask, True, slice(None))
    acc = dot(w_ref[...], jnp.concatenate(taps, axis=0))
    grad = columns_joined(acc[: 3 * up], up, True)
    high = grad.astype(BF)
    rest = (grad - high.astype(F32)).astype(BF)
    part = enlarge[:, pl.ds(start + WF, lanes)]
    window_ref[...] += dot_nt(high, part) + dot_nt(rest, part)
    cols = [cols_ref[:, i : i + 1] for i in range(4)]
    normed = normed_of(low_pre[...], cols)
    dy = columns_joined(acc[3 * up :], LOWC, True)
    dy = dy * silu_slope(cols[2] * normed + cols[3]) * valid_ext[:, pl.ds(start + WF, lanes)]
    low_ref[...] = dy
    sums_step(dy, normed, state_ref, step == 0)

    @pl.when(step == last)
    def _():
        for i in range(2):
            low_sums_ref[i : i + 1] = as_rows([jnp.sum(state_ref[i], axis=1, keepdims=True)])[0]


def decoder_weight_kernel(lanes, outs, dz_ref, a_ref, mask_ref, *refs):
    step = pl.program_id(0)
    start = pl.multiple_of(step * lanes, 128)
    acc_ref = refs[-1]
    wide = dz_ref.shape[0]
    up, extra = wide, a_ref.shape[0] - wide

    @pl.when(step == 0)
    def _():
        acc_ref[...] = jnp.zeros_like(acc_ref)

    taps = stacked(a_ref, start, lanes, mask_ref, False, slice(0, up))
    if a_ref.shape[0] > up:
        taps = taps + stacked(a_ref, start, lanes, mask_ref, False, slice(up, None))
    dz = dz_ref[:, pl.ds(start + WF, lanes)]
    col = lax.broadcasted_iota(jnp.int32, (1, lanes), 1) % WF
    left = pltpu.roll(dz, lanes - 1, 1) * (col < WF - 1).astype(F32).astype(BF)
    right = pltpu.roll(dz, 1, 1) * (col > 0).astype(F32).astype(BF)
    acc_ref[...] += dot_nt(jnp.concatenate([left, dz, right], axis=0), jnp.concatenate(taps, axis=0))

    @pl.when(step == pl.num_programs(0) - 1)
    def _():
        for c in range(wide // outs):
            for b in range(3):
                rows = slice(b * wide + c * outs, b * wide + (c + 1) * outs)
                for a in range(3):
                    refs[0][c, 3 * a + b, :, :up] = acc_ref[rows, a * up : (a + 1) * up].astype(BF)
                    if extra:
                        at = 3 * up + a * extra
                        refs[0][c, 3 * a + b, :, up:] = acc_ref[rows, at : at + extra].astype(BF)


def decoder_weight_grad(dz, a, masks, outs):
    wide, pixels = dz.shape[0], dz.shape[1] - 2 * WF
    cin = a.shape[0]
    lanes = WF * rows_per_step(pixels // WF)
    devices = wide // outs
    whole = pl.BlockSpec(memory_space=pltpu.VMEM)
    return pl.pallas_call(
        lambda *refs: decoder_weight_kernel(lanes, outs, *refs),
        grid=(pixels // lanes,),
        in_specs=[whole] * 3,
        out_specs=whole,
        out_shape=jax.ShapeDtypeStruct((devices, 9, outs, cin), BF),
        scratch_shapes=[pltpu.VMEM((3 * wide, 3 * cin), F32)],
        compiler_params=params(),
        cost_estimate=pl.CostEstimate(flops=18 * cin * wide * pixels, bytes_accessed=2 * (cin + wide) * pixels, transcendentals=0),
    )(dz, a, masks)


def decoder_call(kernel, operands, blocked, smem, outputs, blocked_out, scratch, pixels, flops):
    lanes = WF * rows_per_step(pixels // WF)
    whole = pl.BlockSpec(memory_space=pltpu.VMEM)
    run = lambda channels: pl.BlockSpec((channels, lanes), lambda i: (0, i))
    in_specs = [
        pl.BlockSpec(memory_space=pltpu.SMEM) if i in smem else run(v.shape[0]) if i in blocked else whole
        for i, v in enumerate(operands)
    ]
    out_specs = [run(v.shape[0]) if i in blocked_out else whole for i, v in enumerate(outputs)]
    return pl.pallas_call(
        kernel,
        grid=(pixels // lanes,),
        in_specs=in_specs,
        out_specs=out_specs,
        out_shape=outputs,
        scratch_shapes=scratch,
        compiler_params=params(),
        cost_estimate=pl.CostEstimate(flops=flops, bytes_accessed=16 * 256 * pixels, transcendentals=0),
    )(*operands)


def branch_kernel(centre, from_next, from_prev, valid, out_ref, pieces_ref, stats_ref):
    outs, pixels = centre.shape[1:]
    devices, _, share = pieces_ref.shape
    count = jnp.maximum(jnp.sum(valid[...]), 1.0)
    means, spreads = [], []
    for k in range(4):
        rows = slice(k * outs, (k + 1) * outs)
        v = centre[(k + 3) % 4]
        if k:
            v = v + jnp.concatenate([jnp.zeros((outs, pixels - PAD), F32), from_next[k - 1].astype(F32)], axis=1)
            v = v + jnp.concatenate([from_prev[k - 1].astype(F32), jnp.zeros((outs, pixels - PAD), F32)], axis=1)
        mean = jnp.sum(v * valid[...], axis=1, keepdims=True) / count
        v = (v - mean) * valid[...]
        means.append(mean)
        spreads.append(jnp.sum(v * v, axis=1, keepdims=True))
        out_ref[rows] = v.astype(BF)
        for i in range(devices):
            pieces_ref[i, rows] = v[:, i * share : (i + 1) * share].astype(BF)
    pack_vectors(stats_ref, *as_rows([jnp.concatenate(means, axis=0), jnp.concatenate(spreads, axis=0)]))


def project_kernel(
    swapped, told, counts, gains, w_ref, broad, valid, low_stats, scalars, places, out_ref, left_ref, right_ref, stats_ref
):
    devices, four, share = swapped.shape
    groups = told.shape[0]
    margin = left_ref.shape[1]
    mine = places[0]
    number = lax.broadcasted_iota(jnp.int32, (groups, 1), 0)
    total = broad[...]
    for j in range(devices):
        c = places[1 + j]
        group = told[:, c]
        mean, scale = merged(group, counts[...], scalars[0])
        here = jnp.sum(jnp.where(number == mine, told_vectors(group)[0], 0.0), axis=0, keepdims=True)
        cols = as_columns([mean - here, scale, gains[c, 0:1], gains[c, 1:2]], four)
        total = total + dot(w_ref[c], activation(swapped[j].astype(F32), cols, valid[...]))
    out_ref[...] = total
    left_ref[...] = total[:, :margin]
    right_ref[...] = total[:, share - margin :]
    count = jnp.maximum(jnp.sum(valid[...]), 1.0)
    mean = jnp.sum(total * valid[...], axis=1, keepdims=True) / count
    away = (total - mean) * valid[...]
    pack_vectors(stats_ref, *as_rows([mean, jnp.sum(away * away, axis=1, keepdims=True)]), low_stats[...])


def small_call(kernel, operands, smem, outputs, flops):
    whole = pl.BlockSpec(memory_space=pltpu.VMEM)
    return pl.pallas_call(
        kernel,
        in_specs=[pl.BlockSpec(memory_space=pltpu.SMEM) if i in smem else whole for i in range(len(operands))],
        out_specs=[whole] * len(outputs),
        out_shape=outputs,
        compiler_params=params(),
        cost_estimate=pl.CostEstimate(flops=flops, bytes_accessed=4000000, transcendentals=0),
    )(*operands)


def pyramid_kernel(blocks, outs, perm_ref, *refs):
    x_refs = refs[:blocks]
    w_ref, w_one_ref, mask_ref, centre_ref, up_ref, down_ref, acc_ref = refs[blocks:]
    k = pl.program_id(0)
    rate = 6 * (k + 1)
    depth, pixels = x_refs[0].shape

    def product(weights, width):
        for start, size in tiles(pixels, 512):
            total = None
            for j in range(blocks):
                at = pl.multiple_of(perm_ref[j] * depth, depth)
                part = dot(weights(at, depth), x_refs[j][:, start : start + size])
                total = part if total is None else total + part
            acc_ref[:width, start : start + size] = total

    @pl.when(k == 3)
    def _():
        product(lambda at, n: w_one_ref[:, pl.ds(at, n)], outs)
        centre_ref[0] = acc_ref[:outs]

    @pl.when(k < 3)
    def _():
        product(lambda at, n: w_ref[0, :, pl.ds(at, n)], 9 * outs)
        lane = lax.broadcasted_iota(jnp.int32, (1, pixels), 1)
        col, row = lane % WS, lane // WS
        for a in (0, 1, -1):
            tap = 3 * (a + 1) * outs
            left = pltpu.roll(acc_ref[tap : tap + outs], rate, 1)
            right = pltpu.roll(acc_ref[tap + 2 * outs : tap + 3 * outs], pixels - rate, 1)
            part = acc_ref[tap + outs : tap + 2 * outs] + jnp.where(col >= rate, left, 0.0) + jnp.where(col < WS - rate, right, 0.0)
            if a == 0:
                centre_ref[0] = part
                continue
            part = part * mask_ref[pl.ds(2 * k + (a + 1) // 2, 1)]
            if a == 1:
                moved = pltpu.roll(part, pixels - WS * rate, 1)
                inside = row < pixels // WS - rate
                up_ref[0] = jnp.where(inside, 0.0, moved)[:, pixels - PAD :].astype(BF)
            else:
                moved = pltpu.roll(part, WS * rate, 1)
                inside = row >= rate
                down_ref[0] = jnp.where(inside, 0.0, moved)[:, :PAD].astype(BF)
            centre_ref[0] += jnp.where(inside, moved, 0.0)


def pyramid(x_blocks, perm, w_taps, w_one, masks):
    depth, pixels = x_blocks[0].shape
    outs, cin = w_one.shape
    whole = pl.BlockSpec(memory_space=pltpu.VMEM)
    third = lambda k, p: (jnp.minimum(k, 2), 0, 0)
    return pl.pallas_call(
        lambda *refs: pyramid_kernel(len(x_blocks), outs, *refs),
        grid_spec=pltpu.PrefetchScalarGridSpec(
            num_scalar_prefetch=1,
            grid=(4,),
            in_specs=[whole] * len(x_blocks)
            + [pl.BlockSpec((1, 9 * outs, cin), third), whole, whole],
            out_specs=[
                pl.BlockSpec((1, outs, pixels), lambda k, p: (k, 0, 0)),
                pl.BlockSpec((1, outs, PAD), third),
                pl.BlockSpec((1, outs, PAD), third),
            ],
            scratch_shapes=[pltpu.VMEM((9 * outs, pixels), F32)],
        ),
        out_shape=[
            jax.ShapeDtypeStruct((4, outs, pixels), F32),
            jax.ShapeDtypeStruct((3, outs, PAD), BF),
            jax.ShapeDtypeStruct((3, outs, PAD), BF),
        ],
        compiler_params=params(),
        cost_estimate=pl.CostEstimate(flops=2 * 28 * outs * cin * pixels, bytes_accessed=2 * (28 * outs + pixels) * cin, transcendentals=0),
    )(perm, *x_blocks, w_taps, w_one, masks)


def shifted_taps(read, lanes, rate, masks, store):
    col = lax.broadcasted_iota(jnp.int32, (1, lanes), 1) % WS
    for a in (-1, 0, 1):
        for b in (-1, 0, 1):
            shift = rate * (WS * a + b)
            first = (PAD - shift) // 128 * 128
            rest = PAD - shift - first
            window = read(first, lanes + 128)
            if rest:
                window = pltpu.roll(window, lanes + 128 - rest, 1)
            keep = ((col - b * rate >= 0) & (col - b * rate < WS)).astype(F32)
            if a:
                keep = keep * masks[(a + 1) // 2]
            store(3 * (a + 1) + b + 1, window[:, :lanes] * keep.astype(BF))


def dot_tn(a, b):
    return lax.dot_general(a, b, (((0,), (0,)), ((), ())), preferred_element_type=F32)


def input_grad_kernel(outs, dz_ref, spread_ref, mask_ref, w_ref, one_ref, pool_ref, out_ref, taps_ref):
    pixels = spread_ref.shape[1]

    @pl.when(pl.program_id(0) == 0)
    def _():
        for k in range(3):
            def store(tap, value, k=k):
                at = (9 * k + tap) * outs
                taps_ref[at : at + outs] = value

            masks = (mask_ref[2 * k : 2 * k + 1], mask_ref[2 * k + 1 : 2 * k + 2])
            rows = (k + 1) * outs
            shifted_taps(lambda first, n: dz_ref[rows : rows + outs, first : first + n], pixels, 6 * (k + 1), masks, store)
        taps_ref[27 * outs : 28 * outs] = dz_ref[:outs, PAD : PAD + pixels]
        taps_ref[28 * outs :] = spread_ref[...]

    weights = jnp.concatenate([w_ref[...], one_ref[...], pool_ref[...]], axis=0)
    for start, size in tiles(pixels, 512):
        out_ref[0, :, start : start + size] = dot_tn(weights, taps_ref[:, start : start + size]).astype(BF)


def input_grad(dz, spread, masks, w_taps, w_one, w_pool, perm):
    pixels = spread.shape[1]
    outs, cin = w_one.shape
    blocks = perm.shape[0]
    depth = cin // blocks
    whole = pl.BlockSpec(memory_space=pltpu.VMEM)
    slab = lambda rows: pl.BlockSpec((rows, depth), lambda i, p: (0, p[i]))

    def kernel(perm_ref, *refs):
        input_grad_kernel(outs, *refs)

    return pl.pallas_call(
        kernel,
        grid_spec=pltpu.PrefetchScalarGridSpec(
            num_scalar_prefetch=1,
            grid=(blocks,),
            in_specs=[whole, whole, whole, slab(27 * outs), slab(outs), slab(outs)],
            out_specs=pl.BlockSpec((1, depth, pixels), lambda i, p: (i, 0, 0)),
            scratch_shapes=[pltpu.VMEM((29 * outs, pixels), BF)],
        ),
        out_shape=jax.ShapeDtypeStruct((blocks, depth, pixels), BF),
        compiler_params=params(),
        cost_estimate=pl.CostEstimate(flops=2 * 29 * outs * cin * pixels, bytes_accessed=2 * (29 * outs + pixels) * cin, transcendentals=0),
    )(perm, dz, spread, masks, w_taps.reshape(27 * outs, cin), w_one, w_pool)


def pyramid_weight_kernel(lanes, outs, branches, plain, dz_ref, mask_ref, *refs):
    x_refs, (out_ref, taps_ref, acc_ref) = refs[:-3], refs[-3:]
    step = pl.program_id(0)
    start = pl.multiple_of(step * lanes, 128)

    @pl.when(step == 0)
    def _():
        acc_ref[...] = jnp.zeros_like(acc_ref)

    for n, k in enumerate(branches):
        def store(tap, value, n=n):
            at = (9 * n + tap) * outs
            taps_ref[at : at + outs] = value

        rows = slice((k + 1) * outs, (k + 2) * outs)
        masks = (mask_ref[0, 2 * k : 2 * k + 1], mask_ref[0, 2 * k + 1 : 2 * k + 2])
        shifted_taps(lambda first, n, rows=rows: dz_ref[rows, pl.ds(start + first, n)], lanes, 6 * (k + 1), masks, store)
    if plain:
        taps_ref[9 * len(branches) * outs :] = dz_ref[:outs, pl.ds(start + PAD, lanes)]
    acc_ref[...] += dot_nt(taps_ref[...], jnp.concatenate([x[0] for x in x_refs], axis=0))

    @pl.when(step == pl.num_programs(0) - 1)
    def _():
        out_ref[...] = acc_ref[...].astype(BF)


def pyramid_weight_grad(dz, x_blocks, places, masks, branches, plain):
    groups, slim, lanes = x_blocks[0].shape
    outs, canvas = dz.shape[0] // 4, groups * lanes
    channels = slim * len(x_blocks)
    out_rows = (9 * len(branches) + plain) * outs
    whole = pl.BlockSpec(memory_space=pltpu.VMEM)

    def kernel(places_ref, *refs):
        pyramid_weight_kernel(lanes, outs, branches, plain, *refs)

    return pl.pallas_call(
        kernel,
        grid_spec=pltpu.PrefetchScalarGridSpec(
            num_scalar_prefetch=1,
            grid=(groups,),
            in_specs=[whole, pl.BlockSpec((1, 8, lanes), lambda i, p: (i, 0, 0))]
            + [pl.BlockSpec((1, slim, lanes), lambda i, p: (p[i], 0, 0))] * len(x_blocks),
            out_specs=whole,
            scratch_shapes=[pltpu.VMEM((out_rows, lanes), BF), pltpu.VMEM((out_rows, channels), F32)],
        ),
        out_shape=jax.ShapeDtypeStruct((out_rows, channels), BF),
        compiler_params=params(),
        cost_estimate=pl.CostEstimate(flops=2 * out_rows * channels * canvas, bytes_accessed=2 * (4 * outs + channels) * canvas, transcendentals=0),
    )(places, dz, masks, *x_blocks)


def canvas_kernel(groups, devices, outs, stack_size, count, tab_top, tab_low, *refs):
    piece_refs, refs = refs[: 4 * devices], refs[4 * devices :]
    centred_ref, valid_ref, member_ref, w_ref, cols_ref, offset_ref = refs[:6]
    dz_ref, sums_ref, proj_ref, image_ref, pieces_ref, dy_ref = refs[6:]
    step = pl.program_id(0)
    four = 4 * outs
    half, share = piece_refs[0].shape[1:]
    pixels = share * devices
    group = lax.rem(step, groups)
    gain, shift, scale, mean = (cols_ref[:, i : i + 1] for i in range(4))
    lane = lax.broadcasted_iota(jnp.int32, offset_ref.shape, 1)
    offset = jnp.sum(jnp.where(lane == group, offset_ref[...], 0.0), axis=1, keepdims=True) - mean
    valid = valid_ref[0, 6:7]
    at = pl.multiple_of(group * pixels, 128)

    @pl.when(step == 0)
    def _():
        sums_ref[...] = jnp.zeros_like(sums_ref)
        proj_ref[...] = jnp.zeros_like(proj_ref)
        image_ref[...] = jnp.zeros_like(image_ref)
        dz_ref[:, :PAD] = jnp.zeros((four, PAD), BF)
        dz_ref[:, PAD + groups * pixels :] = jnp.zeros((four, PAD), BF)

    @pl.when(step < groups)
    def _():
        for i in range(devices):
            for h, table in enumerate((tab_top, tab_low)):
                own, near = piece_refs[4 * i + 2 * h], piece_refs[4 * i + 2 * h + 1]
                is_own = table[group * devices + i] < stack_size
                rows, part = slice(h * half, (h + 1) * half), slice(i * share, (i + 1) * share)
                pieces_ref[rows, part] = jnp.where(is_own, own[0], near[0])
        image_ref[...] += dot_nt(pieces_ref[...], member_ref[0].astype(BF))
        total = jnp.zeros((four, 128), F32)
        total_normed = jnp.zeros((four, 128), F32)
        for start, size in tiles(pixels, 384):
            part = slice(start, start + size)
            normed = (centred_ref[0, :, part].astype(F32) + offset) * scale
            y = gain * normed + shift
            gate = jax.nn.sigmoid(y)
            act = (y * gate * valid[:, part]).astype(BF)
            proj_ref[...] += dot_nt(pieces_ref[:, part], act)
            slope = gate * (1.0 + y * (1.0 - gate)) * valid[:, part]
            dy = dot(w_ref[...], pieces_ref[:, part]) * slope
            dy_ref[:, pl.ds(at + start, size)] = dy
            both = dy * normed
            for tile in range(0, size, 128):
                total = total + dy[:, tile : tile + 128]
                total_normed = total_normed + both[:, tile : tile + 128]
        sums_ref[:, 0:1] += jnp.sum(total, axis=1, keepdims=True)
        sums_ref[:, 1:2] += jnp.sum(total_normed, axis=1, keepdims=True)

    @pl.when(step >= groups)
    def _():
        normed = (centred_ref[0].astype(F32) + offset) * scale
        parts = (sums_ref[:, 0:1] + normed * sums_ref[:, 1:2]) * (valid * count[0])
        dz = (scale * gain) * (dy_ref[:, pl.ds(at, pixels)] - parts)
        dz_ref[:, pl.ds(PAD + at, pixels)] = dz.astype(BF)


def canvas_grad(top, low, tables, centred, valid, member, w_turned, cols, offsets, inverse_count):
    groups, four, pixels = centred.shape
    stack_size, half, share = top[0].shape
    devices = tables[0].shape[0] // groups
    wide = 2 * half

    def piece(i, table):
        def index(s, top_table, low_table):
            at = jnp.minimum(s, groups - 1) * devices + i
            return (lax.rem((top_table if table == 0 else low_table)[at], stack_size), 0, 0)

        return pl.BlockSpec((1, half, share), index)

    by_group = lambda s, a, b: (lax.rem(s, groups), 0, 0)
    whole = pl.BlockSpec(memory_space=pltpu.VMEM)

    def kernel(tab_top, tab_low, *refs):
        canvas_kernel(groups, devices, four // 4, stack_size, refs[-7], tab_top, tab_low, *refs[:-7], *refs[-6:])

    return pl.pallas_call(
        kernel,
        grid_spec=pltpu.PrefetchScalarGridSpec(
            num_scalar_prefetch=2,
            grid=(2 * groups,),
            in_specs=[piece(i, table) for i in range(devices) for table in (0, 0, 1, 1)]
            + [
                pl.BlockSpec((1, four, pixels), by_group),
                pl.BlockSpec((1, 8, pixels), by_group),
                pl.BlockSpec((1, member.shape[1], pixels), by_group),
                whole,
                whole,
                whole,
                pl.BlockSpec(memory_space=pltpu.SMEM),
            ],
            out_specs=[whole] * 4,
            scratch_shapes=[pltpu.VMEM((wide, pixels), BF), pltpu.VMEM((four, groups * pixels), F32)],
        ),
        out_shape=[
            jax.ShapeDtypeStruct((four, 2 * PAD + groups * pixels), BF),
            jax.ShapeDtypeStruct((four, 128), F32),
            jax.ShapeDtypeStruct((wide, four), F32),
            jax.ShapeDtypeStruct((wide, member.shape[1]), F32),
        ],
        compiler_params=params(),
        cost_estimate=pl.CostEstimate(flops=4 * wide * four * groups * pixels, bytes_accessed=8 * wide * groups * pixels, transcendentals=four * groups * pixels),
    )(*tables, *([*top, *low] * devices), centred, valid, member, w_turned, cols, offsets, inverse_count)


def assembly_kernel(groups, devices, order, where_ref, perm_ref, pieces, plain, out_ref, one_ref):
    line = groups // 2
    cin = out_ref.shape[1]
    depth = cin // devices
    slim = depth // groups

    def fill(refs, target):
        for r in range(0, groups, 2):
            for j in range(devices):
                part = slice(j * slim, (j + 1) * slim)
                pair = jnp.concatenate([refs[r][:, part], refs[r + 1][:, part]], axis=1)
                at = pl.multiple_of(perm_ref[j] * depth + r * slim, 128)
                target[:, pl.ds(at, 2 * slim)] = pair.astype(F32)

    for z in range(line):
        for e in range(2):
            chosen = [order.index(line_part(z, r // 2 - z, (r ^ e) & 1)) for r in range(groups)]

            @pl.when((where_ref[0] // 2 == z) & (where_ref[0] % 2 == e))
            def _(chosen=chosen):
                fill([pieces[i] for i in chosen], out_ref)
                if one_ref is not None:

                    @pl.when(pl.program_id(0) == 0)
                    def _():
                        fill([plain[i] for i in chosen], one_ref)


def assemble(branches, plain, found, devices, groups, strip, perm, into, outs, cin):
    order = sorted(found)
    pieces = [found[key] for key in order]
    slots, width = len(pieces), pieces[0].shape[1]
    rows = 3 * outs
    smem = pl.BlockSpec(memory_space=pltpu.SMEM)
    operands = [strip[None].astype(jnp.int32), perm] + pieces
    in_specs = [smem, smem] + [pl.BlockSpec((rows, width), lambda i: (i, 0))] * slots
    first = 3 * branches[0]
    out_specs = [pl.BlockSpec((rows, cin), lambda i: (first + i, 0))]
    out_shape = [jax.ShapeDtypeStruct((27 * outs, cin), F32)]
    if plain:
        operands += pieces
        in_specs += [pl.BlockSpec((outs, width), lambda i: (9 * len(branches), 0))] * slots
        out_specs.append(pl.BlockSpec((outs, cin), lambda i: (0, 0)))
        out_shape.append(jax.ShapeDtypeStruct((outs, cin), F32))
    aliases = {}
    if into is not None:
        aliases = {len(operands): 0}
        operands.append(into)
        in_specs.append(pl.BlockSpec(memory_space=pl.ANY))

    def kernel(where_ref, perm_ref, *refs):
        one_ref = refs[-1] if plain else None
        out_ref = refs[-2] if plain else refs[-1]
        assembly_kernel(groups, devices, order, where_ref, perm_ref, refs[:slots], refs[slots : 2 * slots], out_ref, one_ref)

    return pl.pallas_call(
        kernel,
        grid=(3 * len(branches),),
        in_specs=in_specs,
        out_specs=out_specs,
        out_shape=out_shape,
        input_output_aliases=aliases,
        compiler_params=params(),
        cost_estimate=pl.CostEstimate(flops=0, bytes_accessed=9 * len(branches) * outs * cin * 6, transcendentals=0),
    )(*operands)


def local(
    feats,
    lowlevel,
    heights,
    widths,
    w_one,
    w_atrous,
    w_pool,
    w_proj,
    w_low,
    w_dec1,
    w_dec2,
    w_cls,
    b_cls,
    mid_gain,
    mid_shift,
    low_gain,
    low_shift,
    dec_gain,
    dec_shift,
    cotangent,
):
    devices, groups = lax.axis_size("ch"), lax.axis_size("row")
    me, strip = lax.axis_index("ch"), lax.axis_index("row")
    place = strip * devices + me
    everyone = devices * groups
    depth, pixels = feats.shape
    rows = pixels // WS
    canvas = groups * pixels
    outs = w_one.shape[0]
    wide = outs * devices
    images = heights.shape[0]
    share = pixels // devices
    fine = 16 * share
    fine_rows = fine // WF
    margin = WS if fine_rows % 4 == 0 else 2 * WS

    area = (heights * widths).astype(F32)
    count = jnp.sum(area)
    fine_count = 16.0 * count
    scalars = jnp.stack([1.0 / count, 1.0 / fine_count])
    places = jnp.stack([strip, place]).astype(jnp.int32)
    members = -(-images // 16) * 16
    window = share + 2 * margin
    ext = fine + 2 * WF
    shaped = lambda *shape: jax.ShapeDtypeStruct(shape, F32)
    strip_rows, member_strip, valid_fine_strip = geometry_call(
        strip_geometry_kernel,
        heights, widths, places,
        [shaped(8, pixels), jax.ShapeDtypeStruct((members, pixels), BF), jax.ShapeDtypeStruct((1, 16 * pixels), BF)],
    )
    valid_strip = strip_rows[6:7]

    mine = feats * valid_strip.astype(BF)
    x_blocks, origin = gather_blocks(mine)
    perm = jnp.stack(origin).astype(jnp.int32)
    slice_depth = depth // groups
    x_slice = lax.all_to_all(mine.reshape(groups, slice_depth, pixels), "row", 0, 0)

    vectors = jnp.concatenate(
        [
            v.astype(F32).reshape(-1)
            for v in (mid_gain, mid_shift, dec_gain, dec_shift, low_gain, low_shift)
        ]
    )
    sums = dot_nt(mine, member_strip)[:, :images].reshape(-1)
    sums, x_slice = lax.optimization_barrier((jnp.concatenate([sums, vectors]), x_slice))
    told = tell_all(sums).reshape(groups, devices, -1)
    pool_sums = jnp.sum(told[:, :, : depth * images], axis=0).reshape(devices * depth, images)
    vectors = lax.dynamic_index_in_dim(told, strip, 0, False)[:, depth * images :]
    norm_rows = vectors[:, : 16 * outs].reshape(devices, 16, outs)
    gain_rows = [norm_rows[:, k].reshape(-1) for k in range(16)]
    branch_gains = jnp.stack([norm_rows[:, :4].reshape(devices, -1), norm_rows[:, 6:10].reshape(devices, -1)], axis=1)
    branch_gains = jnp.pad(branch_gains, ((0, 0), (0, 0), (0, 256 - 4 * outs)))
    proj_gain = jnp.stack([gain_rows[5], gain_rows[11]])
    first_gain = jnp.stack([gain_rows[12], gain_rows[14]])
    second_gain = jnp.stack([gain_rows[13], gain_rows[15]])
    low_share = LOWC // devices
    low_gain_all = vectors[:, 16 * outs : 16 * outs + low_share].reshape(-1)
    low_shift_all = vectors[:, 16 * outs + low_share : 16 * outs + 2 * low_share].reshape(-1)
    low_gains = jnp.pad(jnp.stack([low_gain_all, low_shift_all]), ((0, 0), (0, 256 - LOWC)))

    low_in = lowlevel * valid_fine_strip
    low_part = dot(w_low, low_in).astype(BF)
    low_pre = lax.psum_scatter(low_part, "ch", scatter_dimension=1, tiled=True).astype(F32)

    first_taps = w_dec1.transpose(1, 0, 2)
    w1 = lax.all_gather(jnp.concatenate([first_taps[:, :, LOWC:], first_taps[:, :, :LOWC]], axis=2), "ch", axis=0)
    proj_taps = w_proj.reshape(outs, 5, wide).transpose(1, 0, 2)
    pool_taps = w_pool.reshape(outs, -1, wide).transpose(1, 0, 2)
    rest = lax.all_gather(jnp.concatenate([w_dec2.transpose(1, 0, 2), proj_taps, pool_taps], axis=0), "ch", axis=0)
    w2, wp, w_pool_all = rest[:, :9], rest[:, 9:14], rest[:, 14:]
    wp_acts = wp[:, :4].reshape(devices, 4, outs, devices, outs).transpose(3, 0, 2, 1, 4).reshape(devices, wide, 4 * outs)
    wp_pool = wp[:, 4].reshape(wide, wide)

    pooled = (pool_sums / area[None]).astype(BF)
    pool_pre = jnp.einsum(
        "ckoi,kin->con", w_pool_all, pooled.reshape(-1, wide, images), preferred_element_type=F32
    ).reshape(wide, images)
    pool_mean = jnp.mean(pool_pre, axis=1)
    pool_scale = lax.rsqrt(jnp.mean(pool_pre * pool_pre, axis=1) - pool_mean * pool_mean + EPSILON)
    pool_normed = (pool_pre - pool_mean[:, None]) * pool_scale[:, None]
    gain_mid, shift_mid = mid_gain.astype(F32), mid_shift.astype(F32)
    pool_shifted = gain_rows[4][:, None] * pool_normed + gain_rows[10][:, None]
    pool_acts = jax.nn.silu(pool_shifted).astype(BF)
    broad_part = dot(wp_pool, pool_acts)
    own_rows = lambda v: lax.dynamic_slice_in_dim(v, me * outs, outs, axis=0)
    pool_act, pool_scale, pool_normed, pool_shifted = map(own_rows, (pool_acts, pool_scale, pool_normed, pool_shifted))

    w_taps = w_atrous.transpose(0, 2, 1, 3).reshape(3, 9 * outs, -1)
    centre, up, down = pyramid(x_blocks, perm, w_taps, w_one, strip_rows)
    up, down, places, low_pre = lax.optimization_barrier((up, down, places, low_pre))
    fwd = [(i, i + 1) for i in range(groups - 1)]
    bwd = [(i + 1, i) for i in range(groups - 1)]
    from_next = lax.ppermute(up, "row", bwd)
    from_prev = lax.ppermute(down, "row", fwd)

    (
        canvas_rows, member_canvas, strip_counts, counts_c, counts_f, mine_rows, window_valid, valid_wide, fine_masks, enlarge,
    ) = geometry_call(
        lambda *refs: geometry_kernel(margin, *refs),
        heights, widths, places,
        [
            shaped(groups, 8, pixels), shaped(groups, members, pixels), shaped(groups, 1), shaped(everyone, 1),
            shaped(everyone, 1), shaped(members + 8, share), shaped(1, window), shaped(1, ext), shaped(2, fine),
            jax.ShapeDtypeStruct((window, ext), BF),
        ],
    )
    member_mine, valid_mine = mine_rows[:images], mine_rows[members : members + 1]
    valid_fine = valid_wide[:, WF:-WF]
    broad_part = jnp.dot(broad_part, member_mine, precision=HIGHEST)
    low_stats = vector_tile(*local_moments(low_pre, valid_fine[0]))[:4]

    order = jnp.argsort(perm)
    x_places = jnp.arange(groups, dtype=jnp.int32)

    def columns(s, lead):
        s = s.reshape((groups,) + lead + (devices, slice_depth))
        s = jnp.take(s, order, axis=len(lead) + 1)
        s = jnp.moveaxis(s, 0, len(lead) + 1)
        return s.reshape(lead + (devices * depth,)).astype(F32)

    tile = jax.ShapeDtypeStruct((everyone, 8, 128), F32)
    centered, pieces, stats = small_call(
        branch_kernel,
        [centre, from_next, from_prev, valid_strip],
        (),
        [
            jax.ShapeDtypeStruct((4 * outs, pixels), BF),
            jax.ShapeDtypeStruct((devices, 4 * outs, share), BF),
            tile,
        ],
        0,
    )
    told_branch = swap_all(stats)
    swapped, x_slice = lax.optimization_barrier((swap_ch(pieces), x_slice))
    slice_blocks, _ = gather_blocks(x_slice)
    proj_pre, proj_left, proj_right, stats = small_call(
        project_kernel,
        [
            swapped, told_branch.reshape(groups, devices, 8, 128), strip_counts, branch_gains, wp_acts, broad_part,
            valid_mine, low_stats, scalars, jnp.concatenate([strip[None].astype(jnp.int32), perm]),
        ],
        (8, 9),
        [
            jax.ShapeDtypeStruct((wide, share), F32),
            jax.ShapeDtypeStruct((wide, margin), F32),
            jax.ShapeDtypeStruct((wide, margin), F32),
            tile,
        ],
        8 * wide * wide * share,
    )
    told_proj = swap_all(stats)
    proj_prev, proj_next = to_next(proj_right), to_previous(proj_left)
    low_prev, low_next = to_next(low_pre[:, -WF:]), to_previous(low_pre[:, :WF])
    canvas_centered = lax.all_gather(centered, "row", axis=0)

    lanes = WF * rows_per_step(fine_rows)
    edge = jax.ShapeDtypeStruct((wide, WF), F32)
    full = jax.ShapeDtypeStruct((wide, fine), F32)
    work = 18 * wide * wide * fine
    state = lambda n, channels: pltpu.VMEM((n, channels, 128), F32)
    decoder_in, first_pre, first_top, first_bottom, stats = decoder_call(
        lambda *refs: first_kernel(lanes, *refs),
        [
            proj_prev, proj_pre, proj_next, told_proj, counts_c, proj_gain, window_valid, enlarge, low_prev, low_pre, low_next,
            told_proj, counts_f, low_gains, valid_wide, fine_masks, w1, scalars,
        ],
        (), (17,),
        [jax.ShapeDtypeStruct((wide + LOWC, ext), BF), full, edge, edge, tile],
        (1,),
        [pltpu.VMEM((wide, window), BF), pltpu.VMEM((3 * wide, 3 * (wide + LOWC)), BF), state(3, wide)],
        fine, work,
    )
    stats, *slice_blocks = lax.optimization_barrier((stats, *slice_blocks))
    told_first = swap_all(stats)
    first_prev, first_next = to_next(first_bottom), to_previous(first_top)
    first_act, second_pre, second_top, second_bottom, stats = decoder_call(
        lambda *refs: second_kernel(lanes, *refs),
        [first_prev, first_pre, first_next, told_first, counts_f, first_gain, valid_wide, fine_masks, w2, scalars],
        (), (9,),
        [jax.ShapeDtypeStruct((wide, ext), BF), full, edge, edge, tile],
        (1,),
        [pltpu.VMEM((3 * wide, 3 * wide), BF), state(3, wide)],
        fine, work,
    )
    told_second = swap_all(stats)
    second_prev, second_next = to_next(second_bottom), to_previous(second_top)

    classes = w_cls.shape[0]
    cot = jnp.pad(cotangent, ((0, -classes % 32), (0, 0)))
    cot_prev, cot_next = to_next(cot[:, -WF:]), to_previous(cot[:, :WF])
    w_cls_wide = jnp.pad(w_cls, ((0, -classes % 32), (0, 0)))
    bias = jnp.pad(b_cls.astype(F32), (0, -classes % 32))[:, None]
    logits, class_part, bias_part, sums = decoder_call(
        class_kernel,
        [
            second_pre, cot, valid_fine, told_second, counts_f, second_gain, w_cls_wide, w_cls_wide.T, bias, scalars,
        ],
        (0, 1, 2), (9,),
        [
            jax.ShapeDtypeStruct((classes, fine), F32),
            jax.ShapeDtypeStruct((w_cls_wide.shape[0], wide), F32),
            jax.ShapeDtypeStruct((w_cls_wide.shape[0], 128), F32),
            tile,
        ],
        (0,),
        [state(2, wide), pltpu.VMEM((wide, 128), F32)],
        fine, work // 8,
    )
    told_sums = swap_all(sums)
    class_part = jnp.concatenate([class_part[:classes].reshape(-1), jnp.sum(bias_part[:classes], axis=1)])
    class_rows = -(-class_part.shape[0] // (128 * everyone))
    class_part = jnp.pad(class_part, (0, class_rows * 128 * everyone - class_part.shape[0])).reshape(everyone, class_rows, 128)
    class_part = jnp.pad(class_part, ((0, 0), (0, 8 - class_rows), (0, 0)))
    second_dz, first_dy, dy_top, dy_bottom, sums = decoder_call(
        lambda *refs: second_back_kernel(lanes, *refs),
        [
            second_prev, second_pre, second_next, told_second, counts_f, second_gain, told_sums, cot_prev, cot, cot_next,
            w_cls_wide.T, valid_wide, fine_masks, w2, first_pre, told_first, first_gain, class_part, scalars,
        ],
        (14,), (18,),
        [jax.ShapeDtypeStruct((wide, ext), BF), full, edge, edge, jax.ShapeDtypeStruct((everyone, 16, 128), F32)],
        (1,),
        [pltpu.VMEM((3 * wide, 3 * wide), BF), state(2, wide), pltpu.VMEM((wide, 128), F32)],
        fine, work,
    )
    second_sums = jnp.sum(told_sums, axis=0)
    told_first_sums = swap_all(sums)
    first_sums = jnp.sum(told_first_sums, axis=0)
    class_share = first_sums[8 : 8 + class_rows]
    first_sums = first_sums[:8]
    dy_prev, dy_next = to_next(dy_bottom), to_previous(dy_top)
    g_dec2 = decoder_weight_grad(second_dz, first_act, fine_masks, outs)
    told_first_sums, g_dec2, canvas_centered = lax.optimization_barrier((told_first_sums, g_dec2, canvas_centered))
    part_dec2 = lax.psum_scatter(g_dec2, "ch", scatter_dimension=0)
    first_dz, grad_window, dy_low, low_part_sums = decoder_call(
        lambda *refs: first_back_kernel(lanes, *refs),
        [
            first_prev, first_pre, first_next, dy_prev, first_dy, dy_next, told_first, counts_f, first_gain, told_first_sums,
            valid_wide, fine_masks, w1, enlarge, low_pre, told_proj, low_gains, scalars,
        ],
        (14,), (17,),
        [
            jax.ShapeDtypeStruct((wide, ext), BF),
            jax.ShapeDtypeStruct((wide, window), F32),
            jax.ShapeDtypeStruct((LOWC, fine), F32),
            jax.ShapeDtypeStruct((2, 256), F32),
        ],
        (2,),
        [pltpu.VMEM((3 * (wide + LOWC), 3 * wide), BF), state(2, LOWC), pltpu.VMEM((LOWC, 128), F32)],
        fine, work,
    )
    g_dec1 = decoder_weight_grad(first_dz, decoder_in, fine_masks, outs)

    def norm_back(dy, normed, scale, gain, totals, valid, total):
        parts = (totals[0][:, None] + normed * totals[1][:, None]) * (valid / total)
        return (scale * gain)[:, None] * (dy - parts)

    grad_coarse = grad_window[:, margin : margin + share]
    grad_coarse = grad_coarse.at[:, :margin].add(to_next(grad_window[:, margin + share :]))
    grad_coarse = grad_coarse.at[:, share - margin :].add(to_previous(grad_window[:, :margin]))
    proj_told = told_proj.reshape(everyone, 8 * 128)
    proj_mean, proj_scale = merge_moments(proj_told[:, :wide], proj_told[:, 256 : 256 + wide], counts_c[:, 0], count)
    proj_normed = (proj_pre - proj_mean[:, None]) * proj_scale[:, None]
    dy = grad_coarse * silu_slope(proj_gain[0][:, None] * proj_normed + proj_gain[1][:, None]) * valid_mine
    both = vector_tile(jnp.sum(dy, axis=1), jnp.sum(dy * proj_normed, axis=1), low_part_sums[0], low_part_sums[1])
    both = jnp.concatenate([both, jnp.pad(class_share, ((0, 8 - class_rows), (0, 0)))])
    told_both, g_dec1, part_dec2 = lax.optimization_barrier((tell_all(both), g_dec1, part_dec2))
    both = jnp.sum(told_both[:, :8], axis=0).reshape(4, 256)
    class_sums = told_both[:, 8 : 8 + class_rows].reshape(-1)
    bias_sums = class_sums[classes * wide : classes * wide + classes]
    class_sums = class_sums[: classes * wide].reshape(classes, wide)
    proj_sums, low_sums = both[:2], both[2:, :LOWC]
    proj_dz = norm_back(dy, proj_normed, proj_scale, proj_gain[0], proj_sums, valid_mine, count).astype(BF)

    part_dec1 = lax.psum_scatter(g_dec1, "ch", scatter_dimension=0)

    low_mean, low_scale = merge_moments(proj_told[:, 512 : 512 + LOWC], proj_told[:, 768 : 768 + LOWC], counts_f[:, 0], fine_count)
    low_normed = (low_pre - low_mean[:, None]) * low_scale[:, None]
    low_dz = norm_back(dy_low, low_normed, low_scale, low_gain_all, low_sums, valid_fine, fine_count).astype(BF)
    low_dz_all = lax.all_gather(low_dz, "ch", axis=1, tiled=True)

    top, low, top_table, low_table = gather_all(proj_dz[: wide // 2], proj_dz[wide // 2 :])
    wp_own = lax.dynamic_index_in_dim(wp_acts, me, 0, False)
    wp_pool_own = lax.dynamic_slice_in_dim(wp_pool, me * outs, outs, axis=1)
    own_told = lax.dynamic_index_in_dim(told_branch.reshape(groups, devices, 8 * 128), me, 1, False)
    own_mean, own_scale = merge_moments(own_told[:, : 4 * outs], own_told[:, 256 : 256 + 4 * outs], strip_counts[:, 0], count)
    cols = jnp.stack([gain_mid[:4].reshape(-1), shift_mid[:4].reshape(-1), own_scale, own_mean], axis=1)
    padded_dz, branch_sums, g_proj_acts, image_dz = canvas_grad(
        top,
        low,
        (top_table, low_table),
        canvas_centered,
        canvas_rows,
        member_canvas,
        wp_own.T,
        cols,
        own_told[:, : 4 * outs].T,
        1.0 / count[None],
    )
    branch_sums = branch_sums[:, :2].T
    image_dz = image_dz[:, :images]

    g_lowlevel = lax.dot_general(w_low, low_dz_all, (((0,), (0,)), ((), ())), preferred_element_type=F32) * valid_fine_strip.astype(F32)
    g_low = dot_nt(low_dz_all, low_in).astype(BF)
    low_columns = g_low.shape[1]
    g_low = jnp.pad(g_low, ((0, -LOWC % outs), (0, wide - low_columns))).reshape(-1, outs, wide)
    padded_dz, g_low, part_dec1, part_dec2 = lax.optimization_barrier((padded_dz, g_low, part_dec1, part_dec2))
    g_dec1, g_rest = lax.psum((part_dec1, jnp.concatenate([part_dec2, g_low])), "row")

    into, g_w_one = None, None
    if groups == 8 and 2 * slice_depth == 128:
        for branches, plain in CHUNKS:
            part = pyramid_weight_grad(padded_dz, slice_blocks, x_places, canvas_rows, branches, plain)
            part, padded_dz = lax.optimization_barrier((part, padded_dz))
            found, (g_dec1, g_rest) = gather_line(part, (g_dec1, g_rest))
            got = assemble(branches, plain, found, devices, groups, strip, perm, into, outs, devices * depth)
            into = got[0]
            if plain:
                g_w_one = got[1]
    else:
        part = pyramid_weight_grad(padded_dz, slice_blocks, x_places, canvas_rows, (0, 1, 2), True)
        found = columns(lax.all_gather(part, "row", axis=0), (28 * outs,))
        into, g_w_one = found[: 27 * outs], found[27 * outs :]
    g_w_atrous = into.reshape(3, 9, outs, devices * depth).transpose(0, 2, 1, 3)

    g_proj_pool = jnp.dot(image_dz, pool_act.astype(F32).T, precision=HIGHEST)
    g_proj_part = jnp.concatenate([g_proj_acts, g_proj_pool], axis=1).astype(BF)
    g_proj = swap_ch(g_proj_part.reshape(devices, outs, 5 * outs))
    g_proj = jnp.take(g_proj, order, axis=0)
    g_w_proj = g_proj.reshape(devices, outs, 5, outs).transpose(1, 2, 0, 3).reshape(outs, -1).astype(F32)

    grad_pool_act = lax.dot_general(wp_pool_own.astype(F32), image_dz, (((0,), (0,)), ((), ())), precision=HIGHEST)
    dy_pool = grad_pool_act * silu_slope(pool_shifted)
    pool_gain_sum = jnp.sum(dy_pool * pool_normed, axis=1)
    pool_shift_sum = jnp.sum(dy_pool, axis=1)
    pool_dz = (
        (pool_scale * gain_mid[4])[:, None]
        * (dy_pool - (pool_shift_sum[:, None] + pool_normed * pool_gain_sum[:, None]) / images)
    ).astype(BF)
    g_w_pool = dot_nt(pool_dz, pooled)
    spread = jnp.dot(pool_dz.astype(F32) / area[None], member_strip[:images].astype(F32), precision=HIGHEST).astype(BF)

    strip_pad = lax.dynamic_slice_in_dim(padded_dz, strip * pixels, pixels + 2 * PAD, axis=1)
    parts = input_grad(strip_pad, spread, strip_rows, w_taps, w_one, w_pool, perm)
    g_feats = reduce_blocks([parts[i] for i in range(devices)]) * valid_strip

    g_dec1, g_rest = g_dec1.astype(F32), g_rest.astype(F32)
    g_dec2, g_low = g_rest[:9], g_rest[9:].reshape(-1, wide)[:LOWC, :low_columns]
    g_w_dec1 = jnp.concatenate([g_dec1[:, :, wide:], g_dec1[:, :, :wide]], axis=2).transpose(1, 0, 2)
    g_w_dec2 = g_dec2.transpose(1, 0, 2)

    def my(v, n):
        return lax.dynamic_slice_in_dim(v, me * n, n, axis=-1)

    second_sums, first_sums = second_sums.reshape(4, 256), first_sums.reshape(4, 256)
    g_mid_gain = jnp.concatenate([branch_sums[1].reshape(4, outs), pool_gain_sum[None], my(proj_sums[1], outs)[None]])
    g_mid_shift = jnp.concatenate([branch_sums[0].reshape(4, outs), pool_shift_sum[None], my(proj_sums[0], outs)[None]])
    return (
        logits,
        g_feats,
        g_lowlevel,
        g_w_one,
        g_w_atrous,
        g_w_pool,
        g_w_proj,
        g_low,
        g_w_dec1,
        g_w_dec2,
        class_sums,
        bias_sums,
        g_mid_gain,
        g_mid_shift,
        my(low_sums[1], low_share),
        my(low_sums[0], low_share),
        jnp.stack([my(first_sums[1], outs), my(second_sums[1], outs)]),
        jnp.stack([my(first_sums[0], outs), my(second_sums[0], outs)]),
    )


def solution(mesh):
    placed = (
        P("ch", "row"),
        P("ch", "row"),
        P(),
        P(),
        P("ch", None),
        P(None, "ch", None, None),
        P("ch", None),
        P("ch", None),
        P(None, "ch"),
        P("ch", None, None),
        P("ch", None, None),
        P(),
        P(),
        P(None, "ch"),
        P(None, "ch"),
        P("ch"),
        P("ch"),
        P(None, "ch"),
        P(None, "ch"),
        P(None, ("row", "ch")),
    )
    return jax.shard_map(
        local,
        mesh=mesh,
        in_specs=placed,
        out_specs=(
            P(None, ("row", "ch")),
            P("ch", "row"),
            P("ch", "row"),
            P("ch", None),
            P(None, "ch", None, None),
            P("ch", None),
            P("ch", None),
            P(None, "ch"),
            P("ch", None, None),
            P("ch", None, None),
            P(),
            P(),
            P(None, "ch"),
            P(None, "ch"),
            P("ch"),
            P("ch"),
            P(None, "ch"),
            P(None, "ch"),
        ),
        check_vma=False,
    )
```

```python
import math

import jax
import jax.numpy as jnp
from jax import lax
from jax.experimental import pallas as pl
from jax.experimental.pallas import tpu as pltpu
from jax.sharding import PartitionSpec as P

LOWC = 48
WS = 32
WF = 4 * WS
REACH = 18
PAD = 640
EPSILON = 1e-05
HIGHEST = lax.Precision.HIGHEST
BF = jnp.bfloat16
F32 = jnp.float32
BOTH = ("row", "ch")
BRIEF = pl.CostEstimate(flops=1, bytes_accessed=1, transcendentals=0)
VMEM_LIMIT = 56 * 1024 * 1024


def params():
    return pltpu.CompilerParams(vmem_limit_bytes=VMEM_LIMIT)


def dot(a, b):
    return jnp.dot(a, b, preferred_element_type=F32)


def dot_nt(a, b):
    return lax.dot_general(a, b, (((1,), (1,)), ((), ())), preferred_element_type=F32)


def tiles(extent, size):
    return [(start, min(size, extent - start)) for start in range(0, extent, size)]


class Images:
    def __init__(self, heights_ref, widths_ref):
        self.ends, self.widths, total = [], [], 0
        for i in range(heights_ref.shape[0]):
            total = total + heights_ref[i]
            self.ends.append(total)
            self.widths.append(widths_ref[i])
        self.total = total

    def image(self, rows, factor=1):
        return sum((rows >= end * factor).astype(jnp.int32) for end in self.ends)

    def same(self, rows, offset, factor=1):
        others = rows + offset
        inside = (rows >= 0) & (rows < self.total * factor) & (others >= 0) & (others < self.total * factor)
        return jnp.where(inside & (self.image(rows, factor) == self.image(others, factor)), 1.0, 0.0)

    def limit(self, rows, factor=1):
        image = self.image(rows, factor)
        value = jnp.zeros(rows.shape, jnp.int32)
        for i, width in enumerate(self.widths):
            value = jnp.where(image == i, width * factor, value)
        return jnp.where(rows >= 0, value, 0)


def iota(shape, axis):
    return lax.broadcasted_iota(jnp.int32, shape, axis)


def split(index, size):
    return jnp.right_shift(index, size.bit_length() - 1), jnp.bitwise_and(index, size - 1)


def tap_rows(images, rows, col):
    masks = [images.same(rows, -a * rate) for rate in (6, 12, 18) for a in (-1, 1)]
    return masks + [jnp.where(col < images.limit(rows), 1.0, 0.0)]


def strip_geometry_kernel(heights, widths, places, rows_ref, member_ref, fine_ref):
    images = Images(heights, widths)
    pixels = rows_ref.shape[1]
    row, col = split(places[0] * pixels + iota((1, pixels), 1), WS)
    values = tap_rows(images, row, col)
    for i, value in enumerate(values):
        rows_ref[i : i + 1] = value
    rows_ref[7:8] = jnp.zeros((1, pixels), F32)
    image = images.image(row)
    number = iota(member_ref.shape, 0)
    member_ref[...] = (jnp.where(number == image, 1.0, 0.0) * values[6]).astype(BF)
    row, col = split(places[0] * 16 * pixels + iota(fine_ref.shape, 1), WF)
    fine_ref[...] = jnp.where(col < images.limit(row, 4), 1.0, 0.0).astype(BF)


def geometry_kernel(
    margin, heights, widths, places,
    canvas_ref, member_ref, strips_ref, shares_ref, fines_ref, mine_ref, window_ref, ext_ref, masks_ref, enlarge_ref,
):
    images = Images(heights, widths)
    groups, _, pixels = canvas_ref.shape
    everyone, share = shares_ref.shape[0], mine_ref.shape[1]
    place = places[1]
    shape = (groups, pixels)
    row, col = split(iota(shape, 0) * pixels + iota(shape, 1), WS)
    values = tap_rows(images, row, col)
    for i, value in enumerate(values):
        canvas_ref[:, i] = value
    canvas_ref[:, 7] = jnp.zeros(shape, F32)
    image = images.image(row)
    for i in range(member_ref.shape[1]):
        member_ref[:, i] = jnp.where(image == i, values[6], 0.0)
    strips_ref[...] = jnp.sum(values[6], axis=1, keepdims=True)

    def counted(pixels, cols, factor):
        row, col = split(iota((everyone, pixels), 0) * pixels + iota((everyone, pixels), 1), cols)
        return jnp.sum(jnp.where(col < images.limit(row, factor), 1.0, 0.0), axis=1, keepdims=True)

    shares_ref[...] = counted(share, WS, 1)
    rows = masks_ref.shape[1] // WF
    number = iota((everyone, rows), 0) * rows + iota((everyone, rows), 1)
    fines_ref[...] = jnp.sum(images.limit(number, 4).astype(F32), axis=1, keepdims=True)

    row, col = split(place * share + iota((1, share), 1), WS)
    valid = jnp.where(col < images.limit(row), 1.0, 0.0)
    image = images.image(row)
    last = mine_ref.shape[0] - 8
    mine_ref[:last] = jnp.where(iota((last, share), 0) == image, 1.0, 0.0) * valid
    mine_ref[last:] = jnp.broadcast_to(valid, (8, share))
    row, col = split(place * share - margin + iota(window_ref.shape, 1), WS)
    window_ref[...] = jnp.where(col < images.limit(row), 1.0, 0.0)

    first = place * rows
    row, col = split(iota((1, masks_ref.shape[1]), 1), WF)
    for i, offset in enumerate((-1, 1)):
        masks_ref[i : i + 1] = images.same(first + row, offset, 4)
    window, ext = enlarge_ref.shape
    at_row, at_col = split(place * share - margin + iota((window, 1), 0), WS)
    for start, size in tiles(ext, 512):
        row, col = split(start + iota((1, size), 1), WF)
        row = first - 1 + row
        valid = jnp.where(col < images.limit(row, 4), 1.0, 0.0)
        ext_ref[:, start : start + size] = valid

        def weights(phase):
            middle = jnp.where((phase == 0) | (phase == 3), 0.625, 0.875)
            before = jnp.where(phase == 0, 0.375, jnp.where(phase == 1, 0.125, 0.0))
            after = jnp.where(phase == 3, 0.375, jnp.where(phase == 2, 0.125, 0.0))
            return middle, before, after

        def part(there, here, middle, before, after):
            apart = there - here
            return jnp.where(apart == 0, middle, jnp.where(apart == -1, before, jnp.where(apart == 1, after, 0.0)))

        q, phase = split(row, 4)
        middle, before, after = weights(phase)
        by_row = part(at_row, q, middle * valid, before * images.same(q, -1) * valid, after * images.same(q, 1) * valid)
        q, phase = split(col, 4)
        enlarge_ref[:, start : start + size] = (by_row * part(at_col, q, *weights(phase))).astype(BF)


def geometry_call(kernel, heights, widths, places, outputs):
    smem = pl.BlockSpec(memory_space=pltpu.SMEM)
    return pl.pallas_call(
        kernel,
        in_specs=[smem] * 3,
        out_specs=[pl.BlockSpec(memory_space=pltpu.VMEM)] * len(outputs),
        out_shape=outputs,
        compiler_params=params(),
        cost_estimate=pl.CostEstimate(flops=20000000, bytes_accessed=6000000, transcendentals=0),
    )(heights, widths, places)


def gather_blocks(x, meanwhile=()):
    count, me = lax.axis_size("ch"), lax.axis_index("ch")
    if count == 4:
        cross = lambda v, m: lax.ppermute(v, "ch", [(i, i ^ m) for i in range(count)])
        far = cross(x, 2)
        near = cross(x, 1)
        if meanwhile:
            far, *meanwhile = lax.optimization_barrier((far, *meanwhile))
        return [x, near, far, cross(far, 1)], [me, me ^ 1, me ^ 2, me ^ 3], meanwhile
    every = lax.all_gather(x, "ch", axis=0)
    return [every[i] for i in range(count)], [jnp.int32(i) for i in range(count)], meanwhile


def swap_ch(x):
    count, me = lax.axis_size("ch"), lax.axis_index("ch")
    if count != 4:
        return lax.all_to_all(x, "ch", 0, 0)
    pick = lambda i: lax.dynamic_index_in_dim(x, i, 0, False)
    blocks = [pick(me)]
    for m in (1, 2, 3):
        blocks.append(lax.ppermute(pick(me ^ m), "ch", [(i, i ^ m) for i in range(count)]))
    return jnp.stack(blocks)


def reduce_blocks(blocks):
    count = lax.axis_size("ch")
    if count == 4:
        cross = lambda v, m: lax.ppermute(v, "ch", [(i, i ^ m) for i in range(count)])
        arrived = cross(jnp.stack([blocks[3], blocks[1]]), 1).astype(F32)
        onward = (blocks[2].astype(F32) + arrived[0]).astype(BF)
        return blocks[0].astype(F32) + arrived[1] + cross(onward, 2).astype(F32)
    return lax.psum_scatter(jnp.stack(blocks), "ch", scatter_dimension=0).astype(F32)


def gather_line(x):
    def along(v, places, step):
        return lax.ppermute(v, "row", [(2 * i + e, 2 * (i + step) + e) for i in places for e in range(2)])

    def beside(v, places):
        return lax.ppermute(v, "row", [(2 * i + e, 2 * i + 1 - e) for i in places for e in range(2)])

    def together(*keys):
        got.update(zip(keys, lax.optimization_barrier(tuple(got[key] for key in keys))))

    got = {(0, 0, 0): x}
    got[-1, 0, 0], got[1, 0, 0] = along(x, (0, 1, 2), 1), along(x, (1, 2, 3), -1)
    got[0, 1, 0] = beside(x, (0, 1, 2, 3))
    together((-1, 0, 0), (1, 0, 0), (0, 1, 0))
    got[-2, 0, 0], got[2, 0, 0] = along(got[-1, 0, 0], (1, 2), 1), along(got[1, 0, 0], (1, 2), -1)
    got[-1, 1, 0], got[1, 1, 0] = beside(got[-1, 0, 0], (1, 2, 3)), beside(got[1, 0, 0], (0,))
    together((-2, 0, 0), (2, 0, 0), (-1, 1, 0), (1, 1, 0), (1, 0, 0))
    got[-3, 0, 0], got[3, 0, 0] = along(got[-2, 0, 0], (2,), 1), along(got[2, 0, 0], (1,), -1)
    got[1, 1, 1] = beside(got[1, 0, 0], (1, 2))
    got[-2, 1, 0], got[2, 1, 0] = beside(got[-2, 0, 0], (3,)), beside(got[2, 0, 0], (0,))
    together((-3, 0, 0), (3, 0, 0), (1, 1, 1), (-2, 1, 0), (2, 1, 0), (-2, 0, 0), (2, 0, 0))
    got[-2, 1, 1], got[2, 1, 1] = beside(got[-2, 0, 0], (2,)), beside(got[2, 0, 0], (1,))
    got[-3, 1, 0], got[3, 1, 0] = beside(got[-3, 0, 0], (3,)), beside(got[3, 0, 0], (0,))
    return got


def line_part(place, steps, side):
    first = {(1, 1): (0,), (-2, 1): (3,), (2, 1): (0,)}.get((steps, side))
    return (steps, side, 0 if first is None or place in first else 1)


def swap_all(values):
    return lax.all_to_all(values, BOTH, 0, 0)


def tell_all(values):
    count = lax.axis_size("row") * lax.axis_size("ch")
    return swap_all(jnp.broadcast_to(values[None], (count,) + values.shape))


def tell_row(values):
    count = lax.axis_size("row")
    return lax.all_to_all(jnp.broadcast_to(values[None], (count,) + values.shape), "row", 0, 0)


def tell_group(values):
    count = lax.axis_size("ch")
    return lax.all_to_all(jnp.broadcast_to(values[None], (count,) + values.shape), "ch", 0, 0)


def vector_tile(*vectors):
    rows = [jnp.pad(v, (0, 256 - v.shape[0])).reshape(2, 128) for v in vectors]
    return jnp.pad(jnp.concatenate(rows), ((0, 8 - 2 * len(rows)), (0, 0)))


def to_next(x):
    count = lax.axis_size("row") * lax.axis_size("ch")
    return lax.ppermute(x, BOTH, [(i, i + 1) for i in range(count - 1)])


def to_previous(x):
    count = lax.axis_size("row") * lax.axis_size("ch")
    return lax.ppermute(x, BOTH, [(i + 1, i) for i in range(count - 1)])


def local_moments(x, valid):
    count = jnp.sum(valid)
    mean = jnp.sum(x * valid[None], axis=1) / jnp.maximum(count, 1.0)
    centered = (x - mean[:, None]) * valid[None]
    return mean, jnp.sum(centered * centered, axis=1)


def merge_moments(means, spreads, counts, total):
    mean = jnp.sum(means * counts[:, None], axis=0) / total
    away = means - mean[None]
    var = (jnp.sum(spreads, axis=0) + jnp.sum(counts[:, None] * away * away, axis=0)) / total
    return mean, lax.rsqrt(var + EPSILON)


def silu_slope(y):
    gate = jax.nn.sigmoid(y)
    return gate * (1.0 + y * (1.0 - gate))


def rows_per_step(rows):
    for step in (6, 4, 3, 2):
        if rows % step == 0:
            return step
    return 1


def pack_vectors(out_ref, first, second, more=None):
    more = jnp.zeros((4, 128), F32) if more is None else more
    tile = jnp.concatenate([first[:, :128], first[:, 128:], second[:, :128], second[:, 128:], more], axis=0)
    out_ref[:, :8] = jnp.broadcast_to(tile[None], (out_ref.shape[0], 8, 128))


def as_rows(columns):
    channels = columns[0].shape[0]
    lane = lax.broadcasted_iota(jnp.int32, (channels, 128), 1)
    block = jnp.zeros((channels, 128), F32)
    for i, column in enumerate(columns):
        block = jnp.where(lane == i, column, block)
    turned = block.T
    if channels < 256:
        turned = jnp.concatenate([turned, jnp.zeros((128, 256 - channels), F32)], axis=1)
    return [turned[i : i + 1] for i in range(len(columns))]


def as_columns(rows, channels):
    block = jnp.concatenate(rows + [jnp.zeros((8 - len(rows), rows[0].shape[1]), F32)], axis=0)
    turned = block.T
    return [turned[:channels, i : i + 1] for i in range(len(rows))]


def told_vectors(told):
    return jnp.concatenate([told[:, 0], told[:, 1]], axis=1), jnp.concatenate([told[:, 2], told[:, 3]], axis=1)


def merged(told, counts, inverse):
    means, spreads = told_vectors(told)
    mean = jnp.sum(means * counts, axis=0, keepdims=True) * inverse
    away = means - mean
    var = jnp.sum(spreads + counts * (away * away), axis=0, keepdims=True) * inverse
    return mean, lax.rsqrt(var + EPSILON)


def norm_columns(told_ref, counts_ref, inverse, gain_rows, channels, first=0):
    mean, scale = merged(told_ref[:, first : first + 4], counts_ref[...], inverse)
    return as_columns([mean, scale, gain_rows[0:1], gain_rows[1:2]], channels)


def sums_columns(told_ref, channels):
    first, second = told_vectors(told_ref[...])
    return as_columns([jnp.sum(first, axis=0, keepdims=True), jnp.sum(second, axis=0, keepdims=True)], channels)


def normed_of(pre, cols):
    return (pre - cols[0]) * cols[1]


def activation(pre, cols, valid):
    y = cols[2] * normed_of(pre, cols) + cols[3]
    return (y * jax.nn.sigmoid(y) * valid).astype(BF)


def fold(x):
    total = x[:, :128]
    for at in range(128, x.shape[1], 128):
        total = total + x[:, at : at + 128]
    return total


def moments_step(v, valid, state_ref, first):
    @pl.when(first)
    def _():
        count = jnp.maximum(jnp.sum(valid), 1.0)
        state_ref[0] = jnp.broadcast_to(jnp.sum(v * valid, axis=1, keepdims=True) / count, state_ref.shape[1:])
        state_ref[1] = jnp.zeros(state_ref.shape[1:], F32)
        state_ref[2] = jnp.zeros(state_ref.shape[1:], F32)

    away = (v - state_ref[0, :, 0:1]) * valid
    state_ref[1] += fold(away)
    state_ref[2] += fold(away * away)


def moments_end(state_ref, count, out_ref):
    total = jnp.sum(state_ref[1], axis=1, keepdims=True)
    squares = jnp.sum(state_ref[2], axis=1, keepdims=True)
    mean = state_ref[0, :, 0:1] + total / count
    pack_vectors(out_ref, *as_rows([mean, squares - total * total / count]))


def sums_step(dy, normed, state_ref, first):
    @pl.when(first)
    def _():
        state_ref[...] = jnp.zeros_like(state_ref)

    state_ref[0] += fold(dy)
    state_ref[1] += fold(dy * normed)


def sums_end(state_ref, out_ref):
    pack_vectors(out_ref, *as_rows([jnp.sum(state_ref[i], axis=1, keepdims=True) for i in range(2)]))


def ext_parts(rows_ext, piece):
    own = rows_ext * WF - 2 * WF
    yield 0, slice(0, WF), slice(0, WF)
    for start, size in tiles(own, piece):
        yield 1, slice(start, start + size), slice(WF + start, WF + start + size)
    yield 2, slice(0, WF), slice(WF + own, 2 * WF + own)


def stacked(a_ref, start, lanes, mask_ref, flip, rows):
    first, last = (1, 0) if flip else (0, 1)
    before = a_ref[rows, pl.ds(start, lanes)]
    middle = a_ref[rows, pl.ds(start + WF, lanes)]
    after = a_ref[rows, pl.ds(start + 2 * WF, lanes)]
    before = before * mask_ref[0:1, pl.ds(start, lanes)].astype(BF)
    after = after * mask_ref[1:2, pl.ds(start, lanes)].astype(BF)
    return [after, middle, before] if flip else [before, middle, after]


def columns_joined(acc, outs, flip):
    lanes = acc.shape[1]
    col = lax.broadcasted_iota(jnp.int32, (1, lanes), 1) % WF
    left, right = (acc[2 * outs :], acc[:outs]) if flip else (acc[:outs], acc[2 * outs :])
    left = jnp.where(col > 0, pltpu.roll(left, 1, 1), 0.0)
    right = jnp.where(col < WF - 1, pltpu.roll(right, lanes - 1, 1), 0.0)
    return acc[outs : 2 * outs] + left + right


def forward_weights(w_ref, up, out_ref):
    devices, _, outs, cin = w_ref.shape
    wide, extra = devices * outs, cin - up
    for c in range(devices):
        for b in range(3):
            rows = slice(b * wide + c * outs, b * wide + (c + 1) * outs)
            for a in range(3):
                piece = w_ref[c, 3 * a + b]
                out_ref[rows, a * up : (a + 1) * up] = piece[:, :up]
                if extra:
                    at = 3 * up + a * extra
                    out_ref[rows, at : at + extra] = piece[:, up:]


def backward_weights(w_ref, up, out_ref):
    devices, _, outs, cin = w_ref.shape
    wide, extra = devices * outs, cin - up
    for a in range(3):
        for b in range(3):
            whole = jnp.concatenate([w_ref[c, 3 * a + b] for c in range(devices)], axis=0).astype(F32)
            columns = slice(a * wide, (a + 1) * wide)
            out_ref[b * up : (b + 1) * up, columns] = whole[:, :up].T.astype(BF)
            if extra:
                tail = jnp.concatenate([whole[:, up:], jnp.zeros((wide, 128 - extra), F32)], axis=1).T
                at = 3 * up + b * extra
                out_ref[at : at + extra, columns] = tail[:extra].astype(BF)


def first_kernel(
    lanes,
    proj_prev, proj_own, proj_next, told_proj, counts_c, proj_gain, window_valid,
    enlarge, low_prev, low_own, low_next, told_low, counts_f, low_gain, valid_ext, mask, w_all, scalars,
    a_ref, out_ref, top_ref, bottom_ref, stats_ref, coarse_ref, w_ref, state_ref,
):
    step, last = pl.program_id(0), pl.num_programs(0) - 1
    up = proj_own.shape[0]
    margin, share = proj_prev.shape[1], proj_own.shape[1]

    @pl.when(step == 0)
    def _():
        forward_weights(w_all, up, w_ref)
        cols = norm_columns(told_proj, counts_c, scalars[0], proj_gain, up)
        for ref, start in ((proj_prev, 0), (proj_own, margin), (proj_next, margin + share)):
            part = slice(start, start + ref.shape[1])
            coarse_ref[:, part] = activation(ref[...], cols, window_valid[:, part])
        ext = a_ref.shape[1]
        for start, size in tiles(ext, 512):
            a_ref[:up, start : start + size] = dot(coarse_ref[...], enlarge[:, start : start + size]).astype(BF)
        cols = norm_columns(told_low, counts_f, scalars[1], low_gain, LOWC, 4)
        for which, part, there in ext_parts(ext // WF, 1536):
            a_ref[up:, there] = activation((low_prev, low_own, low_next)[which][:, part], cols, valid_ext[:, there])

    start = pl.multiple_of(step * lanes, 128)
    taps = stacked(a_ref, start, lanes, mask, False, slice(0, up)) + stacked(a_ref, start, lanes, mask, False, slice(up, up + LOWC))
    acc = dot(w_ref[...], jnp.concatenate(taps, axis=0))
    conv_end(acc, False, step, last, start, lanes, valid_ext, out_ref, top_ref, bottom_ref, stats_ref, state_ref)


def conv_end(acc, flip, step, last, start, lanes, valid_ext, out_ref, top_ref, bottom_ref, stats_ref, state_ref):
    outs = out_ref.shape[0]
    v = columns_joined(acc, outs, flip)
    out_ref[...] = v
    moments_step(v, valid_ext[:, pl.ds(start + WF, lanes)], state_ref, step == 0)

    @pl.when(step == 0)
    def _():
        top_ref[...] = v[:, :WF]

    @pl.when(step == last)
    def _():
        bottom_ref[...] = v[:, lanes - WF :]
        count = jnp.maximum(jnp.sum(valid_ext[:, WF : valid_ext.shape[1] - WF]), 1.0)
        moments_end(state_ref, count, stats_ref)


def second_kernel(
    lanes, prev, own, after, told, counts, gain, valid_ext, mask, w_all, scalars,
    a_ref, out_ref, top_ref, bottom_ref, stats_ref, w_ref, state_ref,
):
    step, last = pl.program_id(0), pl.num_programs(0) - 1

    @pl.when(step == 0)
    def _():
        forward_weights(w_all, w_all.shape[3], w_ref)
        cols = norm_columns(told, counts, scalars[1], gain, a_ref.shape[0])
        for which, part, there in ext_parts(a_ref.shape[1] // WF, 768):
            a_ref[:, there] = activation((prev, own, after)[which][:, part], cols, valid_ext[:, there])

    start = pl.multiple_of(step * lanes, 128)
    taps = stacked(a_ref, start, lanes, mask, False, slice(None))
    acc = dot(w_ref[...], jnp.concatenate(taps, axis=0))
    conv_end(acc, False, step, last, start, lanes, valid_ext, out_ref, top_ref, bottom_ref, stats_ref, state_ref)


def class_kernel(
    pre, cotangent, valid, told, counts, gain, w_cls, w_turned, bias, scalars,
    logits_ref, weights_ref, bias_ref, sums_ref, state_ref, cols_ref,
):
    step, last = pl.program_id(0), pl.num_programs(0) - 1
    classes = logits_ref.shape[0]

    @pl.when(step == 0)
    def _():
        for i, col in enumerate(norm_columns(told, counts, scalars[1], gain, pre.shape[0])):
            cols_ref[:, i : i + 1] = col
        weights_ref[...] = jnp.zeros_like(weights_ref)
        bias_ref[...] = jnp.zeros_like(bias_ref)

    cols = [cols_ref[:, i : i + 1] for i in range(4)]
    normed = normed_of(pre[...], cols)
    y = cols[2] * normed + cols[3]
    gate = jax.nn.sigmoid(y)
    act = (y * gate * valid[...]).astype(BF)
    logits_ref[...] = (dot(w_cls[...], act) + bias[...])[:classes]
    weights_ref[...] += dot_nt(cotangent[...], act)
    bias_ref[...] += fold(cotangent[...].astype(F32))
    d = dot(w_turned[...], cotangent[...]).astype(BF).astype(F32)
    dy = d * (gate * (1.0 + y * (1.0 - gate)) * valid[...])
    sums_step(dy, normed, state_ref, step == 0)

    @pl.when(step == last)
    def _():
        sums_end(state_ref, sums_ref)


def back_dz(dy, normed, cols, sums, valid, inverse):
    return ((cols[1] * cols[2]) * (dy - (sums[0] + normed * sums[1]) * (valid * inverse))).astype(BF)


def second_back_kernel(
    lanes,
    prev, own, after, told, counts, gain, sums, cot_prev, cot_own, cot_after, w_turned, valid_ext, mask, w_all,
    first_pre, told_first, gain_first, riders, scalars,
    dz_ref, dy_ref, top_ref, bottom_ref, sums_ref, w_ref, state_ref, cols_ref,
):
    step, last = pl.program_id(0), pl.num_programs(0) - 1

    @pl.when(step == 0)
    def _():
        backward_weights(w_all, w_all.shape[3], w_ref)
        channels = dz_ref.shape[0]
        cols = norm_columns(told, counts, scalars[1], gain, channels)
        totals = sums_columns(sums, channels)
        for which, part, there in ext_parts(dz_ref.shape[1] // WF, 768):
            pre, cot = ((prev, cot_prev), (own, cot_own), (after, cot_after))[which]
            normed = normed_of(pre[:, part], cols)
            valid = valid_ext[:, there]
            d = dot(w_turned[...], cot[:, part]).astype(BF).astype(F32)
            dy = d * silu_slope(cols[2] * normed + cols[3]) * valid
            dz_ref[:, there] = back_dz(dy, normed, cols, totals, valid, scalars[1])
        for i, col in enumerate(norm_columns(told_first, counts, scalars[1], gain_first, channels)):
            cols_ref[:, i : i + 1] = col

    start = pl.multiple_of(step * lanes, 128)
    taps = stacked(dz_ref, start, lanes, mask, True, slice(None))
    acc = dot(w_ref[...], jnp.concatenate(taps, axis=0))
    grad = columns_joined(acc, dy_ref.shape[0], True)
    cols = [cols_ref[:, i : i + 1] for i in range(4)]
    normed = normed_of(first_pre[...], cols)
    dy = grad * silu_slope(cols[2] * normed + cols[3]) * valid_ext[:, pl.ds(start + WF, lanes)]
    dy_ref[...] = dy
    sums_step(dy, normed, state_ref, step == 0)

    @pl.when(step == 0)
    def _():
        top_ref[...] = dy[:, :WF]

    @pl.when(step == last)
    def _():
        bottom_ref[...] = dy[:, lanes - WF :]
        sums_end(state_ref, sums_ref)
        sums_ref[:, 8:] = riders[...]


def first_back_kernel(
    lanes,
    prev, own, after, dy_prev, dy_own, dy_after, told, counts, gain, sums, valid_ext, mask, w_all,
    enlarge, low_pre, told_low, low_gain, scalars,
    dz_ref, window_ref, low_ref, low_sums_ref, w_ref, state_ref, cols_ref,
):
    step, last = pl.program_id(0), pl.num_programs(0) - 1
    up = window_ref.shape[0]

    @pl.when(step == 0)
    def _():
        backward_weights(w_all, up, w_ref)
        channels = dz_ref.shape[0]
        cols = norm_columns(told, counts, scalars[1], gain, channels)
        totals = sums_columns(sums, channels)
        for which, part, there in ext_parts(dz_ref.shape[1] // WF, 768):
            pre, dy = ((prev, dy_prev), (own, dy_own), (after, dy_after))[which]
            normed = normed_of(pre[:, part], cols)
            dz_ref[:, there] = back_dz(dy[:, part], normed, cols, totals, valid_ext[:, there], scalars[1])
        for i, col in enumerate(norm_columns(told_low, counts, scalars[1], low_gain, LOWC, 4)):
            cols_ref[:, i : i + 1] = col
        window_ref[...] = jnp.zeros_like(window_ref)

    start = pl.multiple_of(step * lanes, 128)
    taps = stacked(dz_ref, start, lanes, mask, True, slice(None))
    acc = dot(w_ref[...], jnp.concatenate(taps, axis=0))
    grad = columns_joined(acc[: 3 * up], up, True)
    high = grad.astype(BF)
    rest = (grad - high.astype(F32)).astype(BF)
    part = enlarge[:, pl.ds(start + WF, lanes)]
    window_ref[...] += dot_nt(high, part) + dot_nt(rest, part)
    cols = [cols_ref[:, i : i + 1] for i in range(4)]
    normed = normed_of(low_pre[...], cols)
    dy = columns_joined(acc[3 * up :], LOWC, True)
    dy = dy * silu_slope(cols[2] * normed + cols[3]) * valid_ext[:, pl.ds(start + WF, lanes)]
    low_ref[...] = dy
    sums_step(dy, normed, state_ref, step == 0)

    @pl.when(step == last)
    def _():
        for i in range(2):
            low_sums_ref[i : i + 1] = as_rows([jnp.sum(state_ref[i], axis=1, keepdims=True)])[0]


def decoder_weight_kernel(lanes, outs, dz_ref, a_ref, mask_ref, *refs):
    step = pl.program_id(0)
    start = pl.multiple_of(step * lanes, 128)
    acc_ref = refs[-1]
    wide = dz_ref.shape[0]
    up, extra = wide, a_ref.shape[0] - wide

    @pl.when(step == 0)
    def _():
        acc_ref[...] = jnp.zeros_like(acc_ref)

    taps = stacked(a_ref, start, lanes, mask_ref, False, slice(0, up))
    if a_ref.shape[0] > up:
        taps = taps + stacked(a_ref, start, lanes, mask_ref, False, slice(up, None))
    dz = dz_ref[:, pl.ds(start + WF, lanes)]
    col = lax.broadcasted_iota(jnp.int32, (1, lanes), 1) % WF
    left = pltpu.roll(dz, lanes - 1, 1) * (col < WF - 1).astype(F32).astype(BF)
    right = pltpu.roll(dz, 1, 1) * (col > 0).astype(F32).astype(BF)
    acc_ref[...] += dot_nt(jnp.concatenate([left, dz, right], axis=0), jnp.concatenate(taps, axis=0))

    @pl.when(step == pl.num_programs(0) - 1)
    def _():
        for c in range(wide // outs):
            for b in range(3):
                rows = slice(b * wide + c * outs, b * wide + (c + 1) * outs)
                for a in range(3):
                    refs[0][c, 3 * a + b, :, :up] = acc_ref[rows, a * up : (a + 1) * up].astype(BF)
                    if extra:
                        at = 3 * up + a * extra
                        refs[0][c, 3 * a + b, :, up:] = acc_ref[rows, at : at + extra].astype(BF)


def decoder_weight_grad(dz, a, masks, outs):
    wide, pixels = dz.shape[0], dz.shape[1] - 2 * WF
    cin = a.shape[0]
    lanes = WF * rows_per_step(pixels // WF)
    devices = wide // outs
    whole = pl.BlockSpec(memory_space=pltpu.VMEM)
    return pl.pallas_call(
        lambda *refs: decoder_weight_kernel(lanes, outs, *refs),
        grid=(pixels // lanes,),
        in_specs=[whole] * 3,
        out_specs=whole,
        out_shape=jax.ShapeDtypeStruct((devices, 9, outs, cin), BF),
        scratch_shapes=[pltpu.VMEM((3 * wide, 3 * cin), F32)],
        compiler_params=params(),
        cost_estimate=BRIEF,
    )(dz, a, masks)


def decoder_call(kernel, operands, blocked, smem, outputs, blocked_out, scratch, pixels, flops):
    lanes = WF * rows_per_step(pixels // WF)
    whole = pl.BlockSpec(memory_space=pltpu.VMEM)
    run = lambda channels: pl.BlockSpec((channels, lanes), lambda i: (0, i))
    in_specs = [
        pl.BlockSpec(memory_space=pltpu.SMEM) if i in smem else run(v.shape[0]) if i in blocked else whole
        for i, v in enumerate(operands)
    ]
    out_specs = [run(v.shape[0]) if i in blocked_out else whole for i, v in enumerate(outputs)]
    return pl.pallas_call(
        kernel,
        grid=(pixels // lanes,),
        in_specs=in_specs,
        out_specs=out_specs,
        out_shape=outputs,
        scratch_shapes=scratch,
        compiler_params=params(),
        cost_estimate=BRIEF,
    )(*operands)


def branch_kernel(centre, from_next, from_prev, valid, out_ref, pieces_ref, stats_ref):
    outs, pixels = centre.shape[1:]
    devices, _, share = pieces_ref.shape
    count = jnp.maximum(jnp.sum(valid[...]), 1.0)
    means, spreads = [], []
    for k in range(4):
        rows = slice(k * outs, (k + 1) * outs)
        v = centre[(k + 3) % 4]
        if k:
            v = v + jnp.concatenate([jnp.zeros((outs, pixels - PAD), F32), from_next[k - 1].astype(F32)], axis=1)
            v = v + jnp.concatenate([from_prev[k - 1].astype(F32), jnp.zeros((outs, pixels - PAD), F32)], axis=1)
        mean = jnp.sum(v * valid[...], axis=1, keepdims=True) / count
        v = (v - mean) * valid[...]
        means.append(mean)
        spreads.append(jnp.sum(v * v, axis=1, keepdims=True))
        out_ref[rows] = v.astype(BF)
        for i in range(devices):
            pieces_ref[i, rows] = v[:, i * share : (i + 1) * share].astype(BF)
    pack_vectors(stats_ref, *as_rows([jnp.concatenate(means, axis=0), jnp.concatenate(spreads, axis=0)]))


def parameter_kernel(
    depth, told_ref, w_pool_ref, w_proj_ref, area_ref, branch_ref, proj_ref, first_ref, second_ref, low_ref, pooled_ref
):
    devices, rows, _ = told_ref.shape
    _, taps, outs, wide = w_pool_ref.shape
    low_share = LOWC // devices
    proj_ref[...] = jnp.zeros_like(proj_ref)
    low_ref[...] = jnp.zeros_like(low_ref)
    branch_ref[...] = jnp.zeros_like(branch_ref)

    def over(row, place):
        pieces = [told_ref[c, row : row + 1, depth + place * outs : depth + (place + 1) * outs] for c in range(devices)]
        return jnp.concatenate(pieces, axis=1)

    for c in range(devices):
        for i in range(2):
            branch_ref[c, i : i + 1, : 4 * outs] = told_ref[c, i : i + 1, depth : depth + 4 * outs]
            at = depth + 128 * i
            low_ref[i : i + 1, c * low_share : (c + 1) * low_share] = told_ref[c, 4:5, at : at + low_share]
    for i in range(2):
        proj_ref[i : i + 1] = over(2, 1 + 2 * i)
        first_ref[i : i + 1] = over(3, 2 * i)
        second_ref[i : i + 1] = over(3, 1 + 2 * i)
    gain, shift = over(2, 0), over(2, 2)
    pre = jnp.zeros((rows, wide), F32)
    means = []
    for c in range(devices):
        means.append((told_ref[c, :, :depth] / area_ref[...]).astype(BF))
    means = jnp.concatenate(means, axis=1)
    for k in range(taps):
        part = means[:, k * wide : (k + 1) * wide]
        pre = pre + jnp.concatenate([dot_nt(part, w_pool_ref[c, k]) for c in range(devices)], axis=1)
    number = iota((rows, 1), 0)
    real = jnp.where(number < pooled_ref.shape[2], 1.0, 0.0)
    images = pooled_ref.shape[2]
    mean = jnp.sum(pre * real, axis=0, keepdims=True) / images
    var = jnp.sum(pre * pre * real, axis=0, keepdims=True) / images - mean * mean
    y = gain * ((pre - mean) * lax.rsqrt(var + EPSILON)) + shift
    act = (y * jax.nn.sigmoid(y)).astype(BF)
    pooled_ref[0] = dot_nt(w_proj_ref[...], act)[:, :images]


def project_kernel(
    swapped, told, counts, gains, w_ref, broad, member, valid, low_stats, scalars, places, out_ref, left_ref, right_ref, stats_ref
):
    devices, four, share = swapped.shape
    groups = told.shape[0]
    margin = left_ref.shape[1]
    mine = places[0]
    number = lax.broadcasted_iota(jnp.int32, (groups, 1), 0)
    total = jnp.zeros(out_ref.shape, F32)
    for i in range(broad.shape[2]):
        total = total + broad[0, :, i : i + 1] * member[i : i + 1]
    for j in range(devices):
        c = places[1 + j]
        group = told[:, c]
        mean, scale = merged(group, counts[...], scalars[0])
        here = jnp.sum(jnp.where(number == mine, told_vectors(group)[0], 0.0), axis=0, keepdims=True)
        cols = as_columns([mean - here, scale, gains[c, 0:1], gains[c, 1:2]], four)
        total = total + dot(w_ref[c], activation(swapped[j].astype(F32), cols, valid[...]))
    out_ref[...] = total
    left_ref[...] = total[:, :margin]
    right_ref[...] = total[:, share - margin :]
    count = jnp.maximum(jnp.sum(valid[...]), 1.0)
    mean = jnp.sum(total * valid[...], axis=1, keepdims=True) / count
    away = (total - mean) * valid[...]
    pack_vectors(stats_ref, *as_rows([mean, jnp.sum(away * away, axis=1, keepdims=True)]), low_stats[...])


def small_call(kernel, operands, smem, outputs, flops):
    whole = pl.BlockSpec(memory_space=pltpu.VMEM)
    return pl.pallas_call(
        kernel,
        in_specs=[pl.BlockSpec(memory_space=pltpu.SMEM) if i in smem else whole for i in range(len(operands))],
        out_specs=[whole] * len(outputs),
        out_shape=outputs,
        compiler_params=params(),
        cost_estimate=pl.CostEstimate(flops=flops, bytes_accessed=4000000, transcendentals=0),
    )(*operands)


def pyramid_kernel(blocks, outs, perm_ref, *refs):
    x_refs = refs[:blocks]
    w_ref, w_one_ref, mask_ref, centre_ref, up_ref, down_ref, acc_ref = refs[blocks:]
    k = pl.program_id(0)
    rate = 6 * (k + 1)
    depth, pixels = x_refs[0].shape

    def product(weights, width):
        for start, size in tiles(pixels, 512):
            total = None
            for j in range(blocks):
                at = pl.multiple_of(perm_ref[j] * depth, depth)
                part = dot(weights(at, depth), x_refs[j][:, start : start + size])
                total = part if total is None else total + part
            acc_ref[:width, start : start + size] = total

    @pl.when(k == 3)
    def _():
        product(lambda at, n: w_one_ref[:, pl.ds(at, n)], outs)
        centre_ref[0] = acc_ref[:outs]

    @pl.when(k < 3)
    def _():
        product(lambda at, n: w_ref[0, :, pl.ds(at, n)], 9 * outs)
        lane = lax.broadcasted_iota(jnp.int32, (1, pixels), 1)
        col, row = lane % WS, lane // WS
        for a in (0, 1, -1):
            tap = 3 * (a + 1) * outs
            left = pltpu.roll(acc_ref[tap : tap + outs], rate, 1)
            right = pltpu.roll(acc_ref[tap + 2 * outs : tap + 3 * outs], pixels - rate, 1)
            part = acc_ref[tap + outs : tap + 2 * outs] + jnp.where(col >= rate, left, 0.0) + jnp.where(col < WS - rate, right, 0.0)
            if a == 0:
                centre_ref[0] = part
                continue
            part = part * mask_ref[pl.ds(2 * k + (a + 1) // 2, 1)]
            if a == 1:
                moved = pltpu.roll(part, pixels - WS * rate, 1)
                inside = row < pixels // WS - rate
                up_ref[0] = jnp.where(inside, 0.0, moved)[:, pixels - PAD :].astype(BF)
            else:
                moved = pltpu.roll(part, WS * rate, 1)
                inside = row >= rate
                down_ref[0] = jnp.where(inside, 0.0, moved)[:, :PAD].astype(BF)
            centre_ref[0] += jnp.where(inside, moved, 0.0)


def pyramid(x_blocks, perm, w_taps, w_one, masks):
    depth, pixels = x_blocks[0].shape
    outs, cin = w_one.shape
    whole = pl.BlockSpec(memory_space=pltpu.VMEM)
    third = lambda k, p: (jnp.minimum(k, 2), 0, 0)
    return pl.pallas_call(
        lambda *refs: pyramid_kernel(len(x_blocks), outs, *refs),
        grid_spec=pltpu.PrefetchScalarGridSpec(
            num_scalar_prefetch=1,
            grid=(4,),
            in_specs=[whole] * len(x_blocks)
            + [pl.BlockSpec((1, 9 * outs, cin), third), whole, whole],
            out_specs=[
                pl.BlockSpec((1, outs, pixels), lambda k, p: (k, 0, 0)),
                pl.BlockSpec((1, outs, PAD), third),
                pl.BlockSpec((1, outs, PAD), third),
            ],
            scratch_shapes=[pltpu.VMEM((9 * outs, pixels), F32)],
        ),
        out_shape=[
            jax.ShapeDtypeStruct((4, outs, pixels), F32),
            jax.ShapeDtypeStruct((3, outs, PAD), BF),
            jax.ShapeDtypeStruct((3, outs, PAD), BF),
        ],
        compiler_params=params(),
        cost_estimate=pl.CostEstimate(flops=2 * 28 * outs * cin * pixels, bytes_accessed=2 * (28 * outs + pixels) * cin, transcendentals=0),
    )(perm, *x_blocks, w_taps, w_one, masks)


def shifted_taps(read, lanes, rate, masks, store):
    col = lax.broadcasted_iota(jnp.int32, (1, lanes), 1) % WS
    for a in (-1, 0, 1):
        for b in (-1, 0, 1):
            shift = rate * (WS * a + b)
            first = (PAD - shift) // 128 * 128
            rest = PAD - shift - first
            window = read(first, lanes + 128)
            if rest:
                window = pltpu.roll(window, lanes + 128 - rest, 1)
            keep = ((col - b * rate >= 0) & (col - b * rate < WS)).astype(F32)
            if a:
                keep = keep * masks[(a + 1) // 2]
            store(3 * (a + 1) + b + 1, window[:, :lanes] * keep.astype(BF))


def dot_tn(a, b):
    return lax.dot_general(a, b, (((0,), (0,)), ((), ())), preferred_element_type=F32)


def input_grad_kernel(outs, dz_ref, spread_ref, mask_ref, w_ref, one_ref, pool_ref, out_ref, taps_ref):
    pixels = spread_ref.shape[1]

    @pl.when(pl.program_id(0) == 0)
    def _():
        for k in range(3):
            def store(tap, value, k=k):
                at = (9 * k + tap) * outs
                taps_ref[at : at + outs] = value

            masks = (mask_ref[2 * k : 2 * k + 1], mask_ref[2 * k + 1 : 2 * k + 2])
            rows = (k + 1) * outs
            shifted_taps(lambda first, n: dz_ref[rows : rows + outs, first : first + n], pixels, 6 * (k + 1), masks, store)
        taps_ref[27 * outs : 28 * outs] = dz_ref[:outs, PAD : PAD + pixels]
        taps_ref[28 * outs :] = spread_ref[...]

    weights = jnp.concatenate([w_ref[...], one_ref[...], pool_ref[...]], axis=0)
    for start, size in tiles(pixels, 512):
        out_ref[0, :, start : start + size] = dot_tn(weights, taps_ref[:, start : start + size]).astype(BF)


def input_grad(dz, spread, masks, w_taps, w_one, w_pool, perm):
    pixels = spread.shape[1]
    outs, cin = w_one.shape
    blocks = perm.shape[0]
    depth = cin // blocks
    whole = pl.BlockSpec(memory_space=pltpu.VMEM)
    slab = lambda rows: pl.BlockSpec((rows, depth), lambda i, p: (0, p[i]))

    def kernel(perm_ref, *refs):
        input_grad_kernel(outs, *refs)

    return pl.pallas_call(
        kernel,
        grid_spec=pltpu.PrefetchScalarGridSpec(
            num_scalar_prefetch=1,
            grid=(blocks,),
            in_specs=[whole, whole, whole, slab(27 * outs), slab(outs), slab(outs)],
            out_specs=pl.BlockSpec((1, depth, pixels), lambda i, p: (i, 0, 0)),
            scratch_shapes=[pltpu.VMEM((29 * outs, pixels), BF)],
        ),
        out_shape=jax.ShapeDtypeStruct((blocks, depth, pixels), BF),
        compiler_params=params(),
        cost_estimate=pl.CostEstimate(flops=2 * 29 * outs * cin * pixels, bytes_accessed=2 * (29 * outs + pixels) * cin, transcendentals=0),
    )(perm, dz, spread, masks, w_taps.reshape(27 * outs, cin), w_one, w_pool)


def pyramid_weight_kernel(lanes, outs, branches, plain, dz_ref, mask_ref, *refs):
    x_refs, (out_ref, taps_ref, acc_ref) = refs[:-3], refs[-3:]
    step = pl.program_id(0)
    start = pl.multiple_of(step * lanes, 128)

    @pl.when(step == 0)
    def _():
        acc_ref[...] = jnp.zeros_like(acc_ref)

    for n, k in enumerate(branches):
        def store(tap, value, n=n):
            at = (9 * n + tap) * outs
            taps_ref[at : at + outs] = value

        rows = slice((k + 1) * outs, (k + 2) * outs)
        masks = (mask_ref[0, 2 * k : 2 * k + 1], mask_ref[0, 2 * k + 1 : 2 * k + 2])
        shifted_taps(lambda first, n, rows=rows: dz_ref[rows, pl.ds(start + first, n)], lanes, 6 * (k + 1), masks, store)
    if plain:
        taps_ref[9 * len(branches) * outs :] = dz_ref[:outs, pl.ds(start + PAD, lanes)]
    acc_ref[...] += dot_nt(taps_ref[...], jnp.concatenate([x[0, 0] for x in x_refs], axis=0))

    @pl.when(step == pl.num_programs(0) - 1)
    def _():
        rows = 9 * len(branches) * outs
        out_ref[:rows] = acc_ref[:rows].astype(BF)
        spare = out_ref.shape[0] - acc_ref.shape[0]
        if spare:
            out_ref[rows : rows + spare] = jnp.zeros((spare, out_ref.shape[1]), BF)
        if plain:
            out_ref[rows + spare :] = acc_ref[rows:].astype(BF)


def pyramid_weight_grad(dz, x, masks, branches, plain, spare=0):
    devices, groups, slim, lanes = x.shape
    outs, canvas = dz.shape[0] // 4, groups * lanes
    channels = slim * devices
    out_rows = (9 * len(branches) + plain) * outs
    whole = pl.BlockSpec(memory_space=pltpu.VMEM)
    block = lambda j: pl.BlockSpec((1, 1, slim, lanes), lambda i: (j, i, 0, 0))
    return pl.pallas_call(
        lambda *refs: pyramid_weight_kernel(lanes, outs, branches, plain, *refs),
        grid=(groups,),
        in_specs=[whole, pl.BlockSpec((1, 8, lanes), lambda i: (i, 0, 0))] + [block(j) for j in range(devices)],
        out_specs=whole,
        out_shape=jax.ShapeDtypeStruct((out_rows + spare, channels), BF),
        scratch_shapes=[pltpu.VMEM((out_rows, lanes), BF), pltpu.VMEM((out_rows, channels), F32)],
        compiler_params=params(),
        cost_estimate=pl.CostEstimate(flops=2 * out_rows * channels * canvas, bytes_accessed=2 * (4 * outs + channels) * canvas, transcendentals=0),
    )(dz, masks, *([x] * devices))


def slope_kernel(first, centred_ref, valid_ref, cols_ref, offset_ref, slope_ref, act_ref):
    lane = iota(offset_ref.shape, 1)
    gain, shift, scale, mean = (cols_ref[:, i : i + 1] for i in range(4))
    group = first + pl.program_id(0)
    offset = jnp.sum(jnp.where(lane == group, offset_ref[...], 0.0), axis=1, keepdims=True) - mean
    slant, level = gain * scale, gain * scale * offset + shift
    y = centred_ref[0].astype(F32) * slant + level
    gate = 0.5 + 0.5 * jnp.tanh(0.5 * y)
    valid = valid_ref[0, 6:7]
    through = gate * valid
    act_ref[0] = (y * through).astype(BF)
    slope_ref[0] = (through * (1.0 + y * (1.0 - gate))).astype(BF)


def slopes(first, number, centred, canvas_rows, cols, offsets, into=None):
    groups, four, pixels = centred.shape
    whole = pl.BlockSpec(memory_space=pltpu.VMEM)
    take = lambda rows: pl.BlockSpec((1, rows, pixels), lambda i: (first + i, 0, 0))
    shape = jax.ShapeDtypeStruct((groups, four, pixels), BF)
    operands = [centred, canvas_rows, cols, offsets]
    in_specs = [take(four), take(8), whole, whole]
    aliases = {}
    if into is not None:
        aliases = {4: 0, 5: 1}
        operands += into
        in_specs += [pl.BlockSpec(memory_space=pl.ANY)] * 2
    return pl.pallas_call(
        lambda *refs: slope_kernel(first, *refs[:4], *refs[-2:]),
        grid=(number,),
        in_specs=in_specs,
        out_specs=[take(four), take(four)],
        out_shape=[shape, shape],
        input_output_aliases=aliases,
        compiler_params=params(),
        cost_estimate=BRIEF,
    )(*operands)


def canvas_kernel(groups, devices, *refs):
    dz_refs, refs = refs[:devices], refs[devices:]
    centred_ref, slope_ref, rows_ref, member_ref, w_ref, cols_ref, offset_ref, count = refs[:8]
    dz_ref, proj_ref, sums_ref, image_ref, pieces_ref, dy_ref = refs[8:]
    step = pl.program_id(0)
    four, pixels = centred_ref.shape[1:]
    share = dz_refs[0].shape[2]
    group = jnp.where(step < groups, step, step - groups)
    gain, scale, mean = (cols_ref[:, i : i + 1] for i in (0, 2, 3))
    offset = jnp.sum(jnp.where(iota(offset_ref.shape, 1) == group, offset_ref[...], 0.0), axis=1, keepdims=True) - mean
    level = offset * scale
    valid = rows_ref[0, 6:7]
    at = pl.multiple_of(group * pixels, 128)

    @pl.when(step == 0)
    def _():
        sums_ref[...] = jnp.zeros_like(sums_ref)
        image_ref[...] = jnp.zeros_like(image_ref)
        dz_ref[:, :PAD] = jnp.zeros((four, PAD), BF)
        dz_ref[:, PAD + groups * pixels :] = jnp.zeros((four, PAD), BF)

    @pl.when(step < groups)
    def _():
        for i in range(devices):
            pieces_ref[:, i * share : (i + 1) * share] = dz_refs[i][0]
        proj_ref[0] = pieces_ref[...]
        image_ref[...] += dot_nt(pieces_ref[...], member_ref[0].astype(BF))
        total = jnp.zeros((four, 128), F32)
        total_normed = jnp.zeros((four, 128), F32)
        for start, size in tiles(pixels, 512):
            part = slice(start, start + size)
            dy = dot(w_ref[...], pieces_ref[:, part]) * slope_ref[0, :, part].astype(F32)
            dy_ref[:, pl.ds(at + start, size)] = dy
            total = total + fold(dy)
            total_normed = total_normed + fold(dy * (centred_ref[0, :, part].astype(F32) * scale + level))
        sums_ref[:, 0:1] += jnp.sum(total, axis=1, keepdims=True)
        sums_ref[:, 1:2] += jnp.sum(total_normed, axis=1, keepdims=True)

    @pl.when(step >= groups)
    def _():
        steep = scale * gain
        rise = steep * count[0] * sums_ref[:, 1:2] * scale
        constant = steep * count[0] * (sums_ref[:, 0:1] + level * sums_ref[:, 1:2])
        parts = centred_ref[0].astype(F32) * rise + constant
        dz_ref[:, pl.ds(PAD + at, pixels)] = (steep * dy_ref[:, pl.ds(at, pixels)] - valid * parts).astype(BF)


def canvas_grad(proj_dz, slope, centred, canvas_rows, member, w_turned, cols, offsets, scalars):
    groups, four, pixels = centred.shape
    everyone, wide, share = proj_dz.shape
    devices = everyone // groups
    ahead = lambda s: jnp.minimum(s, groups - 1)
    by_group = lambda rows: pl.BlockSpec((1, rows, pixels), lambda s: (jnp.where(s < groups, s, s - groups), 0, 0))
    near = lambda rows: pl.BlockSpec((1, rows, pixels), lambda s: (ahead(s), 0, 0))
    piece = lambda i: pl.BlockSpec((1, wide, share), lambda s: (ahead(s) * devices + i, 0, 0))
    whole = pl.BlockSpec(memory_space=pltpu.VMEM)
    return pl.pallas_call(
        lambda *refs: canvas_kernel(groups, devices, *refs),
        grid=(2 * groups,),
        in_specs=[piece(i) for i in range(devices)]
        + [by_group(four), near(four), by_group(8), near(member.shape[1]), whole, whole, whole]
        + [pl.BlockSpec(memory_space=pltpu.SMEM)],
        out_specs=[whole, near(wide), whole, whole],
        out_shape=[
            jax.ShapeDtypeStruct((four, 2 * PAD + groups * pixels), BF),
            jax.ShapeDtypeStruct((groups, wide, pixels), BF),
            jax.ShapeDtypeStruct((four, 128), F32),
            jax.ShapeDtypeStruct((wide, member.shape[1]), F32),
        ],
        scratch_shapes=[pltpu.VMEM((wide, pixels), BF), pltpu.VMEM((four, groups * pixels), F32)],
        compiler_params=params(),
        cost_estimate=pl.CostEstimate(flops=2 * wide * four * groups * pixels, bytes_accessed=8 * wide * groups * pixels, transcendentals=0),
    )(*([proj_dz] * devices), centred, slope, canvas_rows, member, w_turned, cols, offsets, scalars)


def assembly_kernel(groups, devices, order, where_ref, pieces, spare, plain, out_ref, one_ref, rest_ref):
    line = groups // 2
    cin = out_ref.shape[1]
    depth = cin // devices
    slim = depth // groups

    def fill(refs, target):
        for r in range(0, groups, 2):
            for j in range(devices):
                part = slice(j * slim, (j + 1) * slim)
                pair = jnp.concatenate([refs[r][:, part], refs[r + 1][:, part]], axis=1)
                at = j * depth + r * slim
                target[:, at : at + 2 * slim] = pair.astype(F32)

    for z in range(line):
        for e in range(2):
            chosen = [order.index(line_part(z, r // 2 - z, (r ^ e) & 1)) for r in range(groups)]

            @pl.when((where_ref[0] // 2 == z) & (where_ref[0] % 2 == e))
            def _(chosen=chosen):
                fill([pieces[i] for i in chosen], out_ref)

                @pl.when(pl.program_id(0) == 0)
                def _():
                    fill([plain[i] for i in chosen], one_ref)
                    for r, i in enumerate(chosen):
                        rest_ref[r] = spare[i][...]


def assemble(found, devices, groups, strip, outs, cin):
    order = sorted(found)
    pieces = [found[key] for key in order]
    slots, width = len(pieces), pieces[0].shape[1]
    rows, spare = 9 * outs, 3 * outs
    smem = pl.BlockSpec(memory_space=pltpu.SMEM)

    def kernel(where_ref, *refs):
        parts = [refs[i * slots : (i + 1) * slots] for i in range(3)]
        assembly_kernel(groups, devices, order, where_ref, *parts, *refs[3 * slots :])

    return pl.pallas_call(
        kernel,
        grid=(3,),
        in_specs=[smem]
        + [pl.BlockSpec((rows, width), lambda i: (i, 0))] * slots
        + [pl.BlockSpec((spare, width), lambda i: (9, 0))] * slots
        + [pl.BlockSpec((outs, width), lambda i: (30, 0))] * slots,
        out_specs=[
            pl.BlockSpec((rows, cin), lambda i: (i, 0)),
            pl.BlockSpec((outs, cin), lambda i: (0, 0)),
            pl.BlockSpec((groups, spare, width), lambda i: (0, 0, 0)),
        ],
        out_shape=[
            jax.ShapeDtypeStruct((27 * outs, cin), F32),
            jax.ShapeDtypeStruct((outs, cin), F32),
            jax.ShapeDtypeStruct((groups, spare, width), BF),
        ],
        compiler_params=params(),
        cost_estimate=pl.CostEstimate(flops=0, bytes_accessed=27 * outs * cin * 6, transcendentals=0),
    )(strip[None].astype(jnp.int32), *pieces, *pieces, *pieces)


def local(
    feats,
    lowlevel,
    heights,
    widths,
    w_one,
    w_atrous,
    w_pool,
    w_proj,
    w_low,
    w_dec1,
    w_dec2,
    w_cls,
    b_cls,
    mid_gain,
    mid_shift,
    low_gain,
    low_shift,
    dec_gain,
    dec_shift,
    cotangent,
):
    devices, groups = lax.axis_size("ch"), lax.axis_size("row")
    me, strip = lax.axis_index("ch"), lax.axis_index("row")
    place = strip * devices + me
    everyone = devices * groups
    depth, pixels = feats.shape
    rows = pixels // WS
    canvas = groups * pixels
    outs = w_one.shape[0]
    wide = outs * devices
    images = heights.shape[0]
    share = pixels // devices
    fine = 16 * share
    fine_rows = fine // WF
    margin = WS if fine_rows % 4 == 0 else 2 * WS

    area = (heights * widths).astype(F32)
    count = jnp.sum(area)
    fine_count = 16.0 * count
    scalars = jnp.stack([1.0 / count, 1.0 / fine_count])
    places = jnp.stack([strip, place]).astype(jnp.int32)
    members = -(-images // 16) * 16
    window = share + 2 * margin
    ext = fine + 2 * WF
    shaped = lambda *shape: jax.ShapeDtypeStruct(shape, F32)
    strip_rows, member_strip, valid_fine_strip = geometry_call(
        strip_geometry_kernel,
        heights, widths, places,
        [shaped(8, pixels), jax.ShapeDtypeStruct((members, pixels), BF), jax.ShapeDtypeStruct((1, 16 * pixels), BF)],
    )
    valid_strip = strip_rows[6:7]

    mine = feats * valid_strip.astype(BF)
    slice_depth = depth // groups

    line = lambda *parts: jnp.concatenate([jnp.pad(v.astype(F32), (0, size - v.shape[0])) for v, size in parts])
    rank = lambda v: line((v.astype(F32).reshape(-1), 256))
    low_share = LOWC // devices
    vectors = jnp.stack(
        [
            rank(mid_gain[:4]),
            rank(mid_shift[:4]),
            rank(jnp.concatenate([mid_gain[4:], mid_shift[4:]])),
            rank(jnp.concatenate([dec_gain, dec_shift])),
            line((low_gain, 128), (low_shift, 128)),
        ]
    )
    message_rows = -(-images // 8) * 8
    sums = dot_nt(member_strip, mine)[:message_rows]
    told = tell_row(sums)
    told = tell_group(jnp.concatenate([jnp.sum(told, axis=0), jnp.pad(vectors, ((0, message_rows - 5), (0, 0)))], axis=1))

    geometry = geometry_call(
        lambda *refs: geometry_kernel(margin, *refs),
        heights, widths, places,
        [
            shaped(groups, 8, pixels), shaped(groups, members, pixels), shaped(groups, 1), shaped(everyone, 1),
            shaped(everyone, 1), shaped(members + 8, share), shaped(1, window), shaped(1, ext), shaped(2, fine),
            jax.ShapeDtypeStruct((window, ext), BF),
        ],
    )

    x_blocks, origin, (told, late_low, late_w1, late_w2, late_proj, late_pool, *geometry) = gather_blocks(
        mine, (told, lowlevel, w_dec1, w_dec2, w_proj, w_pool, *geometry)
    )
    (
        canvas_rows, member_canvas, strip_counts, counts_c, counts_f, mine_rows, window_valid, valid_wide, fine_masks, enlarge,
    ) = geometry
    perm = jnp.stack(origin).astype(jnp.int32)
    mine, told = lax.optimization_barrier((mine, told))
    x_slice = lax.all_to_all(mine.reshape(groups, slice_depth, pixels), "row", 0, 0)
    first_told = told

    proj_taps = late_proj.reshape(outs, 5, wide).transpose(1, 0, 2)
    pool_taps = late_pool.reshape(outs, -1, wide).transpose(1, 0, 2)
    rest = lax.all_gather(jnp.concatenate([late_w2.transpose(1, 0, 2), proj_taps, pool_taps], axis=0), "ch", axis=0)
    w2, wp, w_pool_all = rest[:, :9], rest[:, 9:14], rest[:, 14:]
    wp_acts = wp[:, :4].reshape(devices, 4, outs, devices, outs).transpose(3, 0, 2, 1, 4).reshape(devices, wide, 4 * outs)
    wp_pool = wp[:, 4].reshape(wide, wide)

    low_in = late_low * valid_fine_strip
    low_part = dot(w_low, low_in).astype(BF)
    low_pre = lax.psum_scatter(low_part, "ch", scatter_dimension=1, tiled=True).astype(F32)
    first_taps = late_w1.transpose(1, 0, 2)
    w1 = lax.all_gather(jnp.concatenate([first_taps[:, :, LOWC:], first_taps[:, :, :LOWC]], axis=2), "ch", axis=0)

    area_rows = jnp.pad(area, (0, message_rows - images), constant_values=1.0)[:, None]
    pair = shaped(2, 256)
    branch_gains, proj_gain, first_gain, second_gain, low_gains, broad_part = small_call(
        lambda *refs: parameter_kernel(depth, *refs),
        [first_told, w_pool_all, wp_pool, area_rows],
        (),
        [shaped(devices, 2, 256), pair, pair, pair, pair, shaped(1, wide, images)],
        0,
    )

    w_taps = w_atrous.transpose(0, 2, 1, 3).reshape(3, 9 * outs, -1)
    centre, up, down = pyramid(x_blocks, perm, w_taps, w_one, strip_rows)
    up, down, x_slice = lax.optimization_barrier((up, down, x_slice))
    x_canvas = lax.all_gather(x_slice, "ch", axis=0)
    fwd = [(i, i + 1) for i in range(groups - 1)]
    bwd = [(i + 1, i) for i in range(groups - 1)]
    from_next = lax.ppermute(up, "row", bwd)
    from_prev = lax.ppermute(down, "row", fwd)

    member_mine, valid_mine = mine_rows[:images], mine_rows[members : members + 1]
    valid_fine = valid_wide[:, WF:-WF]
    low_stats = vector_tile(*local_moments(low_pre, valid_fine[0]))[:4]

    order = jnp.argsort(perm)

    def columns(s, lead):
        s = s.reshape((groups,) + lead + (devices, slice_depth))
        s = jnp.moveaxis(s, 0, len(lead) + 1)
        return s.reshape(lead + (devices * depth,)).astype(F32)

    gain_mid, shift_mid = mid_gain.astype(F32), mid_shift.astype(F32)

    branch_valid, branch_gains, wp_acts, broad_part = lax.optimization_barrier((valid_strip, branch_gains, wp_acts, broad_part))

    tile = jax.ShapeDtypeStruct((everyone, 8, 128), F32)
    centered, pieces, stats = small_call(
        branch_kernel,
        [centre, from_next, from_prev, branch_valid],
        (),
        [
            jax.ShapeDtypeStruct((4 * outs, pixels), BF),
            jax.ShapeDtypeStruct((devices, 4 * outs, share), BF),
            tile,
        ],
        0,
    )
    told_branch = swap_all(stats)
    swapped = swap_ch(pieces)
    proj_pre, proj_left, proj_right, stats = small_call(
        project_kernel,
        [
            swapped, told_branch.reshape(groups, devices, 8, 128), strip_counts, branch_gains, wp_acts, broad_part, member_mine,
            valid_mine, low_stats, scalars, jnp.concatenate([strip[None].astype(jnp.int32), perm]),
        ],
        (9, 10),
        [
            jax.ShapeDtypeStruct((wide, share), F32),
            jax.ShapeDtypeStruct((wide, margin), F32),
            jax.ShapeDtypeStruct((wide, margin), F32),
            tile,
        ],
        8 * wide * wide * share,
    )
    proj_prev, proj_next = to_next(proj_right), to_previous(proj_left)
    low_prev, low_next = to_next(low_pre[:, -WF:]), to_previous(low_pre[:, :WF])
    told_proj, proj_prev, proj_next, low_prev, low_next = lax.optimization_barrier(
        (swap_all(stats), proj_prev, proj_next, low_prev, low_next)
    )
    canvas_centered = lax.all_gather(centered, "row", axis=0)
    own_told = lax.dynamic_index_in_dim(told_branch.reshape(groups, devices, 8 * 128), me, 1, False)
    own_mean, own_scale = merge_moments(own_told[:, : 4 * outs], own_told[:, 256 : 256 + 4 * outs], strip_counts[:, 0], count)
    cols = jnp.stack([gain_mid[:4].reshape(-1), shift_mid[:4].reshape(-1), own_scale, own_mean], axis=1)
    offsets = own_told[:, : 4 * outs].T

    lanes = WF * rows_per_step(fine_rows)
    edge = jax.ShapeDtypeStruct((wide, WF), F32)
    full = jax.ShapeDtypeStruct((wide, fine), F32)
    work = 18 * wide * wide * fine
    state = lambda n, channels: pltpu.VMEM((n, channels, 128), F32)
    decoder_in, first_pre, first_top, first_bottom, stats = decoder_call(
        lambda *refs: first_kernel(lanes, *refs),
        [
            proj_prev, proj_pre, proj_next, told_proj, counts_c, proj_gain, window_valid, enlarge, low_prev, low_pre, low_next,
            told_proj, counts_f, low_gains, valid_wide, fine_masks, w1, scalars,
        ],
        (), (17,),
        [jax.ShapeDtypeStruct((wide + LOWC, ext), BF), full, edge, edge, tile],
        (1,),
        [pltpu.VMEM((wide, window), BF), pltpu.VMEM((3 * wide, 3 * (wide + LOWC)), BF), state(3, wide)],
        fine, work,
    )
    first_prev, first_next = to_next(first_bottom), to_previous(first_top)
    told_first, first_prev, first_next, told_proj = lax.optimization_barrier((swap_all(stats), first_prev, first_next, told_proj))
    proj_told = told_proj.reshape(everyone, 8 * 128)
    proj_mean, proj_scale = merge_moments(proj_told[:, :wide], proj_told[:, 256 : 256 + wide], counts_c[:, 0], count)
    proj_normed = (proj_pre - proj_mean[:, None]) * proj_scale[:, None]
    first_act, second_pre, second_top, second_bottom, stats = decoder_call(
        lambda *refs: second_kernel(lanes, *refs),
        [first_prev, first_pre, first_next, told_first, counts_f, first_gain, valid_wide, fine_masks, w2, scalars],
        (), (9,),
        [jax.ShapeDtypeStruct((wide, ext), BF), full, edge, edge, tile],
        (1,),
        [pltpu.VMEM((3 * wide, 3 * wide), BF), state(3, wide)],
        fine, work,
    )
    told_second = swap_all(stats)
    second_prev, second_next = to_next(second_bottom), to_previous(second_top)
    told_second, second_prev, second_next, x_canvas = lax.optimization_barrier(
        (told_second, second_prev, second_next, x_canvas)
    )

    classes = w_cls.shape[0]
    cot = jnp.pad(cotangent, ((0, -classes % 32), (0, 0)))
    cot_prev, cot_next = to_next(cot[:, -WF:]), to_previous(cot[:, :WF])
    w_cls_wide = jnp.pad(w_cls, ((0, -classes % 32), (0, 0)))
    bias = jnp.pad(b_cls.astype(F32), (0, -classes % 32))[:, None]
    logits, class_part, bias_part, sums = decoder_call(
        class_kernel,
        [
            second_pre, cot, valid_fine, told_second, counts_f, second_gain, w_cls_wide, w_cls_wide.T, bias, scalars,
        ],
        (0, 1, 2), (9,),
        [
            jax.ShapeDtypeStruct((classes, fine), F32),
            jax.ShapeDtypeStruct((w_cls_wide.shape[0], wide), F32),
            jax.ShapeDtypeStruct((w_cls_wide.shape[0], 128), F32),
            tile,
        ],
        (0,),
        [state(2, wide), pltpu.VMEM((wide, 128), F32)],
        fine, work // 8,
    )
    told_sums = swap_all(sums)
    class_part = jnp.concatenate([class_part[:classes].reshape(-1), jnp.sum(bias_part[:classes], axis=1)])
    class_rows = -(-class_part.shape[0] // (128 * everyone))
    class_part = jnp.pad(class_part, (0, class_rows * 128 * everyone - class_part.shape[0])).reshape(everyone, class_rows, 128)
    class_part = jnp.pad(class_part, ((0, 0), (0, 8 - class_rows), (0, 0)))
    second_dz, first_dy, dy_top, dy_bottom, sums = decoder_call(
        lambda *refs: second_back_kernel(lanes, *refs),
        [
            second_prev, second_pre, second_next, told_second, counts_f, second_gain, told_sums, cot_prev, cot, cot_next,
            w_cls_wide.T, valid_wide, fine_masks, w2, first_pre, told_first, first_gain, class_part, scalars,
        ],
        (14,), (18,),
        [jax.ShapeDtypeStruct((wide, ext), BF), full, edge, edge, jax.ShapeDtypeStruct((everyone, 16, 128), F32)],
        (1,),
        [pltpu.VMEM((3 * wide, 3 * wide), BF), state(2, wide), pltpu.VMEM((wide, 128), F32)],
        fine, work,
    )
    second_sums = jnp.sum(told_sums, axis=0)
    dy_prev, dy_next = to_next(dy_bottom), to_previous(dy_top)
    told_first_sums, dy_prev, dy_next = lax.optimization_barrier((swap_all(sums), dy_prev, dy_next))
    first_sums = jnp.sum(told_first_sums, axis=0)
    class_share = first_sums[8 : 8 + class_rows]
    first_sums = first_sums[:8]
    g_dec2 = decoder_weight_grad(second_dz, first_act, fine_masks, outs)
    told_first_sums, g_dec2 = lax.optimization_barrier((told_first_sums, g_dec2))
    first_dz, grad_window, dy_low, low_part_sums = decoder_call(
        lambda *refs: first_back_kernel(lanes, *refs),
        [
            first_prev, first_pre, first_next, dy_prev, first_dy, dy_next, told_first, counts_f, first_gain, told_first_sums,
            valid_wide, fine_masks, w1, enlarge, low_pre, told_proj, low_gains, scalars,
        ],
        (14,), (17,),
        [
            jax.ShapeDtypeStruct((wide, ext), BF),
            jax.ShapeDtypeStruct((wide, window), F32),
            jax.ShapeDtypeStruct((LOWC, fine), F32),
            jax.ShapeDtypeStruct((2, 256), F32),
        ],
        (2,),
        [pltpu.VMEM((3 * (wide + LOWC), 3 * wide), BF), state(2, LOWC), pltpu.VMEM((LOWC, 128), F32)],
        fine, work,
    )
    g_dec1 = decoder_weight_grad(first_dz, decoder_in, fine_masks, outs)

    def norm_back(dy, normed, scale, gain, totals, valid, total):
        parts = (totals[0][:, None] + normed * totals[1][:, None]) * (valid / total)
        return (scale * gain)[:, None] * (dy - parts)

    grad_coarse = grad_window[:, margin : margin + share]
    grad_coarse = grad_coarse.at[:, :margin].add(to_next(grad_window[:, margin + share :]))
    grad_coarse = grad_coarse.at[:, share - margin :].add(to_previous(grad_window[:, :margin]))
    dy = grad_coarse * silu_slope(proj_gain[0][:, None] * proj_normed + proj_gain[1][:, None]) * valid_mine
    both = vector_tile(jnp.sum(dy, axis=1), jnp.sum(dy * proj_normed, axis=1), low_part_sums[0], low_part_sums[1])
    both = jnp.concatenate([both, jnp.pad(class_share, ((0, 8 - class_rows), (0, 0)))])
    told_both, g_dec1 = lax.optimization_barrier((tell_all(both), g_dec1))
    part_dec = lax.psum_scatter(jnp.concatenate([g_dec2, g_dec1], axis=3), "ch", scatter_dimension=0)
    both = jnp.sum(told_both[:, :8], axis=0).reshape(4, 256)
    class_sums = told_both[:, 8 : 8 + class_rows].reshape(-1)
    bias_sums = class_sums[classes * wide : classes * wide + classes]
    class_sums = class_sums[: classes * wide].reshape(classes, wide)
    proj_sums, low_sums = both[:2], both[2:, :LOWC]

    proj_dz = norm_back(dy, proj_normed, proj_scale, proj_gain[0], proj_sums, valid_mine, count).astype(BF)
    canvas_dz = lax.all_gather(proj_dz, BOTH, axis=0)
    slope = slopes(0, groups, canvas_centered, canvas_rows, cols, offsets)
    canvas_dz, *slope = lax.optimization_barrier((canvas_dz, *slope))

    wp_own = lax.dynamic_index_in_dim(wp_acts, me, 0, False)
    wp_pool_own = lax.dynamic_slice_in_dim(wp_pool, me * outs, outs, axis=1)
    padded_dz, strips_dz, branch_sums, image_dz = canvas_grad(
        canvas_dz, slope[0], canvas_centered, canvas_rows, member_canvas, wp_own.T, cols, offsets, 1.0 / count[None],
    )
    branch_sums = branch_sums[:, :2].T
    image_dz = image_dz[:, :images]

    padded_dz, part_dec = lax.optimization_barrier((padded_dz, part_dec))

    def by_row(v):
        v = v.reshape(groups, -1)
        return jnp.pad(v, ((0, 0), (0, -v.shape[1] % wide))).reshape(groups, -1, wide)

    shares = [by_row(part_dec[..., :wide]), by_row(part_dec[..., wide : 2 * wide]), by_row(part_dec[..., 2 * wide :])]
    share_rows, split_at = shares[0].shape[1], 2 * shares[0].shape[1]
    shares = lax.all_to_all(jnp.concatenate(shares, axis=1), "row", 0, 0)
    shares = jnp.sum(shares.astype(F32), axis=0).astype(BF)

    lined = groups == 8 and 2 * slice_depth == 128 and shares.shape[0] <= 3 * outs
    part = pyramid_weight_grad(padded_dz, x_canvas, canvas_rows, (0, 1, 2), True, 3 * outs if lined else 0)
    if lined:
        part = part.at[27 * outs : 27 * outs + shares.shape[0]].set(shares)
    part, padded_dz, first_told, image_dz, strips_dz, dy_low = lax.optimization_barrier(
        (part, padded_dz, first_told, image_dz, strips_dz, dy_low)
    )

    low_mean, low_scale = merge_moments(proj_told[:, 512 : 512 + LOWC], proj_told[:, 768 : 768 + LOWC], counts_f[:, 0], fine_count)
    low_normed = (low_pre - low_mean[:, None]) * low_scale[:, None]
    low_dz = norm_back(dy_low, low_normed, low_scale, low_gains[0, :LOWC], low_sums, valid_fine, fine_count).astype(BF)

    pool_sums = first_told[:, :images, :depth].transpose(0, 2, 1).reshape(devices * depth, images)
    pooled = (pool_sums / area[None]).astype(BF)
    pool_pre = dot(w_pool, pooled)
    pool_mean = jnp.mean(pool_pre, axis=1)
    pool_scale = lax.rsqrt(jnp.mean(pool_pre * pool_pre, axis=1) - pool_mean * pool_mean + EPSILON)
    pool_normed = (pool_pre - pool_mean[:, None]) * pool_scale[:, None]
    pool_shifted = gain_mid[4][:, None] * pool_normed + shift_mid[4][:, None]
    pool_act = jax.nn.silu(pool_shifted).astype(BF)

    g_proj_pool = jnp.dot(image_dz, pool_act.astype(F32).T, precision=HIGHEST)

    grad_pool_act = lax.dot_general(wp_pool_own.astype(F32), image_dz, (((0,), (0,)), ((), ())), precision=HIGHEST)
    dy_pool = grad_pool_act * silu_slope(pool_shifted)
    pool_gain_sum = jnp.sum(dy_pool * pool_normed, axis=1)
    pool_shift_sum = jnp.sum(dy_pool, axis=1)
    pool_dz = (
        (pool_scale * gain_mid[4])[:, None]
        * (dy_pool - (pool_shift_sum[:, None] + pool_normed * pool_gain_sum[:, None]) / images)
    ).astype(BF)
    g_w_pool = dot_nt(pool_dz, pooled)
    spread = jnp.dot(pool_dz.astype(F32) / area[None], member_strip[:images].astype(F32), precision=HIGHEST).astype(BF)

    strip_pad = lax.dynamic_slice_in_dim(padded_dz, strip * pixels, pixels + 2 * PAD, axis=1)

    parts = input_grad(strip_pad, spread, strip_rows, w_taps, w_one, w_pool, jnp.arange(devices, dtype=jnp.int32))
    g_feats = lax.psum_scatter(parts, "ch", scatter_dimension=0).astype(F32) * valid_strip
    low_dz_all = lax.all_gather(low_dz, "ch", axis=1, tiled=True)
    g_lowlevel = lax.dot_general(w_low, low_dz_all, (((0,), (0,)), ((), ())), preferred_element_type=F32)
    g_lowlevel = g_lowlevel * valid_fine_strip.astype(F32)
    g_low = jnp.sum(tell_row(dot_nt(low_dz_all, low_in)), axis=0)
    g_proj_acts = jnp.einsum("gop,gcp->oc", strips_dz, slope[1], preferred_element_type=F32)
    g_proj_part = jnp.concatenate([g_proj_acts, g_proj_pool], axis=1).astype(BF)
    g_proj = jnp.take(swap_ch(g_proj_part.reshape(devices, outs, 5 * outs)), order, axis=0)
    g_w_proj = g_proj.reshape(devices, outs, 5, outs).transpose(1, 2, 0, 3).reshape(outs, -1).astype(F32)

    if lined:
        into, g_w_one, rest = assemble(gather_line(part), devices, groups, strip, outs, devices * depth)
    else:
        found = columns(lax.all_gather(part, "row", axis=0), (28 * outs,))
        into, g_w_one = found[: 27 * outs], found[27 * outs :]
        rest = lax.all_gather(shares, "row", axis=0)
    g_w_atrous = into.reshape(3, 9, outs, devices * depth).transpose(0, 2, 1, 3)

    rest = rest[:, : shares.shape[0]].astype(F32)
    back = lambda v, shape: v.reshape(groups, -1)[:, : math.prod(shape) // groups].reshape(shape)
    g_dec2 = back(rest[:, :share_rows], (9, outs, wide))
    g_dec1 = jnp.concatenate(
        [back(rest[:, share_rows:split_at], (9, outs, wide)), back(rest[:, split_at:], (9, outs, LOWC))], axis=2
    )
    g_w_dec1 = jnp.concatenate([g_dec1[:, :, wide:], g_dec1[:, :, :wide]], axis=2).transpose(1, 0, 2)
    g_w_dec2 = g_dec2.transpose(1, 0, 2)

    def my(v, n):
        return lax.dynamic_slice_in_dim(v, me * n, n, axis=-1)

    second_sums, first_sums = second_sums.reshape(4, 256), first_sums.reshape(4, 256)
    g_mid_gain = jnp.concatenate([branch_sums[1].reshape(4, outs), pool_gain_sum[None], my(proj_sums[1], outs)[None]])
    g_mid_shift = jnp.concatenate([branch_sums[0].reshape(4, outs), pool_shift_sum[None], my(proj_sums[0], outs)[None]])
    return (
        logits,
        g_feats,
        g_lowlevel,
        g_w_one,
        g_w_atrous,
        g_w_pool,
        g_w_proj,
        g_low,
        g_w_dec1,
        g_w_dec2,
        class_sums,
        bias_sums,
        g_mid_gain,
        g_mid_shift,
        my(low_sums[1], low_share),
        my(low_sums[0], low_share),
        jnp.stack([my(first_sums[1], outs), my(second_sums[1], outs)]),
        jnp.stack([my(first_sums[0], outs), my(second_sums[0], outs)]),
    )


def solution(mesh):
    placed = (
        P("ch", "row"),
        P("ch", "row"),
        P(),
        P(),
        P("ch", None),
        P(None, "ch", None, None),
        P("ch", None),
        P("ch", None),
        P(None, "ch"),
        P("ch", None, None),
        P("ch", None, None),
        P(),
        P(),
        P(None, "ch"),
        P(None, "ch"),
        P("ch"),
        P("ch"),
        P(None, "ch"),
        P(None, "ch"),
        P(None, ("row", "ch")),
    )
    return jax.shard_map(
        local,
        mesh=mesh,
        in_specs=placed,
        out_specs=(
            P(None, ("row", "ch")),
            P("ch", "row"),
            P("ch", "row"),
            P("ch", None),
            P(None, "ch", None, None),
            P("ch", None),
            P("ch", None),
            P(None, "ch"),
            P("ch", None, None),
            P("ch", None, None),
            P(),
            P(),
            P(None, "ch"),
            P(None, "ch"),
            P("ch"),
            P("ch"),
            P(None, "ch"),
            P(None, "ch"),
        ),
        check_vma=False,
    )
```

```python
import math

import jax
import jax.numpy as jnp
from jax import lax
from jax.experimental import pallas as pl
from jax.experimental.pallas import tpu as pltpu
from jax.sharding import PartitionSpec as P

LOWC = 48
WS = 32
WF = 4 * WS
REACH = 18
PAD = 640
EPSILON = 1e-05
HIGHEST = lax.Precision.HIGHEST
BF = jnp.bfloat16
F32 = jnp.float32
BOTH = ("row", "ch")
BRIEF = pl.CostEstimate(flops=1, bytes_accessed=1, transcendentals=0)
VMEM_LIMIT = 56 * 1024 * 1024


def params():
    return pltpu.CompilerParams(vmem_limit_bytes=VMEM_LIMIT)


def dot(a, b):
    return jnp.dot(a, b, preferred_element_type=F32)


def dot_nt(a, b):
    return lax.dot_general(a, b, (((1,), (1,)), ((), ())), preferred_element_type=F32)


def tiles(extent, size):
    return [(start, min(size, extent - start)) for start in range(0, extent, size)]


class Images:
    def __init__(self, heights_ref, widths_ref):
        self.ends, self.widths, total = [], [], 0
        for i in range(heights_ref.shape[0]):
            total = total + heights_ref[i]
            self.ends.append(total)
            self.widths.append(widths_ref[i])
        self.total = total

    def image(self, rows, factor=1):
        return sum((rows >= end * factor).astype(jnp.int32) for end in self.ends)

    def same(self, rows, offset, factor=1):
        others = rows + offset
        inside = (rows >= 0) & (rows < self.total * factor) & (others >= 0) & (others < self.total * factor)
        return jnp.where(inside & (self.image(rows, factor) == self.image(others, factor)), 1.0, 0.0)

    def limit(self, rows, factor=1):
        image = self.image(rows, factor)
        value = jnp.zeros(rows.shape, jnp.int32)
        for i, width in enumerate(self.widths):
            value = jnp.where(image == i, width * factor, value)
        return jnp.where(rows >= 0, value, 0)


def iota(shape, axis):
    return lax.broadcasted_iota(jnp.int32, shape, axis)


def split(index, size):
    return jnp.right_shift(index, size.bit_length() - 1), jnp.bitwise_and(index, size - 1)


def tap_rows(images, rows, col):
    masks = [images.same(rows, -a * rate) for rate in (6, 12, 18) for a in (-1, 1)]
    return masks + [jnp.where(col < images.limit(rows), 1.0, 0.0)]


def strip_geometry_kernel(heights, widths, places, rows_ref, member_ref, fine_ref):
    images = Images(heights, widths)
    pixels = rows_ref.shape[1]
    row, col = split(places[0] * pixels + iota((1, pixels), 1), WS)
    values = tap_rows(images, row, col)
    for i, value in enumerate(values):
        rows_ref[i : i + 1] = value
    rows_ref[7:8] = jnp.zeros((1, pixels), F32)
    image = images.image(row)
    number = iota(member_ref.shape, 0)
    member_ref[...] = (jnp.where(number == image, 1.0, 0.0) * values[6]).astype(BF)
    row, col = split(places[0] * 16 * pixels + iota(fine_ref.shape, 1), WF)
    fine_ref[...] = jnp.where(col < images.limit(row, 4), 1.0, 0.0).astype(BF)


def geometry_kernel(
    margin, heights, widths, places,
    canvas_ref, member_ref, strips_ref, shares_ref, fines_ref, mine_ref, window_ref, ext_ref, masks_ref, enlarge_ref,
):
    images = Images(heights, widths)
    groups, _, pixels = canvas_ref.shape
    everyone, share = shares_ref.shape[0], mine_ref.shape[1]
    place = places[1]
    shape = (groups, pixels)
    row, col = split(iota(shape, 0) * pixels + iota(shape, 1), WS)
    values = tap_rows(images, row, col)
    for i, value in enumerate(values):
        canvas_ref[:, i] = value
    canvas_ref[:, 7] = jnp.zeros(shape, F32)
    image = images.image(row)
    for i in range(member_ref.shape[1]):
        member_ref[:, i] = jnp.where(image == i, values[6], 0.0)
    strips_ref[...] = jnp.sum(values[6], axis=1, keepdims=True)

    def counted(pixels, cols, factor):
        row, col = split(iota((everyone, pixels), 0) * pixels + iota((everyone, pixels), 1), cols)
        return jnp.sum(jnp.where(col < images.limit(row, factor), 1.0, 0.0), axis=1, keepdims=True)

    shares_ref[...] = counted(share, WS, 1)
    rows = masks_ref.shape[1] // WF
    number = iota((everyone, rows), 0) * rows + iota((everyone, rows), 1)
    fines_ref[...] = jnp.sum(images.limit(number, 4).astype(F32), axis=1, keepdims=True)

    row, col = split(place * share + iota((1, share), 1), WS)
    valid = jnp.where(col < images.limit(row), 1.0, 0.0)
    image = images.image(row)
    last = mine_ref.shape[0] - 8
    mine_ref[:last] = jnp.where(iota((last, share), 0) == image, 1.0, 0.0) * valid
    mine_ref[last:] = jnp.broadcast_to(valid, (8, share))
    row, col = split(place * share - margin + iota(window_ref.shape, 1), WS)
    window_ref[...] = jnp.where(col < images.limit(row), 1.0, 0.0)

    first = place * rows
    row, col = split(iota((1, masks_ref.shape[1]), 1), WF)
    for i, offset in enumerate((-1, 1)):
        masks_ref[i : i + 1] = images.same(first + row, offset, 4)
    window, ext = enlarge_ref.shape
    at_row, at_col = split(place * share - margin + iota((window, 1), 0), WS)
    for start, size in tiles(ext, 512):
        row, col = split(start + iota((1, size), 1), WF)
        row = first - 1 + row
        valid = jnp.where(col < images.limit(row, 4), 1.0, 0.0)
        ext_ref[:, start : start + size] = valid

        def weights(phase):
            middle = jnp.where((phase == 0) | (phase == 3), 0.625, 0.875)
            before = jnp.where(phase == 0, 0.375, jnp.where(phase == 1, 0.125, 0.0))
            after = jnp.where(phase == 3, 0.375, jnp.where(phase == 2, 0.125, 0.0))
            return middle, before, after

        def part(there, here, middle, before, after):
            apart = there - here
            return jnp.where(apart == 0, middle, jnp.where(apart == -1, before, jnp.where(apart == 1, after, 0.0)))

        q, phase = split(row, 4)
        middle, before, after = weights(phase)
        by_row = part(at_row, q, middle * valid, before * images.same(q, -1) * valid, after * images.same(q, 1) * valid)
        q, phase = split(col, 4)
        enlarge_ref[:, start : start + size] = (by_row * part(at_col, q, *weights(phase))).astype(BF)


def geometry_call(kernel, heights, widths, places, outputs):
    smem = pl.BlockSpec(memory_space=pltpu.SMEM)
    return pl.pallas_call(
        kernel,
        in_specs=[smem] * 3,
        out_specs=[pl.BlockSpec(memory_space=pltpu.VMEM)] * len(outputs),
        out_shape=outputs,
        compiler_params=params(),
        cost_estimate=pl.CostEstimate(flops=20000000, bytes_accessed=6000000, transcendentals=0),
    )(heights, widths, places)


def gather_blocks(x, meanwhile=()):
    count, me = lax.axis_size("ch"), lax.axis_index("ch")
    if count == 4:
        cross = lambda v, m: lax.ppermute(v, "ch", [(i, i ^ m) for i in range(count)])
        far = cross(x, 2)
        near = cross(x, 1)
        if meanwhile:
            far, *meanwhile = lax.optimization_barrier((far, *meanwhile))
        return [x, near, far, cross(far, 1)], [me, me ^ 1, me ^ 2, me ^ 3], meanwhile
    every = lax.all_gather(x, "ch", axis=0)
    return [every[i] for i in range(count)], [jnp.int32(i) for i in range(count)], meanwhile


def swap_ch(x):
    count, me = lax.axis_size("ch"), lax.axis_index("ch")
    if count != 4:
        return lax.all_to_all(x, "ch", 0, 0)
    pick = lambda i: lax.dynamic_index_in_dim(x, i, 0, False)
    blocks = [pick(me)]
    for m in (1, 2, 3):
        blocks.append(lax.ppermute(pick(me ^ m), "ch", [(i, i ^ m) for i in range(count)]))
    return jnp.stack(blocks)


def reduce_blocks(blocks):
    count = lax.axis_size("ch")
    if count == 4:
        cross = lambda v, m: lax.ppermute(v, "ch", [(i, i ^ m) for i in range(count)])
        arrived = cross(jnp.stack([blocks[3], blocks[1]]), 1).astype(F32)
        onward = (blocks[2].astype(F32) + arrived[0]).astype(BF)
        return blocks[0].astype(F32) + arrived[1] + cross(onward, 2).astype(F32)
    return lax.psum_scatter(jnp.stack(blocks), "ch", scatter_dimension=0).astype(F32)


def gather_line(x, later, finish):
    def along(v, places, step):
        return lax.ppermute(v, "row", [(2 * i + e, 2 * (i + step) + e) for i in places for e in range(2)])

    def beside(v, places):
        return lax.ppermute(v, "row", [(2 * i + e, 2 * i + 1 - e) for i in places for e in range(2)])

    def together(*keys):
        got.update(zip(keys, lax.optimization_barrier(tuple(got[key] for key in keys))))

    got = {(0, 0, 0): x}
    got[-1, 0, 0], got[1, 0, 0] = along(x, (0, 1, 2), 1), along(x, (1, 2, 3), -1)
    got[0, 1, 0] = beside(x, (0, 1, 2, 3))
    together((-1, 0, 0), (1, 0, 0), (0, 1, 0))
    got[0, 1, 0], later = lax.optimization_barrier((got[0, 1, 0], later))
    finished = finish(*later)
    got[-2, 0, 0], got[2, 0, 0] = along(got[-1, 0, 0], (1, 2), 1), along(got[1, 0, 0], (1, 2), -1)
    got[-1, 1, 0], got[1, 1, 0] = beside(got[-1, 0, 0], (1, 2, 3)), beside(got[1, 0, 0], (0,))
    together((-2, 0, 0), (2, 0, 0), (-1, 1, 0), (1, 1, 0), (1, 0, 0))
    got[-3, 0, 0], got[3, 0, 0] = along(got[-2, 0, 0], (2,), 1), along(got[2, 0, 0], (1,), -1)
    got[1, 1, 1] = beside(got[1, 0, 0], (1, 2))
    got[-2, 1, 0], got[2, 1, 0] = beside(got[-2, 0, 0], (3,)), beside(got[2, 0, 0], (0,))
    together((-3, 0, 0), (3, 0, 0), (1, 1, 1), (-2, 1, 0), (2, 1, 0), (-2, 0, 0), (2, 0, 0))
    got[-2, 1, 1], got[2, 1, 1] = beside(got[-2, 0, 0], (2,)), beside(got[2, 0, 0], (1,))
    got[-3, 1, 0], got[3, 1, 0] = beside(got[-3, 0, 0], (3,)), beside(got[3, 0, 0], (0,))
    got[-3, 1, 0], finished = lax.optimization_barrier((got[-3, 1, 0], finished))
    return got, finished


def line_part(place, steps, side):
    first = {(1, 1): (0,), (-2, 1): (3,), (2, 1): (0,)}.get((steps, side))
    return (steps, side, 0 if first is None or place in first else 1)


def swap_all(values):
    return lax.all_to_all(values, BOTH, 0, 0)


def tell_all(values):
    count = lax.axis_size("row") * lax.axis_size("ch")
    return swap_all(jnp.broadcast_to(values[None], (count,) + values.shape))


def tell_row(values):
    count = lax.axis_size("row")
    return lax.all_to_all(jnp.broadcast_to(values[None], (count,) + values.shape), "row", 0, 0)


def tell_group(values):
    count = lax.axis_size("ch")
    return lax.all_to_all(jnp.broadcast_to(values[None], (count,) + values.shape), "ch", 0, 0)


def vector_tile(*vectors):
    rows = [jnp.pad(v, (0, 256 - v.shape[0])).reshape(2, 128) for v in vectors]
    return jnp.pad(jnp.concatenate(rows), ((0, 8 - 2 * len(rows)), (0, 0)))


def to_next(x):
    count = lax.axis_size("row") * lax.axis_size("ch")
    return lax.ppermute(x, BOTH, [(i, i + 1) for i in range(count - 1)])


def to_previous(x):
    count = lax.axis_size("row") * lax.axis_size("ch")
    return lax.ppermute(x, BOTH, [(i + 1, i) for i in range(count - 1)])


def merge_moments(means, spreads, counts, total):
    mean = jnp.sum(means * counts[:, None], axis=0) / total
    away = means - mean[None]
    var = (jnp.sum(spreads, axis=0) + jnp.sum(counts[:, None] * away * away, axis=0)) / total
    return mean, lax.rsqrt(var + EPSILON)


def silu_slope(y):
    gate = jax.nn.sigmoid(y)
    return gate * (1.0 + y * (1.0 - gate))


def rows_per_step(rows):
    for step in (6, 4, 3, 2):
        if rows % step == 0:
            return step
    return 1


def pack_vectors(out_ref, first, second, more=None):
    more = jnp.zeros((4, 128), F32) if more is None else more
    tile = jnp.concatenate([first[:, :128], first[:, 128:], second[:, :128], second[:, 128:], more], axis=0)
    out_ref[:, :8] = jnp.broadcast_to(tile[None], (out_ref.shape[0], 8, 128))


def as_rows(columns):
    channels = columns[0].shape[0]
    lane = lax.broadcasted_iota(jnp.int32, (channels, 128), 1)
    block = jnp.zeros((channels, 128), F32)
    for i, column in enumerate(columns):
        block = jnp.where(lane == i, column, block)
    turned = block.T
    if channels < 256:
        turned = jnp.concatenate([turned, jnp.zeros((128, 256 - channels), F32)], axis=1)
    return [turned[i : i + 1] for i in range(len(columns))]


def as_columns(rows, channels):
    block = jnp.concatenate(rows + [jnp.zeros((8 - len(rows), rows[0].shape[1]), F32)], axis=0)
    turned = block.T
    return [turned[:channels, i : i + 1] for i in range(len(rows))]


def told_vectors(told):
    return jnp.concatenate([told[:, 0], told[:, 1]], axis=1), jnp.concatenate([told[:, 2], told[:, 3]], axis=1)


def merged(told, counts, inverse):
    means, spreads = told_vectors(told)
    mean = jnp.sum(means * counts, axis=0, keepdims=True) * inverse
    away = means - mean
    var = jnp.sum(spreads + counts * (away * away), axis=0, keepdims=True) * inverse
    return mean, lax.rsqrt(var + EPSILON)


def norm_columns(told_ref, counts_ref, inverse, gain_rows, channels, first=0):
    mean, scale = merged(told_ref[:, first : first + 4], counts_ref[...], inverse)
    return as_columns([mean, scale, gain_rows[0:1], gain_rows[1:2]], channels)


def sums_columns(told_ref, channels):
    first, second = told_vectors(told_ref[...])
    return as_columns([jnp.sum(first, axis=0, keepdims=True), jnp.sum(second, axis=0, keepdims=True)], channels)


def normed_of(pre, cols):
    return (pre - cols[0]) * cols[1]


def activation(pre, cols, valid):
    y = cols[2] * normed_of(pre, cols) + cols[3]
    return (y * jax.nn.sigmoid(y) * valid).astype(BF)


def fold(x):
    total = x[:, :128]
    for at in range(128, x.shape[1], 128):
        total = total + x[:, at : at + 128]
    return total


def moments_step(v, valid, state_ref, first):
    @pl.when(first)
    def _():
        count = jnp.maximum(jnp.sum(valid), 1.0)
        state_ref[0] = jnp.broadcast_to(jnp.sum(v * valid, axis=1, keepdims=True) / count, state_ref.shape[1:])
        state_ref[1] = jnp.zeros(state_ref.shape[1:], F32)
        state_ref[2] = jnp.zeros(state_ref.shape[1:], F32)

    away = (v - state_ref[0, :, 0:1]) * valid
    state_ref[1] += fold(away)
    state_ref[2] += fold(away * away)


def moments_end(state_ref, count, out_ref):
    total = jnp.sum(state_ref[1], axis=1, keepdims=True)
    squares = jnp.sum(state_ref[2], axis=1, keepdims=True)
    mean = state_ref[0, :, 0:1] + total / count
    pack_vectors(out_ref, *as_rows([mean, squares - total * total / count]))


def sums_step(dy, normed, state_ref, first):
    @pl.when(first)
    def _():
        state_ref[...] = jnp.zeros_like(state_ref)

    state_ref[0] += fold(dy)
    state_ref[1] += fold(dy * normed)


def sums_end(state_ref, out_ref):
    pack_vectors(out_ref, *as_rows([jnp.sum(state_ref[i], axis=1, keepdims=True) for i in range(2)]))


def ext_parts(rows_ext, piece):
    own = rows_ext * WF - 2 * WF
    yield 0, slice(0, WF), slice(0, WF)
    for start, size in tiles(own, piece):
        yield 1, slice(start, start + size), slice(WF + start, WF + start + size)
    yield 2, slice(0, WF), slice(WF + own, 2 * WF + own)


def stacked(a_ref, start, lanes, mask_ref, flip, rows):
    first, last = (1, 0) if flip else (0, 1)
    before = a_ref[rows, pl.ds(start, lanes)]
    middle = a_ref[rows, pl.ds(start + WF, lanes)]
    after = a_ref[rows, pl.ds(start + 2 * WF, lanes)]
    before = before * mask_ref[0:1, pl.ds(start, lanes)].astype(BF)
    after = after * mask_ref[1:2, pl.ds(start, lanes)].astype(BF)
    return [after, middle, before] if flip else [before, middle, after]


def columns_joined(acc, outs, flip):
    lanes = acc.shape[1]
    col = lax.broadcasted_iota(jnp.int32, (1, lanes), 1) % WF
    left, right = (acc[2 * outs :], acc[:outs]) if flip else (acc[:outs], acc[2 * outs :])
    left = jnp.where(col > 0, pltpu.roll(left, 1, 1), 0.0)
    right = jnp.where(col < WF - 1, pltpu.roll(right, lanes - 1, 1), 0.0)
    return acc[outs : 2 * outs] + left + right


def forward_weights(w_ref, up, out_ref):
    devices, _, outs, cin = w_ref.shape
    wide, extra = devices * outs, cin - up
    for c in range(devices):
        for b in range(3):
            rows = slice(b * wide + c * outs, b * wide + (c + 1) * outs)
            for a in range(3):
                piece = w_ref[c, 3 * a + b]
                out_ref[rows, a * up : (a + 1) * up] = piece[:, :up]
                if extra:
                    at = 3 * up + a * extra
                    out_ref[rows, at : at + extra] = piece[:, up:]


def backward_weights(w_ref, up, out_ref):
    devices, _, outs, cin = w_ref.shape
    wide, extra = devices * outs, cin - up
    for a in range(3):
        for b in range(3):
            whole = jnp.concatenate([w_ref[c, 3 * a + b] for c in range(devices)], axis=0).astype(F32)
            columns = slice(a * wide, (a + 1) * wide)
            out_ref[b * up : (b + 1) * up, columns] = whole[:, :up].T.astype(BF)
            if extra:
                tail = jnp.concatenate([whole[:, up:], jnp.zeros((wide, 128 - extra), F32)], axis=1).T
                at = 3 * up + b * extra
                out_ref[at : at + extra, columns] = tail[:extra].astype(BF)


def first_kernel(
    lanes,
    proj_prev, proj_own, proj_next, told_proj, counts_c, proj_gain, window_valid,
    enlarge, low_prev, low_own, low_next, told_low, counts_f, low_gain, valid_ext, mask, w_all, scalars,
    a_ref, out_ref, top_ref, bottom_ref, stats_ref, coarse_ref, w_ref, state_ref,
):
    step, last = pl.program_id(0), pl.num_programs(0) - 1
    up = proj_own.shape[0]
    margin, share = proj_prev.shape[1], proj_own.shape[1]

    @pl.when(step == 0)
    def _():
        forward_weights(w_all, up, w_ref)
        cols = norm_columns(told_proj, counts_c, scalars[0], proj_gain, up)
        for ref, start in ((proj_prev, 0), (proj_own, margin), (proj_next, margin + share)):
            part = slice(start, start + ref.shape[1])
            coarse_ref[:, part] = activation(ref[...], cols, window_valid[:, part])
        ext = a_ref.shape[1]
        for start, size in tiles(ext, 512):
            a_ref[:up, start : start + size] = dot(coarse_ref[...], enlarge[:, start : start + size]).astype(BF)
        cols = norm_columns(told_low, counts_f, scalars[1], low_gain, LOWC, 4)
        for which, part, there in ext_parts(ext // WF, 1536):
            a_ref[up:, there] = activation((low_prev, low_own, low_next)[which][:, part], cols, valid_ext[:, there])

    start = pl.multiple_of(step * lanes, 128)
    taps = stacked(a_ref, start, lanes, mask, False, slice(0, up)) + stacked(a_ref, start, lanes, mask, False, slice(up, up + LOWC))
    acc = dot(w_ref[...], jnp.concatenate(taps, axis=0))
    conv_end(acc, False, step, last, start, lanes, valid_ext, out_ref, top_ref, bottom_ref, stats_ref, state_ref)


def conv_end(acc, flip, step, last, start, lanes, valid_ext, out_ref, top_ref, bottom_ref, stats_ref, state_ref):
    outs = out_ref.shape[0]
    v = columns_joined(acc, outs, flip)
    out_ref[...] = v
    moments_step(v, valid_ext[:, pl.ds(start + WF, lanes)], state_ref, step == 0)

    @pl.when(step == 0)
    def _():
        top_ref[...] = v[:, :WF]

    @pl.when(step == last)
    def _():
        bottom_ref[...] = v[:, lanes - WF :]
        count = jnp.maximum(jnp.sum(valid_ext[:, WF : valid_ext.shape[1] - WF]), 1.0)
        moments_end(state_ref, count, stats_ref)


def second_kernel(
    lanes, prev, own, after, told, counts, gain, valid_ext, mask, w_all, scalars,
    a_ref, out_ref, top_ref, bottom_ref, stats_ref, w_ref, state_ref,
):
    step, last = pl.program_id(0), pl.num_programs(0) - 1

    @pl.when(step == 0)
    def _():
        forward_weights(w_all, w_all.shape[3], w_ref)
        cols = norm_columns(told, counts, scalars[1], gain, a_ref.shape[0])
        for which, part, there in ext_parts(a_ref.shape[1] // WF, 768):
            a_ref[:, there] = activation((prev, own, after)[which][:, part], cols, valid_ext[:, there])

    start = pl.multiple_of(step * lanes, 128)
    taps = stacked(a_ref, start, lanes, mask, False, slice(None))
    acc = dot(w_ref[...], jnp.concatenate(taps, axis=0))
    conv_end(acc, False, step, last, start, lanes, valid_ext, out_ref, top_ref, bottom_ref, stats_ref, state_ref)


def class_kernel(
    pre, cotangent, valid, told, counts, gain, w_cls, w_turned, bias, scalars,
    logits_ref, weights_ref, bias_ref, sums_ref, state_ref, cols_ref,
):
    step, last = pl.program_id(0), pl.num_programs(0) - 1
    classes = logits_ref.shape[0]

    @pl.when(step == 0)
    def _():
        for i, col in enumerate(norm_columns(told, counts, scalars[1], gain, pre.shape[0])):
            cols_ref[:, i : i + 1] = col
        weights_ref[...] = jnp.zeros_like(weights_ref)
        bias_ref[...] = jnp.zeros_like(bias_ref)

    cols = [cols_ref[:, i : i + 1] for i in range(4)]
    normed = normed_of(pre[...], cols)
    y = cols[2] * normed + cols[3]
    gate = jax.nn.sigmoid(y)
    act = (y * gate * valid[...]).astype(BF)
    logits_ref[...] = (dot(w_cls[...], act) + bias[...])[:classes]
    weights_ref[...] += dot_nt(cotangent[...], act)
    bias_ref[...] += fold(cotangent[...].astype(F32))
    d = dot(w_turned[...], cotangent[...]).astype(BF).astype(F32)
    dy = d * (gate * (1.0 + y * (1.0 - gate)) * valid[...])
    sums_step(dy, normed, state_ref, step == 0)

    @pl.when(step == last)
    def _():
        sums_end(state_ref, sums_ref)


def back_dz(dy, normed, cols, sums, valid, inverse):
    return ((cols[1] * cols[2]) * (dy - (sums[0] + normed * sums[1]) * (valid * inverse))).astype(BF)


def second_back_kernel(
    lanes,
    prev, own, after, told, counts, gain, sums, cot_prev, cot_own, cot_after, w_turned, valid_ext, mask, w_all,
    first_pre, told_first, gain_first, riders, scalars,
    dz_ref, dy_ref, top_ref, bottom_ref, sums_ref, w_ref, state_ref, cols_ref,
):
    step, last = pl.program_id(0), pl.num_programs(0) - 1

    @pl.when(step == 0)
    def _():
        backward_weights(w_all, w_all.shape[3], w_ref)
        channels = dz_ref.shape[0]
        cols = norm_columns(told, counts, scalars[1], gain, channels)
        totals = sums_columns(sums, channels)
        for which, part, there in ext_parts(dz_ref.shape[1] // WF, 768):
            pre, cot = ((prev, cot_prev), (own, cot_own), (after, cot_after))[which]
            normed = normed_of(pre[:, part], cols)
            valid = valid_ext[:, there]
            d = dot(w_turned[...], cot[:, part]).astype(BF).astype(F32)
            dy = d * silu_slope(cols[2] * normed + cols[3]) * valid
            dz_ref[:, there] = back_dz(dy, normed, cols, totals, valid, scalars[1])
        for i, col in enumerate(norm_columns(told_first, counts, scalars[1], gain_first, channels)):
            cols_ref[:, i : i + 1] = col

    start = pl.multiple_of(step * lanes, 128)
    taps = stacked(dz_ref, start, lanes, mask, True, slice(None))
    acc = dot(w_ref[...], jnp.concatenate(taps, axis=0))
    grad = columns_joined(acc, dy_ref.shape[0], True)
    cols = [cols_ref[:, i : i + 1] for i in range(4)]
    normed = normed_of(first_pre[...], cols)
    dy = grad * silu_slope(cols[2] * normed + cols[3]) * valid_ext[:, pl.ds(start + WF, lanes)]
    dy_ref[...] = dy
    sums_step(dy, normed, state_ref, step == 0)

    @pl.when(step == 0)
    def _():
        top_ref[...] = dy[:, :WF]

    @pl.when(step == last)
    def _():
        bottom_ref[...] = dy[:, lanes - WF :]
        sums_end(state_ref, sums_ref)
        sums_ref[:, 8:] = riders[...]


def first_back_kernel(
    lanes,
    prev, own, after, dy_prev, dy_own, dy_after, told, counts, gain, sums, valid_ext, mask, w_all,
    enlarge, low_pre, told_low, low_gain, scalars,
    dz_ref, window_ref, low_ref, low_sums_ref, w_ref, state_ref, cols_ref,
):
    step, last = pl.program_id(0), pl.num_programs(0) - 1
    up = window_ref.shape[0]

    @pl.when(step == 0)
    def _():
        backward_weights(w_all, up, w_ref)
        channels = dz_ref.shape[0]
        cols = norm_columns(told, counts, scalars[1], gain, channels)
        totals = sums_columns(sums, channels)
        for which, part, there in ext_parts(dz_ref.shape[1] // WF, 768):
            pre, dy = ((prev, dy_prev), (own, dy_own), (after, dy_after))[which]
            normed = normed_of(pre[:, part], cols)
            dz_ref[:, there] = back_dz(dy[:, part], normed, cols, totals, valid_ext[:, there], scalars[1])
        for i, col in enumerate(norm_columns(told_low, counts, scalars[1], low_gain, LOWC, 4)):
            cols_ref[:, i : i + 1] = col
        window_ref[...] = jnp.zeros_like(window_ref)

    start = pl.multiple_of(step * lanes, 128)
    taps = stacked(dz_ref, start, lanes, mask, True, slice(None))
    acc = dot(w_ref[...], jnp.concatenate(taps, axis=0))
    grad = columns_joined(acc[: 3 * up], up, True)
    high = grad.astype(BF)
    rest = (grad - high.astype(F32)).astype(BF)
    part = enlarge[:, pl.ds(start + WF, lanes)]
    window_ref[...] += dot_nt(high, part) + dot_nt(rest, part)
    cols = [cols_ref[:, i : i + 1] for i in range(4)]
    normed = normed_of(low_pre[...], cols)
    dy = columns_joined(acc[3 * up :], LOWC, True)
    dy = dy * silu_slope(cols[2] * normed + cols[3]) * valid_ext[:, pl.ds(start + WF, lanes)]
    low_ref[...] = dy
    sums_step(dy, normed, state_ref, step == 0)

    @pl.when(step == last)
    def _():
        for i in range(2):
            low_sums_ref[i : i + 1] = as_rows([jnp.sum(state_ref[i], axis=1, keepdims=True)])[0]


def decoder_weight_kernel(lanes, outs, dz_ref, a_ref, mask_ref, *refs):
    step = pl.program_id(0)
    start = pl.multiple_of(step * lanes, 128)
    acc_ref = refs[-1]
    wide = dz_ref.shape[0]
    up, extra = wide, a_ref.shape[0] - wide

    @pl.when(step == 0)
    def _():
        acc_ref[...] = jnp.zeros_like(acc_ref)

    taps = stacked(a_ref, start, lanes, mask_ref, False, slice(0, up))
    if a_ref.shape[0] > up:
        taps = taps + stacked(a_ref, start, lanes, mask_ref, False, slice(up, None))
    dz = dz_ref[:, pl.ds(start + WF, lanes)]
    col = lax.broadcasted_iota(jnp.int32, (1, lanes), 1) % WF
    left = pltpu.roll(dz, lanes - 1, 1) * (col < WF - 1).astype(F32).astype(BF)
    right = pltpu.roll(dz, 1, 1) * (col > 0).astype(F32).astype(BF)
    acc_ref[...] += dot_nt(jnp.concatenate([left, dz, right], axis=0), jnp.concatenate(taps, axis=0))

    @pl.when(step == pl.num_programs(0) - 1)
    def _():
        for c in range(wide // outs):
            for b in range(3):
                rows = slice(b * wide + c * outs, b * wide + (c + 1) * outs)
                for a in range(3):
                    refs[0][c, 3 * a + b, :, :up] = acc_ref[rows, a * up : (a + 1) * up].astype(BF)
                    if extra:
                        at = 3 * up + a * extra
                        refs[0][c, 3 * a + b, :, up:] = acc_ref[rows, at : at + extra].astype(BF)


def decoder_weight_grad(dz, a, masks, outs):
    wide, pixels = dz.shape[0], dz.shape[1] - 2 * WF
    cin = a.shape[0]
    lanes = WF * rows_per_step(pixels // WF)
    devices = wide // outs
    whole = pl.BlockSpec(memory_space=pltpu.VMEM)
    return pl.pallas_call(
        lambda *refs: decoder_weight_kernel(lanes, outs, *refs),
        grid=(pixels // lanes,),
        in_specs=[whole] * 3,
        out_specs=whole,
        out_shape=jax.ShapeDtypeStruct((devices, 9, outs, cin), BF),
        scratch_shapes=[pltpu.VMEM((3 * wide, 3 * cin), F32)],
        compiler_params=params(),
        cost_estimate=BRIEF,
    )(dz, a, masks)


def decoder_call(kernel, operands, blocked, smem, outputs, blocked_out, scratch, pixels, flops):
    lanes = WF * rows_per_step(pixels // WF)
    whole = pl.BlockSpec(memory_space=pltpu.VMEM)
    run = lambda channels: pl.BlockSpec((channels, lanes), lambda i: (0, i))
    in_specs = [
        pl.BlockSpec(memory_space=pltpu.SMEM) if i in smem else run(v.shape[0]) if i in blocked else whole
        for i, v in enumerate(operands)
    ]
    out_specs = [run(v.shape[0]) if i in blocked_out else whole for i, v in enumerate(outputs)]
    return pl.pallas_call(
        kernel,
        grid=(pixels // lanes,),
        in_specs=in_specs,
        out_specs=out_specs,
        out_shape=outputs,
        scratch_shapes=scratch,
        compiler_params=params(),
        cost_estimate=BRIEF,
    )(*operands)


def branch_kernel(centre, from_next, from_prev, valid, out_ref, pieces_ref, stats_ref):
    outs, pixels = centre.shape[1:]
    devices, _, share = pieces_ref.shape
    count = jnp.maximum(jnp.sum(valid[...]), 1.0)
    means, spreads = [], []
    for k in range(4):
        rows = slice(k * outs, (k + 1) * outs)
        v = centre[(k + 3) % 4]
        if k:
            v = v + jnp.concatenate([jnp.zeros((outs, pixels - PAD), F32), from_next[k - 1].astype(F32)], axis=1)
            v = v + jnp.concatenate([from_prev[k - 1].astype(F32), jnp.zeros((outs, pixels - PAD), F32)], axis=1)
        mean = jnp.sum(v * valid[...], axis=1, keepdims=True) / count
        v = (v - mean) * valid[...]
        means.append(mean)
        spreads.append(jnp.sum(v * v, axis=1, keepdims=True))
        out_ref[rows] = v.astype(BF)
        for i in range(devices):
            pieces_ref[i, rows] = v[:, i * share : (i + 1) * share].astype(BF)
    pack_vectors(stats_ref, *as_rows([jnp.concatenate(means, axis=0), jnp.concatenate(spreads, axis=0)]))


def parameter_kernel(
    depth, told_ref, w_pool_ref, w_proj_ref, area_ref, branch_ref, proj_ref, first_ref, second_ref, low_ref, pooled_ref
):
    devices, rows, _ = told_ref.shape
    _, taps, outs, wide = w_pool_ref.shape
    low_share = LOWC // devices
    proj_ref[...] = jnp.zeros_like(proj_ref)
    low_ref[...] = jnp.zeros_like(low_ref)
    branch_ref[...] = jnp.zeros_like(branch_ref)

    def over(row, place):
        pieces = [told_ref[c, row : row + 1, depth + place * outs : depth + (place + 1) * outs] for c in range(devices)]
        return jnp.concatenate(pieces, axis=1)

    for c in range(devices):
        for i in range(2):
            branch_ref[c, i : i + 1, : 4 * outs] = told_ref[c, i : i + 1, depth : depth + 4 * outs]
            at = depth + 128 * i
            low_ref[i : i + 1, c * low_share : (c + 1) * low_share] = told_ref[c, 4:5, at : at + low_share]
    for i in range(2):
        proj_ref[i : i + 1] = over(2, 1 + 2 * i)
        first_ref[i : i + 1] = over(3, 2 * i)
        second_ref[i : i + 1] = over(3, 1 + 2 * i)
    gain, shift = over(2, 0), over(2, 2)
    pre = jnp.zeros((rows, wide), F32)
    means = []
    for c in range(devices):
        means.append((told_ref[c, :, :depth] / area_ref[...]).astype(BF))
    means = jnp.concatenate(means, axis=1)
    for k in range(taps):
        part = means[:, k * wide : (k + 1) * wide]
        pre = pre + jnp.concatenate([dot_nt(part, w_pool_ref[c, k]) for c in range(devices)], axis=1)
    number = iota((rows, 1), 0)
    real = jnp.where(number < pooled_ref.shape[2], 1.0, 0.0)
    images = pooled_ref.shape[2]
    mean = jnp.sum(pre * real, axis=0, keepdims=True) / images
    var = jnp.sum(pre * pre * real, axis=0, keepdims=True) / images - mean * mean
    y = gain * ((pre - mean) * lax.rsqrt(var + EPSILON)) + shift
    act = (y * jax.nn.sigmoid(y)).astype(BF)
    pooled_ref[0] = dot_nt(w_proj_ref[...], act)[:, :images]


def project_kernel(
    swapped, told, counts, gains, w_ref, broad, member, valid, low_ref, valid_fine, scalars, places, out_ref, left_ref, right_ref, stats_ref
):
    devices, four, share = swapped.shape
    groups = told.shape[0]
    margin = left_ref.shape[1]
    mine = places[0]
    number = lax.broadcasted_iota(jnp.int32, (groups, 1), 0)
    total = jnp.zeros(out_ref.shape, F32)
    for i in range(broad.shape[2]):
        total = total + broad[0, :, i : i + 1] * member[i : i + 1]
    for j in range(devices):
        c = places[1 + j]
        group = told[:, c]
        mean, scale = merged(group, counts[...], scalars[0])
        here = jnp.sum(jnp.where(number == mine, told_vectors(group)[0], 0.0), axis=0, keepdims=True)
        cols = as_columns([mean - here, scale, gains[c, 0:1], gains[c, 1:2]], four)
        total = total + dot(w_ref[c], activation(swapped[j].astype(F32), cols, valid[...]))
    out_ref[...] = total
    left_ref[...] = total[:, :margin]
    right_ref[...] = total[:, share - margin :]
    count = jnp.maximum(jnp.sum(valid[...]), 1.0)
    mean = jnp.sum(total * valid[...], axis=1, keepdims=True) / count
    away = (total - mean) * valid[...]
    rows = as_rows([mean, jnp.sum(away * away, axis=1, keepdims=True)])
    low_count = jnp.maximum(jnp.sum(valid_fine[...]), 1.0)
    low_mean = jnp.sum(low_ref[...] * valid_fine[...], axis=1, keepdims=True) / low_count
    away = (low_ref[...] - low_mean) * valid_fine[...]
    low_rows = as_rows([low_mean, jnp.sum(away * away, axis=1, keepdims=True)])
    more = [part for row in low_rows for part in (row[:, :128], row[:, 128:])]
    pack_vectors(stats_ref, *rows, jnp.concatenate(more, axis=0))


def small_call(kernel, operands, smem, outputs, flops):
    whole = pl.BlockSpec(memory_space=pltpu.VMEM)
    return pl.pallas_call(
        kernel,
        in_specs=[pl.BlockSpec(memory_space=pltpu.SMEM) if i in smem else whole for i in range(len(operands))],
        out_specs=[whole] * len(outputs),
        out_shape=outputs,
        compiler_params=params(),
        cost_estimate=pl.CostEstimate(flops=flops, bytes_accessed=4000000, transcendentals=0),
    )(*operands)


def pyramid_kernel(blocks, outs, perm_ref, *refs):
    x_refs = refs[:blocks]
    w_ref, w_one_ref, mask_ref, centre_ref, up_ref, down_ref, acc_ref = refs[blocks:]
    k = pl.program_id(0)
    rate = 6 * (k + 1)
    depth, pixels = x_refs[0].shape

    def product(weights, width):
        for start, size in tiles(pixels, 512):
            total = None
            for j in range(blocks):
                at = pl.multiple_of(perm_ref[j] * depth, depth)
                part = dot(weights(at, depth), x_refs[j][:, start : start + size])
                total = part if total is None else total + part
            acc_ref[:width, start : start + size] = total

    @pl.when(k == 3)
    def _():
        product(lambda at, n: w_one_ref[:, pl.ds(at, n)], outs)
        centre_ref[0] = acc_ref[:outs]

    @pl.when(k < 3)
    def _():
        product(lambda at, n: w_ref[0, :, pl.ds(at, n)], 9 * outs)
        lane = lax.broadcasted_iota(jnp.int32, (1, pixels), 1)
        col, row = lane % WS, lane // WS
        for a in (0, 1, -1):
            tap = 3 * (a + 1) * outs
            left = pltpu.roll(acc_ref[tap : tap + outs], rate, 1)
            right = pltpu.roll(acc_ref[tap + 2 * outs : tap + 3 * outs], pixels - rate, 1)
            part = acc_ref[tap + outs : tap + 2 * outs] + jnp.where(col >= rate, left, 0.0) + jnp.where(col < WS - rate, right, 0.0)
            if a == 0:
                centre_ref[0] = part
                continue
            part = part * mask_ref[pl.ds(2 * k + (a + 1) // 2, 1)]
            if a == 1:
                moved = pltpu.roll(part, pixels - WS * rate, 1)
                inside = row < pixels // WS - rate
                up_ref[0] = jnp.where(inside, 0.0, moved)[:, pixels - PAD :].astype(BF)
            else:
                moved = pltpu.roll(part, WS * rate, 1)
                inside = row >= rate
                down_ref[0] = jnp.where(inside, 0.0, moved)[:, :PAD].astype(BF)
            centre_ref[0] += jnp.where(inside, moved, 0.0)


def pyramid(x_blocks, perm, w_taps, w_one, masks):
    depth, pixels = x_blocks[0].shape
    outs, cin = w_one.shape
    whole = pl.BlockSpec(memory_space=pltpu.VMEM)
    third = lambda k, p: (jnp.minimum(k, 2), 0, 0)
    return pl.pallas_call(
        lambda *refs: pyramid_kernel(len(x_blocks), outs, *refs),
        grid_spec=pltpu.PrefetchScalarGridSpec(
            num_scalar_prefetch=1,
            grid=(4,),
            in_specs=[whole] * len(x_blocks)
            + [pl.BlockSpec((1, 9 * outs, cin), third), whole, whole],
            out_specs=[
                pl.BlockSpec((1, outs, pixels), lambda k, p: (k, 0, 0)),
                pl.BlockSpec((1, outs, PAD), third),
                pl.BlockSpec((1, outs, PAD), third),
            ],
            scratch_shapes=[pltpu.VMEM((9 * outs, pixels), F32)],
        ),
        out_shape=[
            jax.ShapeDtypeStruct((4, outs, pixels), F32),
            jax.ShapeDtypeStruct((3, outs, PAD), BF),
            jax.ShapeDtypeStruct((3, outs, PAD), BF),
        ],
        compiler_params=params(),
        cost_estimate=pl.CostEstimate(flops=2 * 28 * outs * cin * pixels, bytes_accessed=2 * (28 * outs + pixels) * cin, transcendentals=0),
    )(perm, *x_blocks, w_taps, w_one, masks)


def shifted_taps(read, lanes, rate, masks, store):
    col = lax.broadcasted_iota(jnp.int32, (1, lanes), 1) % WS
    for a in (-1, 0, 1):
        for b in (-1, 0, 1):
            shift = rate * (WS * a + b)
            first = (PAD - shift) // 128 * 128
            rest = PAD - shift - first
            window = read(first, lanes + 128)
            if rest:
                window = pltpu.roll(window, lanes + 128 - rest, 1)
            keep = ((col - b * rate >= 0) & (col - b * rate < WS)).astype(F32)
            if a:
                keep = keep * masks[(a + 1) // 2]
            store(3 * (a + 1) + b + 1, window[:, :lanes] * keep.astype(BF))


def dot_tn(a, b):
    return lax.dot_general(a, b, (((0,), (0,)), ((), ())), preferred_element_type=F32)


def input_grad_kernel(outs, dz_ref, spread_ref, mask_ref, w_ref, one_ref, pool_ref, out_ref, taps_ref):
    pixels = spread_ref.shape[1]

    @pl.when(pl.program_id(0) == 0)
    def _():
        for k in range(3):
            def store(tap, value, k=k):
                at = (9 * k + tap) * outs
                taps_ref[at : at + outs] = value

            masks = (mask_ref[2 * k : 2 * k + 1], mask_ref[2 * k + 1 : 2 * k + 2])
            rows = (k + 1) * outs
            shifted_taps(lambda first, n: dz_ref[rows : rows + outs, first : first + n], pixels, 6 * (k + 1), masks, store)
        taps_ref[27 * outs : 28 * outs] = dz_ref[:outs, PAD : PAD + pixels]
        taps_ref[28 * outs :] = spread_ref[...]

    weights = jnp.concatenate([w_ref[...], one_ref[...], pool_ref[...]], axis=0)
    for start, size in tiles(pixels, 512):
        out_ref[0, :, start : start + size] = dot_tn(weights, taps_ref[:, start : start + size]).astype(BF)


def input_grad(dz, spread, masks, w_taps, w_one, w_pool, perm):
    pixels = spread.shape[1]
    outs, cin = w_one.shape
    blocks = perm.shape[0]
    depth = cin // blocks
    whole = pl.BlockSpec(memory_space=pltpu.VMEM)
    slab = lambda rows: pl.BlockSpec((rows, depth), lambda i, p: (0, p[i]))

    def kernel(perm_ref, *refs):
        input_grad_kernel(outs, *refs)

    return pl.pallas_call(
        kernel,
        grid_spec=pltpu.PrefetchScalarGridSpec(
            num_scalar_prefetch=1,
            grid=(blocks,),
            in_specs=[whole, whole, whole, slab(27 * outs), slab(outs), slab(outs)],
            out_specs=pl.BlockSpec((1, depth, pixels), lambda i, p: (i, 0, 0)),
            scratch_shapes=[pltpu.VMEM((29 * outs, pixels), BF)],
        ),
        out_shape=jax.ShapeDtypeStruct((blocks, depth, pixels), BF),
        compiler_params=params(),
        cost_estimate=BRIEF,
    )(perm, dz, spread, masks, w_taps.reshape(27 * outs, cin), w_one, w_pool)


def pyramid_weight_kernel(lanes, outs, branches, plain, dz_ref, mask_ref, *refs):
    x_refs, (out_ref, taps_ref, acc_ref) = refs[:-3], refs[-3:]
    step = pl.program_id(0)
    start = pl.multiple_of(step * lanes, 128)

    @pl.when(step == 0)
    def _():
        acc_ref[...] = jnp.zeros_like(acc_ref)

    for n, k in enumerate(branches):
        def store(tap, value, n=n):
            at = (9 * n + tap) * outs
            taps_ref[at : at + outs] = value

        rows = slice((k + 1) * outs, (k + 2) * outs)
        masks = (mask_ref[0, 2 * k : 2 * k + 1], mask_ref[0, 2 * k + 1 : 2 * k + 2])
        shifted_taps(lambda first, n, rows=rows: dz_ref[rows, pl.ds(start + first, n)], lanes, 6 * (k + 1), masks, store)
    if plain:
        taps_ref[9 * len(branches) * outs :] = dz_ref[:outs, pl.ds(start + PAD, lanes)]
    acc_ref[...] += dot_nt(taps_ref[...], jnp.concatenate([x[0, 0] for x in x_refs], axis=0))

    @pl.when(step == pl.num_programs(0) - 1)
    def _():
        rows = 9 * len(branches) * outs
        out_ref[:rows] = acc_ref[:rows].astype(BF)
        spare = out_ref.shape[0] - acc_ref.shape[0]
        if spare:
            out_ref[rows : rows + spare] = jnp.zeros((spare, out_ref.shape[1]), BF)
        if plain:
            out_ref[rows + spare :] = acc_ref[rows:].astype(BF)


def pyramid_weight_grad(dz, x, masks, branches, plain, spare=0):
    devices, groups, slim, lanes = x.shape
    outs, canvas = dz.shape[0] // 4, groups * lanes
    channels = slim * devices
    out_rows = (9 * len(branches) + plain) * outs
    whole = pl.BlockSpec(memory_space=pltpu.VMEM)
    block = lambda j: pl.BlockSpec((1, 1, slim, lanes), lambda i: (j, i, 0, 0))
    return pl.pallas_call(
        lambda *refs: pyramid_weight_kernel(lanes, outs, branches, plain, *refs),
        grid=(groups,),
        in_specs=[whole, pl.BlockSpec((1, 8, lanes), lambda i: (i, 0, 0))] + [block(j) for j in range(devices)],
        out_specs=whole,
        out_shape=jax.ShapeDtypeStruct((out_rows + spare, channels), BF),
        scratch_shapes=[pltpu.VMEM((out_rows, lanes), BF), pltpu.VMEM((out_rows, channels), F32)],
        compiler_params=params(),
        cost_estimate=pl.CostEstimate(flops=2 * out_rows * channels * canvas, bytes_accessed=2 * (4 * outs + channels) * canvas, transcendentals=0),
    )(dz, masks, *([x] * devices))


def slope_kernel(first, centred_ref, valid_ref, cols_ref, offset_ref, slope_ref, act_ref):
    lane = iota(offset_ref.shape, 1)
    gain, shift, scale, mean = (cols_ref[:, i : i + 1] for i in range(4))
    group = first + pl.program_id(0)
    offset = jnp.sum(jnp.where(lane == group, offset_ref[...], 0.0), axis=1, keepdims=True) - mean
    slant, level = gain * scale, gain * scale * offset + shift
    y = centred_ref[0].astype(F32) * slant + level
    gate = 0.5 + 0.5 * jnp.tanh(0.5 * y)
    valid = valid_ref[0, 6:7]
    through = gate * valid
    act_ref[0] = (y * through).astype(BF)
    slope_ref[0] = (through * (1.0 + y * (1.0 - gate))).astype(BF)


def slopes(first, number, centred, canvas_rows, cols, offsets, into=None):
    groups, four, pixels = centred.shape
    whole = pl.BlockSpec(memory_space=pltpu.VMEM)
    take = lambda rows: pl.BlockSpec((1, rows, pixels), lambda i: (first + i, 0, 0))
    shape = jax.ShapeDtypeStruct((groups, four, pixels), BF)
    operands = [centred, canvas_rows, cols, offsets]
    in_specs = [take(four), take(8), whole, whole]
    aliases = {}
    if into is not None:
        aliases = {4: 0, 5: 1}
        operands += into
        in_specs += [pl.BlockSpec(memory_space=pl.ANY)] * 2
    return pl.pallas_call(
        lambda *refs: slope_kernel(first, *refs[:4], *refs[-2:]),
        grid=(number,),
        in_specs=in_specs,
        out_specs=[take(four), take(four)],
        out_shape=[shape, shape],
        input_output_aliases=aliases,
        compiler_params=params(),
        cost_estimate=BRIEF,
    )(*operands)


def canvas_kernel(groups, devices, *refs):
    dz_refs, refs = refs[:devices], refs[devices:]
    centred_ref, slope_ref, rows_ref, member_ref, w_ref, cols_ref, offset_ref, count = refs[:8]
    dz_ref, proj_ref, sums_ref, image_ref, pieces_ref, dy_ref = refs[8:]
    step = pl.program_id(0)
    four, pixels = centred_ref.shape[1:]
    share = dz_refs[0].shape[2]
    group = jnp.where(step < groups, step, step - groups)
    gain, scale, mean = (cols_ref[:, i : i + 1] for i in (0, 2, 3))
    offset = jnp.sum(jnp.where(iota(offset_ref.shape, 1) == group, offset_ref[...], 0.0), axis=1, keepdims=True) - mean
    level = offset * scale
    valid = rows_ref[0, 6:7]
    at = pl.multiple_of(group * pixels, 128)

    @pl.when(step == 0)
    def _():
        sums_ref[...] = jnp.zeros_like(sums_ref)
        image_ref[...] = jnp.zeros_like(image_ref)
        dz_ref[:, :PAD] = jnp.zeros((four, PAD), BF)
        dz_ref[:, PAD + groups * pixels :] = jnp.zeros((four, PAD), BF)

    @pl.when(step < groups)
    def _():
        for i in range(devices):
            pieces_ref[:, i * share : (i + 1) * share] = dz_refs[i][0]
        proj_ref[0] = pieces_ref[...]
        image_ref[...] += dot_nt(pieces_ref[...], member_ref[0].astype(BF))
        total = jnp.zeros((four, 128), F32)
        total_normed = jnp.zeros((four, 128), F32)
        for start, size in tiles(pixels, 512):
            part = slice(start, start + size)
            dy = dot(w_ref[...], pieces_ref[:, part]) * slope_ref[0, :, part].astype(F32)
            dy_ref[:, pl.ds(at + start, size)] = dy
            total = total + fold(dy)
            total_normed = total_normed + fold(dy * (centred_ref[0, :, part].astype(F32) * scale + level))
        sums_ref[:, 0:1] += jnp.sum(total, axis=1, keepdims=True)
        sums_ref[:, 1:2] += jnp.sum(total_normed, axis=1, keepdims=True)

    @pl.when(step >= groups)
    def _():
        steep = scale * gain
        rise = steep * count[0] * sums_ref[:, 1:2] * scale
        constant = steep * count[0] * (sums_ref[:, 0:1] + level * sums_ref[:, 1:2])
        parts = centred_ref[0].astype(F32) * rise + constant
        dz_ref[:, pl.ds(PAD + at, pixels)] = (steep * dy_ref[:, pl.ds(at, pixels)] - valid * parts).astype(BF)


def canvas_grad(proj_dz, slope, centred, canvas_rows, member, w_turned, cols, offsets, scalars):
    groups, four, pixels = centred.shape
    everyone, wide, share = proj_dz.shape
    devices = everyone // groups
    ahead = lambda s: jnp.minimum(s, groups - 1)
    by_group = lambda rows: pl.BlockSpec((1, rows, pixels), lambda s: (jnp.where(s < groups, s, s - groups), 0, 0))
    near = lambda rows: pl.BlockSpec((1, rows, pixels), lambda s: (ahead(s), 0, 0))
    piece = lambda i: pl.BlockSpec((1, wide, share), lambda s: (ahead(s) * devices + i, 0, 0))
    whole = pl.BlockSpec(memory_space=pltpu.VMEM)
    return pl.pallas_call(
        lambda *refs: canvas_kernel(groups, devices, *refs),
        grid=(2 * groups,),
        in_specs=[piece(i) for i in range(devices)]
        + [by_group(four), near(four), by_group(8), near(member.shape[1]), whole, whole, whole]
        + [pl.BlockSpec(memory_space=pltpu.SMEM)],
        out_specs=[whole, near(wide), whole, whole],
        out_shape=[
            jax.ShapeDtypeStruct((four, 2 * PAD + groups * pixels), BF),
            jax.ShapeDtypeStruct((groups, wide, pixels), BF),
            jax.ShapeDtypeStruct((four, 128), F32),
            jax.ShapeDtypeStruct((wide, member.shape[1]), F32),
        ],
        scratch_shapes=[pltpu.VMEM((wide, pixels), BF), pltpu.VMEM((four, groups * pixels), F32)],
        compiler_params=params(),
        cost_estimate=pl.CostEstimate(flops=2 * wide * four * groups * pixels, bytes_accessed=8 * wide * groups * pixels, transcendentals=0),
    )(*([proj_dz] * devices), centred, slope, canvas_rows, member, w_turned, cols, offsets, scalars)


def assembly_kernel(groups, devices, order, where_ref, pieces, spare, plain, out_ref, one_ref, rest_ref):
    line = groups // 2
    cin = out_ref.shape[1]
    depth = cin // devices
    slim = depth // groups

    def fill(refs, target):
        for r in range(0, groups, 2):
            for j in range(devices):
                part = slice(j * slim, (j + 1) * slim)
                pair = jnp.concatenate([refs[r][:, part], refs[r + 1][:, part]], axis=1)
                at = j * depth + r * slim
                target[:, at : at + 2 * slim] = pair.astype(F32)

    for z in range(line):
        for e in range(2):
            chosen = [order.index(line_part(z, r // 2 - z, (r ^ e) & 1)) for r in range(groups)]

            @pl.when((where_ref[0] // 2 == z) & (where_ref[0] % 2 == e))
            def _(chosen=chosen):
                fill([pieces[i] for i in chosen], out_ref)

                @pl.when(pl.program_id(0) == 0)
                def _():
                    fill([plain[i] for i in chosen], one_ref)
                    for r, i in enumerate(chosen):
                        rest_ref[r] = spare[i][...]


def assemble(found, devices, groups, strip, outs, cin):
    order = sorted(found)
    pieces = [found[key] for key in order]
    slots, width = len(pieces), pieces[0].shape[1]
    rows, spare = 9 * outs, 3 * outs
    smem = pl.BlockSpec(memory_space=pltpu.SMEM)

    def kernel(where_ref, *refs):
        parts = [refs[i * slots : (i + 1) * slots] for i in range(3)]
        assembly_kernel(groups, devices, order, where_ref, *parts, *refs[3 * slots :])

    return pl.pallas_call(
        kernel,
        grid=(3,),
        in_specs=[smem]
        + [pl.BlockSpec((rows, width), lambda i: (i, 0))] * slots
        + [pl.BlockSpec((spare, width), lambda i: (9, 0))] * slots
        + [pl.BlockSpec((outs, width), lambda i: (30, 0))] * slots,
        out_specs=[
            pl.BlockSpec((rows, cin), lambda i: (i, 0)),
            pl.BlockSpec((outs, cin), lambda i: (0, 0)),
            pl.BlockSpec((groups, spare, width), lambda i: (0, 0, 0)),
        ],
        out_shape=[
            jax.ShapeDtypeStruct((27 * outs, cin), F32),
            jax.ShapeDtypeStruct((outs, cin), F32),
            jax.ShapeDtypeStruct((groups, spare, width), BF),
        ],
        compiler_params=params(),
        cost_estimate=pl.CostEstimate(flops=0, bytes_accessed=27 * outs * cin * 6, transcendentals=0),
    )(strip[None].astype(jnp.int32), *pieces, *pieces, *pieces)


def local(
    feats,
    lowlevel,
    heights,
    widths,
    w_one,
    w_atrous,
    w_pool,
    w_proj,
    w_low,
    w_dec1,
    w_dec2,
    w_cls,
    b_cls,
    mid_gain,
    mid_shift,
    low_gain,
    low_shift,
    dec_gain,
    dec_shift,
    cotangent,
):
    devices, groups = lax.axis_size("ch"), lax.axis_size("row")
    me, strip = lax.axis_index("ch"), lax.axis_index("row")
    place = strip * devices + me
    everyone = devices * groups
    depth, pixels = feats.shape
    rows = pixels // WS
    canvas = groups * pixels
    outs = w_one.shape[0]
    wide = outs * devices
    images = heights.shape[0]
    share = pixels // devices
    fine = 16 * share
    fine_rows = fine // WF
    margin = WS if fine_rows % 4 == 0 else 2 * WS

    area = (heights * widths).astype(F32)
    count = jnp.sum(area)
    fine_count = 16.0 * count
    scalars = jnp.stack([1.0 / count, 1.0 / fine_count])
    places = jnp.stack([strip, place]).astype(jnp.int32)
    members = -(-images // 16) * 16
    window = share + 2 * margin
    ext = fine + 2 * WF
    shaped = lambda *shape: jax.ShapeDtypeStruct(shape, F32)
    strip_rows, member_strip, valid_fine_strip = geometry_call(
        strip_geometry_kernel,
        heights, widths, places,
        [shaped(8, pixels), jax.ShapeDtypeStruct((members, pixels), BF), jax.ShapeDtypeStruct((1, 16 * pixels), BF)],
    )
    valid_strip = strip_rows[6:7]

    mine = feats * valid_strip.astype(BF)
    slice_depth = depth // groups

    line = lambda *parts: jnp.concatenate([jnp.pad(v.astype(F32), (0, size - v.shape[0])) for v, size in parts])
    rank = lambda v: line((v.astype(F32).reshape(-1), 256))
    low_share = LOWC // devices
    vectors = jnp.stack(
        [
            rank(mid_gain[:4]),
            rank(mid_shift[:4]),
            rank(jnp.concatenate([mid_gain[4:], mid_shift[4:]])),
            rank(jnp.concatenate([dec_gain, dec_shift])),
            line((low_gain, 128), (low_shift, 128)),
        ]
    )
    message_rows = -(-images // 8) * 8
    sums = dot_nt(member_strip, mine)[:message_rows]
    told = tell_row(sums)
    told = tell_group(jnp.concatenate([jnp.sum(told, axis=0), jnp.pad(vectors, ((0, message_rows - 5), (0, 0)))], axis=1))

    geometry = geometry_call(
        lambda *refs: geometry_kernel(margin, *refs),
        heights, widths, places,
        [
            shaped(groups, 8, pixels), shaped(groups, members, pixels), shaped(groups, 1), shaped(everyone, 1),
            shaped(everyone, 1), shaped(members + 8, share), shaped(1, window), shaped(1, ext), shaped(2, fine),
            jax.ShapeDtypeStruct((window, ext), BF),
        ],
    )

    x_blocks, origin, (told, late_low, late_w1, late_w2, late_proj, late_pool, *geometry) = gather_blocks(
        mine, (told, lowlevel, w_dec1, w_dec2, w_proj, w_pool, *geometry)
    )
    (
        canvas_rows, member_canvas, strip_counts, counts_c, counts_f, mine_rows, window_valid, valid_wide, fine_masks, enlarge,
    ) = geometry
    perm = jnp.stack(origin).astype(jnp.int32)
    mine, told = lax.optimization_barrier((mine, told))
    x_slice = lax.all_to_all(mine.reshape(groups, slice_depth, pixels), "row", 0, 0)
    first_told = told

    proj_taps = late_proj.reshape(outs, 5, wide).transpose(1, 0, 2)
    pool_taps = late_pool.reshape(outs, -1, wide).transpose(1, 0, 2)
    rest = lax.all_gather(jnp.concatenate([late_w2.transpose(1, 0, 2), proj_taps, pool_taps], axis=0), "ch", axis=0)
    w2, wp, w_pool_all = rest[:, :9], rest[:, 9:14], rest[:, 14:]
    wp_acts = wp[:, :4].reshape(devices, 4, outs, devices, outs).transpose(3, 0, 2, 1, 4).reshape(devices, wide, 4 * outs)
    wp_pool = wp[:, 4].reshape(wide, wide)

    low_in = late_low * valid_fine_strip
    low_part = dot(w_low, low_in).astype(BF)
    low_pre = lax.psum_scatter(low_part, "ch", scatter_dimension=1, tiled=True).astype(F32)
    first_taps = late_w1.transpose(1, 0, 2)
    w1 = lax.all_gather(jnp.concatenate([first_taps[:, :, LOWC:], first_taps[:, :, :LOWC]], axis=2), "ch", axis=0)

    area_rows = jnp.pad(area, (0, message_rows - images), constant_values=1.0)[:, None]
    pair = shaped(2, 256)
    branch_gains, proj_gain, first_gain, second_gain, low_gains, broad_part = small_call(
        lambda *refs: parameter_kernel(depth, *refs),
        [first_told, w_pool_all, wp_pool, area_rows],
        (),
        [shaped(devices, 2, 256), pair, pair, pair, pair, shaped(1, wide, images)],
        0,
    )

    w_taps = w_atrous.transpose(0, 2, 1, 3).reshape(3, 9 * outs, -1)
    centre, up, down = pyramid(x_blocks, perm, w_taps, w_one, strip_rows)
    up, down, x_slice = lax.optimization_barrier((up, down, x_slice))
    x_canvas = lax.all_gather(x_slice, "ch", axis=0)
    fwd = [(i, i + 1) for i in range(groups - 1)]
    bwd = [(i + 1, i) for i in range(groups - 1)]
    from_next = lax.ppermute(up, "row", bwd)
    from_prev = lax.ppermute(down, "row", fwd)

    member_mine, valid_mine = mine_rows[:images], mine_rows[members : members + 1]
    valid_fine = valid_wide[:, WF:-WF]

    order = jnp.argsort(perm)

    def columns(s, lead):
        s = s.reshape((groups,) + lead + (devices, slice_depth))
        s = jnp.moveaxis(s, 0, len(lead) + 1)
        return s.reshape(lead + (devices * depth,)).astype(F32)

    gain_mid, shift_mid = mid_gain.astype(F32), mid_shift.astype(F32)

    branch_valid, branch_gains, wp_acts, broad_part = lax.optimization_barrier((valid_strip, branch_gains, wp_acts, broad_part))

    tile = jax.ShapeDtypeStruct((everyone, 8, 128), F32)
    centered, pieces, stats = small_call(
        branch_kernel,
        [centre, from_next, from_prev, branch_valid],
        (),
        [
            jax.ShapeDtypeStruct((4 * outs, pixels), BF),
            jax.ShapeDtypeStruct((devices, 4 * outs, share), BF),
            tile,
        ],
        0,
    )
    told_branch = swap_all(stats)
    swapped = swap_ch(pieces)
    proj_pre, proj_left, proj_right, stats = small_call(
        project_kernel,
        [
            swapped, told_branch.reshape(groups, devices, 8, 128), strip_counts, branch_gains, wp_acts, broad_part, member_mine,
            valid_mine, low_pre, valid_fine, scalars, jnp.concatenate([strip[None].astype(jnp.int32), perm]),
        ],
        (10, 11),
        [
            jax.ShapeDtypeStruct((wide, share), F32),
            jax.ShapeDtypeStruct((wide, margin), F32),
            jax.ShapeDtypeStruct((wide, margin), F32),
            tile,
        ],
        8 * wide * wide * share,
    )
    proj_prev, proj_next = to_next(proj_right), to_previous(proj_left)
    low_prev, low_next = to_next(low_pre[:, -WF:]), to_previous(low_pre[:, :WF])
    told_proj, proj_prev, proj_next, low_prev, low_next, cotangent, w_cls, b_cls = lax.optimization_barrier(
        (swap_all(stats), proj_prev, proj_next, low_prev, low_next, cotangent, w_cls, b_cls)
    )
    canvas_centered = lax.all_gather(centered, "row", axis=0)
    own_told = lax.dynamic_index_in_dim(told_branch.reshape(groups, devices, 8 * 128), me, 1, False)
    own_mean, own_scale = merge_moments(own_told[:, : 4 * outs], own_told[:, 256 : 256 + 4 * outs], strip_counts[:, 0], count)
    cols = jnp.stack([gain_mid[:4].reshape(-1), shift_mid[:4].reshape(-1), own_scale, own_mean], axis=1)
    offsets = own_told[:, : 4 * outs].T

    lanes = WF * rows_per_step(fine_rows)
    edge = jax.ShapeDtypeStruct((wide, WF), F32)
    full = jax.ShapeDtypeStruct((wide, fine), F32)
    work = 18 * wide * wide * fine
    state = lambda n, channels: pltpu.VMEM((n, channels, 128), F32)
    decoder_in, first_pre, first_top, first_bottom, stats = decoder_call(
        lambda *refs: first_kernel(lanes, *refs),
        [
            proj_prev, proj_pre, proj_next, told_proj, counts_c, proj_gain, window_valid, enlarge, low_prev, low_pre, low_next,
            told_proj, counts_f, low_gains, valid_wide, fine_masks, w1, scalars,
        ],
        (), (17,),
        [jax.ShapeDtypeStruct((wide + LOWC, ext), BF), full, edge, edge, tile],
        (1,),
        [pltpu.VMEM((wide, window), BF), pltpu.VMEM((3 * wide, 3 * (wide + LOWC)), BF), state(3, wide)],
        fine, work,
    )
    first_prev, first_next = to_next(first_bottom), to_previous(first_top)
    told_first, first_prev, first_next, told_proj = lax.optimization_barrier((swap_all(stats), first_prev, first_next, told_proj))
    proj_told = told_proj.reshape(everyone, 8 * 128)
    proj_mean, proj_scale = merge_moments(proj_told[:, :wide], proj_told[:, 256 : 256 + wide], counts_c[:, 0], count)
    proj_normed = (proj_pre - proj_mean[:, None]) * proj_scale[:, None]
    first_act, second_pre, second_top, second_bottom, stats = decoder_call(
        lambda *refs: second_kernel(lanes, *refs),
        [first_prev, first_pre, first_next, told_first, counts_f, first_gain, valid_wide, fine_masks, w2, scalars],
        (), (9,),
        [jax.ShapeDtypeStruct((wide, ext), BF), full, edge, edge, tile],
        (1,),
        [pltpu.VMEM((3 * wide, 3 * wide), BF), state(3, wide)],
        fine, work,
    )
    told_second = swap_all(stats)
    second_prev, second_next = to_next(second_bottom), to_previous(second_top)
    told_second, second_prev, second_next, x_canvas = lax.optimization_barrier(
        (told_second, second_prev, second_next, x_canvas)
    )

    classes = w_cls.shape[0]
    cot = jnp.pad(cotangent, ((0, -classes % 32), (0, 0)))
    cot_prev, cot_next = to_next(cot[:, -WF:]), to_previous(cot[:, :WF])
    w_cls_wide = jnp.pad(w_cls, ((0, -classes % 32), (0, 0)))
    bias = jnp.pad(b_cls.astype(F32), (0, -classes % 32))[:, None]
    logits, class_part, bias_part, sums = decoder_call(
        class_kernel,
        [
            second_pre, cot, valid_fine, told_second, counts_f, second_gain, w_cls_wide, w_cls_wide.T, bias, scalars,
        ],
        (0, 1, 2), (9,),
        [
            jax.ShapeDtypeStruct((classes, fine), F32),
            jax.ShapeDtypeStruct((w_cls_wide.shape[0], wide), F32),
            jax.ShapeDtypeStruct((w_cls_wide.shape[0], 128), F32),
            tile,
        ],
        (0,),
        [state(2, wide), pltpu.VMEM((wide, 128), F32)],
        fine, work // 8,
    )
    told_sums = swap_all(sums)
    class_part = jnp.concatenate([class_part[:classes].reshape(-1), jnp.sum(bias_part[:classes], axis=1)])
    class_rows = -(-class_part.shape[0] // (128 * everyone))
    class_part = jnp.pad(class_part, (0, class_rows * 128 * everyone - class_part.shape[0])).reshape(everyone, class_rows, 128)
    class_part = jnp.pad(class_part, ((0, 0), (0, 8 - class_rows), (0, 0)))
    second_dz, first_dy, dy_top, dy_bottom, sums = decoder_call(
        lambda *refs: second_back_kernel(lanes, *refs),
        [
            second_prev, second_pre, second_next, told_second, counts_f, second_gain, told_sums, cot_prev, cot, cot_next,
            w_cls_wide.T, valid_wide, fine_masks, w2, first_pre, told_first, first_gain, class_part, scalars,
        ],
        (14,), (18,),
        [jax.ShapeDtypeStruct((wide, ext), BF), full, edge, edge, jax.ShapeDtypeStruct((everyone, 16, 128), F32)],
        (1,),
        [pltpu.VMEM((3 * wide, 3 * wide), BF), state(2, wide), pltpu.VMEM((wide, 128), F32)],
        fine, work,
    )
    second_sums = jnp.sum(told_sums, axis=0)
    dy_prev, dy_next = to_next(dy_bottom), to_previous(dy_top)
    told_first_sums, dy_prev, dy_next = lax.optimization_barrier((swap_all(sums), dy_prev, dy_next))
    first_sums = jnp.sum(told_first_sums, axis=0)
    class_share = first_sums[8 : 8 + class_rows]
    first_sums = first_sums[:8]
    g_dec2 = decoder_weight_grad(second_dz, first_act, fine_masks, outs)
    told_first_sums, g_dec2 = lax.optimization_barrier((told_first_sums, g_dec2))
    first_dz, grad_window, dy_low, low_part_sums = decoder_call(
        lambda *refs: first_back_kernel(lanes, *refs),
        [
            first_prev, first_pre, first_next, dy_prev, first_dy, dy_next, told_first, counts_f, first_gain, told_first_sums,
            valid_wide, fine_masks, w1, enlarge, low_pre, told_proj, low_gains, scalars,
        ],
        (14,), (17,),
        [
            jax.ShapeDtypeStruct((wide, ext), BF),
            jax.ShapeDtypeStruct((wide, window), F32),
            jax.ShapeDtypeStruct((LOWC, fine), F32),
            jax.ShapeDtypeStruct((2, 256), F32),
        ],
        (2,),
        [pltpu.VMEM((3 * (wide + LOWC), 3 * wide), BF), state(2, LOWC), pltpu.VMEM((LOWC, 128), F32)],
        fine, work,
    )
    g_dec1 = decoder_weight_grad(first_dz, decoder_in, fine_masks, outs)

    def norm_back(dy, normed, scale, gain, totals, valid, total):
        parts = (totals[0][:, None] + normed * totals[1][:, None]) * (valid / total)
        return (scale * gain)[:, None] * (dy - parts)

    grad_coarse = grad_window[:, margin : margin + share]
    grad_coarse = grad_coarse.at[:, :margin].add(to_next(grad_window[:, margin + share :]))
    grad_coarse = grad_coarse.at[:, share - margin :].add(to_previous(grad_window[:, :margin]))
    dy = grad_coarse * silu_slope(proj_gain[0][:, None] * proj_normed + proj_gain[1][:, None]) * valid_mine
    both = vector_tile(jnp.sum(dy, axis=1), jnp.sum(dy * proj_normed, axis=1), low_part_sums[0], low_part_sums[1])
    both = jnp.concatenate([both, jnp.pad(class_share, ((0, 8 - class_rows), (0, 0)))])
    told_both, g_dec1 = lax.optimization_barrier((tell_all(both), g_dec1))
    decs = jnp.concatenate([g_dec2, g_dec1], axis=3)
    pick = lambda i: lax.dynamic_index_in_dim(decs, i, 0, False)
    part_dec = reduce_blocks([pick(i) for i in origin]).astype(BF)
    both = jnp.sum(told_both[:, :8], axis=0).reshape(4, 256)
    class_sums = told_both[:, 8 : 8 + class_rows].reshape(-1)
    bias_sums = class_sums[classes * wide : classes * wide + classes]
    class_sums = class_sums[: classes * wide].reshape(classes, wide)
    proj_sums, low_sums = both[:2], both[2:, :LOWC]

    proj_dz = norm_back(dy, proj_normed, proj_scale, proj_gain[0], proj_sums, valid_mine, count).astype(BF)
    canvas_dz = lax.all_gather(proj_dz, BOTH, axis=0)
    slope = slopes(0, groups, canvas_centered, canvas_rows, cols, offsets)
    canvas_dz, part_dec, *slope = lax.optimization_barrier((canvas_dz, part_dec, *slope))

    wp_own = lax.dynamic_index_in_dim(wp_acts, me, 0, False)
    wp_pool_own = lax.dynamic_slice_in_dim(wp_pool, me * outs, outs, axis=1)
    padded_dz, strips_dz, branch_sums, image_dz = canvas_grad(
        canvas_dz, slope[0], canvas_centered, canvas_rows, member_canvas, wp_own.T, cols, offsets, 1.0 / count[None],
    )
    branch_sums = branch_sums[:, :2].T
    image_dz = image_dz[:, :images]


    def by_row(v):
        v = v.reshape(groups, -1)
        return jnp.pad(v, ((0, 0), (0, -v.shape[1] % wide))).reshape(groups, -1, wide)

    shares = [by_row(part_dec[..., :wide]), by_row(part_dec[..., wide : 2 * wide]), by_row(part_dec[..., 2 * wide :])]
    share_rows, split_at = shares[0].shape[1], 2 * shares[0].shape[1]
    shares = lax.all_to_all(jnp.concatenate(shares, axis=1), "row", 0, 0)
    shares = jnp.sum(shares.astype(F32), axis=0).astype(BF)

    lined = groups == 8 and 2 * slice_depth == 128 and shares.shape[0] <= 3 * outs
    part = pyramid_weight_grad(padded_dz, x_canvas, canvas_rows, (0, 1, 2), True, 3 * outs if lined else 0)
    if lined:
        part = part.at[27 * outs : 27 * outs + shares.shape[0]].set(shares)
    strip_pad = lax.dynamic_slice_in_dim(padded_dz, strip * pixels, pixels + 2 * PAD, axis=1)

    def finish(strip_pad, first_told, image_dz, strips_dz, dy_low):
        low_mean, low_scale = merge_moments(proj_told[:, 512 : 512 + LOWC], proj_told[:, 768 : 768 + LOWC], counts_f[:, 0], fine_count)
        low_normed = (low_pre - low_mean[:, None]) * low_scale[:, None]
        low_dz = norm_back(dy_low, low_normed, low_scale, low_gains[0, :LOWC], low_sums, valid_fine, fine_count).astype(BF)

        pool_sums = first_told[:, :images, :depth].transpose(0, 2, 1).reshape(devices * depth, images)
        pooled = (pool_sums / area[None]).astype(BF)
        pool_pre = dot(w_pool, pooled)
        pool_mean = jnp.mean(pool_pre, axis=1)
        pool_scale = lax.rsqrt(jnp.mean(pool_pre * pool_pre, axis=1) - pool_mean * pool_mean + EPSILON)
        pool_normed = (pool_pre - pool_mean[:, None]) * pool_scale[:, None]
        pool_shifted = gain_mid[4][:, None] * pool_normed + shift_mid[4][:, None]
        pool_act = jax.nn.silu(pool_shifted).astype(BF)

        g_proj_pool = jnp.dot(image_dz, pool_act.astype(F32).T, precision=HIGHEST)

        grad_pool_act = lax.dot_general(wp_pool_own.astype(F32), image_dz, (((0,), (0,)), ((), ())), precision=HIGHEST)
        dy_pool = grad_pool_act * silu_slope(pool_shifted)
        pool_gain_sum = jnp.sum(dy_pool * pool_normed, axis=1)
        pool_shift_sum = jnp.sum(dy_pool, axis=1)
        pool_dz = (
            (pool_scale * gain_mid[4])[:, None]
            * (dy_pool - (pool_shift_sum[:, None] + pool_normed * pool_gain_sum[:, None]) / images)
        ).astype(BF)
        g_w_pool = dot_nt(pool_dz, pooled)
        spread = jnp.dot(pool_dz.astype(F32) / area[None], member_strip[:images].astype(F32), precision=HIGHEST).astype(BF)


        parts = input_grad(strip_pad, spread, strip_rows, w_taps, w_one, w_pool, jnp.arange(devices, dtype=jnp.int32))
        g_feats = lax.psum_scatter(parts, "ch", scatter_dimension=0).astype(F32) * valid_strip
        low_dz_all = lax.all_gather(low_dz, "ch", axis=1, tiled=True)
        g_lowlevel = lax.dot_general(w_low, low_dz_all, (((0,), (0,)), ((), ())), preferred_element_type=F32)
        g_lowlevel = g_lowlevel * valid_fine_strip.astype(F32)
        g_low = jnp.sum(tell_row(dot_nt(low_dz_all, low_in)), axis=0)
        g_proj_acts = jnp.einsum("gop,gcp->oc", strips_dz, slope[1], preferred_element_type=F32)
        g_proj_part = jnp.concatenate([g_proj_acts, g_proj_pool], axis=1).astype(BF)
        g_proj = jnp.take(swap_ch(g_proj_part.reshape(devices, outs, 5 * outs)), order, axis=0)
        g_w_proj = g_proj.reshape(devices, outs, 5, outs).transpose(1, 2, 0, 3).reshape(outs, -1).astype(F32)
        return g_feats, g_lowlevel, g_low, g_w_proj, g_w_pool, pool_gain_sum, pool_shift_sum

    later = (strip_pad, first_told, image_dz, strips_dz, dy_low)
    if lined:
        found, finished = gather_line(part, later, finish)
        into, g_w_one, rest = assemble(found, devices, groups, strip, outs, devices * depth)
    else:
        part, later = lax.optimization_barrier((part, later))
        finished = finish(*later)
        found = columns(lax.all_gather(part, "row", axis=0), (28 * outs,))
        into, g_w_one = found[: 27 * outs], found[27 * outs :]
        rest = lax.all_gather(shares, "row", axis=0)
    g_feats, g_lowlevel, g_low, g_w_proj, g_w_pool, pool_gain_sum, pool_shift_sum = finished
    g_w_atrous = into.reshape(3, 9, outs, devices * depth).transpose(0, 2, 1, 3)

    rest = rest[:, : shares.shape[0]].astype(F32)
    back = lambda v, shape: v.reshape(groups, -1)[:, : math.prod(shape) // groups].reshape(shape)
    g_dec2 = back(rest[:, :share_rows], (9, outs, wide))
    g_dec1 = jnp.concatenate(
        [back(rest[:, share_rows:split_at], (9, outs, wide)), back(rest[:, split_at:], (9, outs, LOWC))], axis=2
    )
    g_w_dec1 = jnp.concatenate([g_dec1[:, :, wide:], g_dec1[:, :, :wide]], axis=2).transpose(1, 0, 2)
    g_w_dec2 = g_dec2.transpose(1, 0, 2)

    def my(v, n):
        return lax.dynamic_slice_in_dim(v, me * n, n, axis=-1)

    second_sums, first_sums = second_sums.reshape(4, 256), first_sums.reshape(4, 256)
    g_mid_gain = jnp.concatenate([branch_sums[1].reshape(4, outs), pool_gain_sum[None], my(proj_sums[1], outs)[None]])
    g_mid_shift = jnp.concatenate([branch_sums[0].reshape(4, outs), pool_shift_sum[None], my(proj_sums[0], outs)[None]])
    return (
        logits,
        g_feats,
        g_lowlevel,
        g_w_one,
        g_w_atrous,
        g_w_pool,
        g_w_proj,
        g_low,
        g_w_dec1,
        g_w_dec2,
        class_sums,
        bias_sums,
        g_mid_gain,
        g_mid_shift,
        my(low_sums[1], low_share),
        my(low_sums[0], low_share),
        jnp.stack([my(first_sums[1], outs), my(second_sums[1], outs)]),
        jnp.stack([my(first_sums[0], outs), my(second_sums[0], outs)]),
    )


def solution(mesh):
    placed = (
        P("ch", "row"),
        P("ch", "row"),
        P(),
        P(),
        P("ch", None),
        P(None, "ch", None, None),
        P("ch", None),
        P("ch", None),
        P(None, "ch"),
        P("ch", None, None),
        P("ch", None, None),
        P(),
        P(),
        P(None, "ch"),
        P(None, "ch"),
        P("ch"),
        P("ch"),
        P(None, "ch"),
        P(None, "ch"),
        P(None, ("row", "ch")),
    )
    return jax.shard_map(
        local,
        mesh=mesh,
        in_specs=placed,
        out_specs=(
            P(None, ("row", "ch")),
            P("ch", "row"),
            P("ch", "row"),
            P("ch", None),
            P(None, "ch", None, None),
            P("ch", None),
            P("ch", None),
            P(None, "ch"),
            P("ch", None, None),
            P("ch", None, None),
            P(),
            P(),
            P(None, "ch"),
            P(None, "ch"),
            P("ch"),
            P("ch"),
            P(None, "ch"),
            P(None, "ch"),
        ),
        check_vma=False,
    )
```
